32 devices in a mesh: group: 4 (over x, core), dp: 2 (over y), mp: 4 (over z).
Axes of the slice: x: 2, y: 2, z: 4, core: 2. Of those that a mesh axis runs over, the one named last changes fastest.
Arguments:
- hidden_in: bfloat16 [8, 2048, 768], P(('group', 'dp'), 'mp'), may hold values from -6 to 6
- doc_ids: int32 [8, 2048], P(('group', 'dp'), 'mp'), may hold values from 0 to 2, as said below
- out_cotangent: bfloat16 [8, 2048, 768], P(('group', 'dp'), 'mp'), may hold values from -6 to 6
- entry_weight: float32 [4, 768, 3840], P('group', 'dp', 'mp')
- entry_first: float32 [4, 768, 3840], P('group', 'dp', 'mp')
- entry_second: float32 [4, 768, 3840], P('group', 'dp', 'mp'), as said below
- entry_anchor: float32 [768, 3840], P('dp', 'mp')
- entry_velocity: float32 [768, 3840], P('dp', 'mp')
- exit_weight: float32 [4, 3840, 768], P('group', 'mp', 'dp')
- exit_first: float32 [4, 3840, 768], P('group', 'mp', 'dp')
- exit_second: float32 [4, 3840, 768], P('group', 'mp', 'dp'), as said below
- exit_anchor: float32 [3840, 768], P('mp', 'dp')
- exit_velocity: float32 [3840, 768], P('mp', 'dp')
- shared_weight: float32 [4, 768, 128], P('group', ('dp', 'mp')), may hold values from -0.21875 to 0.21875
- shared_first: float32 [4, 768, 128], P('group', ('dp', 'mp'))
- shared_second: float32 [4, 768, 128], P('group', ('dp', 'mp')), as said below
- shared_anchor: float32 [768, 128], P(('dp', 'mp')), may hold values from -0.21875 to 0.21875
- shared_velocity: float32 [768, 128], P(('dp', 'mp'))
- vector_weight: float32 [4, 8576], P('group')
- vector_first: float32 [4, 8576], P('group')
- vector_second: float32 [4, 8576], P('group'), as said below
- vector_anchor: float32 [8576], replicated
- vector_velocity: float32 [8576], replicated
Outputs:
- block_output: float32 [8, 2048, 768], P(('group', 'dp'), 'mp')
- input_grad: float32 [8, 2048, 768], P(('group', 'dp'), 'mp')
- entry_moment: float32 [4, 768, 3840], P('group', 'dp', 'mp')
- entry_square: float32 [4, 768, 3840], P('group', 'dp', 'mp')
- entry_local: float32 [4, 768, 3840], P('group', 'dp', 'mp')
- entry_change: float32 [768, 3840], P('dp', 'mp')
- entry_momentum: float32 [768, 3840], P('dp', 'mp')
- entry_global: float32 [768, 3840], P('dp', 'mp')
- exit_moment: float32 [4, 3840, 768], P('group', 'mp', 'dp')
- exit_square: float32 [4, 3840, 768], P('group', 'mp', 'dp')
- exit_local: float32 [4, 3840, 768], P('group', 'mp', 'dp')
- exit_change: float32 [3840, 768], P('mp', 'dp')
- exit_momentum: float32 [3840, 768], P('mp', 'dp')
- exit_global: float32 [3840, 768], P('mp', 'dp')
- shared_moment: float32 [4, 768, 128], P('group', ('dp', 'mp'))
- shared_square: float32 [4, 768, 128], P('group', ('dp', 'mp'))
- shared_local: float32 [4, 768, 128], P('group', ('dp', 'mp'))
- shared_change: float32 [768, 128], P(('dp', 'mp'))
- shared_momentum: float32 [768, 128], P(('dp', 'mp'))
- shared_global: float32 [768, 128], P(('dp', 'mp'))
- vector_moment: float32 [4, 8576], P('group')
- vector_square: float32 [4, 8576], P('group')
- vector_local: float32 [4, 8576], P('group')
- vector_change: float32 [8576], replicated
- vector_momentum: float32 [8576], replicated
- vector_global: float32 [8576], replicated
The draws below stay inside these ranges and needn't reach their ends.
Inputs may be any that keep to these rules, and one draw needn't show every extreme that they name: `doc_ids`: each row's ids do not fall, start at 0 and end at 2; document 1 begins before position 256 and its last position is at or after 7 * 256. `entry_second`: second moments are positive. `exit_second`: second moments are positive. `shared_second`: second moments are positive. `vector_second`: second moments are positive.
All inputs are finite; a program needn't handle non-finite values.
Results may differ from the reference program's by a relative error of at most 0.004.
The reference program's roundings to bfloat16 on the way count: a program that leaves them out, or rounds other values in their place, can miss the bound.
Values may be sent and summed in bfloat16 or wider, within the bound.
A program may use at most 192 MiB of HBM per device.

```python
import math
import jax
import jax.numpy as jnp
from jax import lax

D = 768
HEADS = 12
HS = 64
ROT = 16
FF = 3072
SEQ = 2048
SEQ_DEV = 1
STEP = 5
ROWS = 8
GROUP_TOKENS = 4096
IN_COLS = 3840
QW = 192
PW = 960
VEC = 8576
N_GROUP = 4
N_DP = 2
N_MP = 4


def bounded(key, array_shape):
    return jax.random.truncated_normal(key, -3.0, 3.0, array_shape, jnp.float32)


def entry_spread():
    column = jnp.arange(IN_COLS) % PW
    return jnp.where(column < QW, 2.0, 1.0).astype(jnp.float32) / math.sqrt(D)


def exit_spread():
    row_place = jnp.arange(IN_COLS) % PW
    return jnp.where(row_place < QW, 4.0 / math.sqrt(HEADS * HS), 1.5 / math.sqrt(FF)).astype(jnp.float32)[:, None]


def vector_layout():
    place = jnp.arange(VEC)
    is_gain = (place < D) | (place >= 2 * D) & (place < 3 * D)
    base_value = jnp.where(is_gain, 1.0, 0.0).astype(jnp.float32)
    spread = jnp.where(is_gain, 0.1, 0.2).astype(jnp.float32)
    return (base_value, spread)


def first_moment(key, array_shape, grad_size):
    return bounded(key, array_shape) * (0.1 / 0.9) * grad_size * math.sqrt(GROUP_TOKENS)


def second_moment(key, array_shape, grad_size):
    key_one, key_two = jax.random.split(key)
    factor_one = jnp.exp(jax.random.uniform(key_one, array_shape, jnp.float32, 0.0, math.log(4.0)))
    factor_two = jnp.exp(jax.random.uniform(key_two, array_shape, jnp.float32, math.log(0.5), math.log(2.0)))
    return factor_one * factor_two * (0.05 / 0.95) * (grad_size * math.sqrt(GROUP_TOKENS)) ** 2


def draw_doc_ids(key, part):
    key = jax.random.fold_in(key, 31)
    key_one, key_two = jax.random.split(key)
    begins = jax.random.randint(key_one, (ROWS, 1), 1, max(SEQ // 8, 2))
    ends = jax.random.randint(key_two, (ROWS, 1), SEQ - SEQ // 8 + 1, SEQ)
    positions = jnp.arange(SEQ)[None, :]
    return ((positions >= begins).astype(jnp.int32) + (positions >= ends).astype(jnp.int32)).astype(jnp.int32)


def draw_entry_weight(key, part):
    key = jax.random.fold_in(key, 11)
    return bounded(key, (N_GROUP, D, IN_COLS)) * entry_spread()[None, None, :]


def draw_entry_first(key, part):
    key = jax.random.fold_in(key, 12)
    return first_moment(key, (N_GROUP, D, IN_COLS), 0.25)


def draw_entry_second(key, part):
    key = jax.random.fold_in(key, 13)
    return second_moment(key, (N_GROUP, D, IN_COLS), 0.25)


def draw_entry_anchor(key, part):
    key = jax.random.fold_in(key, 14)
    return bounded(key, (D, IN_COLS)) * entry_spread()[None, :]


def draw_entry_velocity(key, part):
    key = jax.random.fold_in(key, 15)
    return 0.5 * bounded(key, (D, IN_COLS)) * entry_spread()[None, :]


def draw_exit_weight(key, part):
    key = jax.random.fold_in(key, 21)
    return bounded(key, (N_GROUP, IN_COLS, D)) * exit_spread()[None]


def draw_exit_first(key, part):
    key = jax.random.fold_in(key, 22)
    return first_moment(key, (N_GROUP, IN_COLS, D), 0.4)


def draw_exit_second(key, part):
    key = jax.random.fold_in(key, 23)
    return second_moment(key, (N_GROUP, IN_COLS, D), 0.4)


def draw_exit_anchor(key, part):
    key = jax.random.fold_in(key, 24)
    return bounded(key, (IN_COLS, D)) * exit_spread()


def draw_exit_velocity(key, part):
    key = jax.random.fold_in(key, 25)
    return 0.5 * bounded(key, (IN_COLS, D)) * exit_spread()


def draw_shared_first(key, part):
    key = jax.random.fold_in(key, 42)
    return first_moment(key, (N_GROUP, D, 2 * HS), 0.5)


def draw_shared_second(key, part):
    key = jax.random.fold_in(key, 43)
    return second_moment(key, (N_GROUP, D, 2 * HS), 0.5)


def draw_shared_velocity(key, part):
    key = jax.random.fold_in(key, 45)
    return 0.5 * bounded(key, (D, 2 * HS)) / math.sqrt(D)


def draw_vector_weight(key, part):
    key = jax.random.fold_in(key, 51)
    base_value, spread = vector_layout()
    return base_value[None] + spread[None] * bounded(key, (N_GROUP, VEC))


def draw_vector_first(key, part):
    key = jax.random.fold_in(key, 52)
    return first_moment(key, (N_GROUP, VEC), 1.0)


def draw_vector_second(key, part):
    key = jax.random.fold_in(key, 53)
    return second_moment(key, (N_GROUP, VEC), 1.0)


def draw_vector_anchor(key, part):
    key = jax.random.fold_in(key, 54)
    base_value, spread = vector_layout()
    return base_value + spread * bounded(key, (VEC,))


def draw_vector_velocity(key, part):
    key = jax.random.fold_in(key, 55)
    base_value, spread = vector_layout()
    return 0.5 * spread * bounded(key, (VEC,))


def level_of(rng, shape, cuts, smallest, top_value):
    loudness = 1.0
    for axis_at, blocks in cuts:
        draws = jax.random.uniform(jax.random.fold_in(jax.random.fold_in(rng, 6), axis_at), (blocks,), jnp.float32, smallest / len(cuts), top_value / len(cuts))
        loudness = loudness * jnp.repeat(jnp.exp(draws), shape[axis_at] // blocks).reshape((-1,) + (1,) * (len(shape) - 1 - axis_at))
    return loudness


def bell_draw(key, shape, scale, most, cuts=(), held_as=jnp.bfloat16):
    array = jax.random.normal(key, shape, jnp.float32) * scale
    if len(cuts) > 0:
        array = level_of(key, shape, cuts, -0.22, 0.18) * array
    return jnp.clip(array, min=-most, max=most).astype(held_as)


def setup_inputs(seed: int = 0) -> dict:
    key_list = jax.random.split(jax.random.key(seed), 24)
    hidden_in = bell_draw(key_list[0], (ROWS, SEQ, D), 1.0, 6.0, ((0, 8), (1, 4)))
    doc_ids = draw_doc_ids(jax.random.fold_in(key_list[23], 71), 0)
    out_cotangent = bell_draw(key_list[2], (ROWS, SEQ, D), 1.0, 6.0, ((0, 8), (1, 4)))
    entry_weight = draw_entry_weight(jax.random.fold_in(key_list[23], 71), 0)
    entry_first = draw_entry_first(jax.random.fold_in(key_list[23], 71), 0)
    entry_second = draw_entry_second(jax.random.fold_in(key_list[23], 71), 0)
    entry_anchor = draw_entry_anchor(jax.random.fold_in(key_list[23], 71), 0)
    entry_velocity = draw_entry_velocity(jax.random.fold_in(key_list[23], 71), 0)
    exit_weight = draw_exit_weight(jax.random.fold_in(key_list[23], 71), 0)
    exit_first = draw_exit_first(jax.random.fold_in(key_list[23], 71), 0)
    exit_second = draw_exit_second(jax.random.fold_in(key_list[23], 71), 0)
    exit_anchor = draw_exit_anchor(jax.random.fold_in(key_list[23], 71), 0)
    exit_velocity = draw_exit_velocity(jax.random.fold_in(key_list[23], 71), 0)
    shared_weight = bell_draw(key_list[13], (N_GROUP, D, 2 * HS), D ** -0.5, 0.21875, ((0, 4), (1, 8)), jnp.float32)
    shared_first = draw_shared_first(jax.random.fold_in(key_list[23], 71), 0)
    shared_second = draw_shared_second(jax.random.fold_in(key_list[23], 71), 0)
    shared_anchor = bell_draw(key_list[16], (D, 2 * HS), D ** -0.5, 0.21875, ((0, 8),), jnp.float32)
    shared_velocity = draw_shared_velocity(jax.random.fold_in(key_list[23], 71), 0)
    vector_weight = draw_vector_weight(jax.random.fold_in(key_list[23], 71), 0)
    vector_first = draw_vector_first(jax.random.fold_in(key_list[23], 71), 0)
    vector_second = draw_vector_second(jax.random.fold_in(key_list[23], 71), 0)
    vector_anchor = draw_vector_anchor(jax.random.fold_in(key_list[23], 71), 0)
    vector_velocity = draw_vector_velocity(jax.random.fold_in(key_list[23], 71), 0)
    return dict(hidden_in=hidden_in, doc_ids=doc_ids, out_cotangent=out_cotangent, entry_weight=entry_weight, entry_first=entry_first, entry_second=entry_second, entry_anchor=entry_anchor, entry_velocity=entry_velocity, exit_weight=exit_weight, exit_first=exit_first, exit_second=exit_second, exit_anchor=exit_anchor, exit_velocity=exit_velocity, shared_weight=shared_weight, shared_first=shared_first, shared_second=shared_second, shared_anchor=shared_anchor, shared_velocity=shared_velocity, vector_weight=vector_weight, vector_first=vector_first, vector_second=vector_second, vector_anchor=vector_anchor, vector_velocity=vector_velocity)


@jax.custom_vjp
def low(v):
    return lax.optimization_barrier(v.astype(jnp.bfloat16)).astype(jnp.float32)

@jax.custom_vjp
def low_back(v):
    return v

def low_keep(v):
    return (low(v), None)

def low_pass(kept, grad):
    return (grad,)

def back_keep(v):
    return (v, None)

def back_low(kept, grad):
    return (low(grad),)
low.defvjp(low_keep, low_pass)
low_back.defvjp(back_keep, back_low)
HIGHEST_PRECISION = lax.Precision.HIGHEST
NORM_EPS = 1e-05
BETA_ONE = 0.9
BETA_TWO = 0.95
ADAM_EPS = 1e-08
MATRIX_RATE = 0.03
MATRIX_DECAY = 0.1
VECTOR_RATE = 0.3
OUTER_RATE = 0.7
OUTER_BETA = 0.9

def product(left, right):
    return jnp.dot(left, right, precision=HIGHEST_PRECISION, preferred_element_type=jnp.float32)

def layer_norm(inputs, gain, shift):
    centered = inputs - lax.optimization_barrier(jnp.mean(inputs, -1, keepdims=True))
    spread = lax.optimization_barrier(jnp.mean(centered * centered, -1, keepdims=True))
    return centered * lax.rsqrt(spread + NORM_EPS) * gain + shift

def rotation_tables():
    half_width = ROT // 2
    positions = jnp.arange(SEQ).astype(jnp.float32)
    frequency = 10000.0 ** (-(jnp.arange(half_width).astype(jnp.float32) * 2.0 / ROT))
    angles = positions[:, None] * frequency[None, :]
    cosine_table = jnp.concatenate([jnp.cos(angles), jnp.cos(angles)], -1)[:, None, :]
    sine_table = jnp.concatenate([jnp.sin(angles), jnp.sin(angles)], -1)[:, None, :]
    return (cosine_table, sine_table)

def rotate(tensor, cosine_table, sine_table):
    half_width = ROT // 2
    leading = tensor[..., :ROT]
    turned = jnp.concatenate([-leading[..., half_width:], leading[..., :half_width]], -1)
    return jnp.concatenate([leading * cosine_table + turned * sine_table, tensor[..., ROT:]], -1)

def attend(rotated_queries, rotated_keys, values, key_ids):
    block_rows = min(512, SEQ)
    number = SEQ // block_rows
    score_scale = 1.0 / math.sqrt(HS)
    key_pos = jnp.arange(SEQ).astype(jnp.int32)

    def one_block(position):
        offset = (position * block_rows).astype(jnp.int32)
        query_rows = lax.dynamic_slice_in_dim(rotated_queries, offset, block_rows, 0)
        query_ids = lax.dynamic_slice_in_dim(key_ids, offset, block_rows, 0)
        query_pos = offset + jnp.arange(block_rows).astype(jnp.int32)
        raw_scores = jnp.einsum('qhd,kd->hqk', query_rows, rotated_keys, precision=HIGHEST_PRECISION)
        scores = low_back(raw_scores) * score_scale
        allowed = (key_pos[None, :] <= query_pos[:, None]) & (query_ids[:, None] == key_ids[None, :])
        scores = jnp.where(allowed[None], scores, -1000000000.0)
        highest = lax.optimization_barrier(jnp.max(scores, -1, keepdims=True))
        exponent = jnp.exp(scores - highest)
        softmax = exponent / lax.optimization_barrier(jnp.sum(exponent, -1, keepdims=True))
        return jnp.einsum('hqk,kd->qhd', low(softmax), values, precision=HIGHEST_PRECISION)
    mixed = lax.map(jax.checkpoint(one_block), jnp.arange(number).astype(jnp.int32))
    return mixed.reshape(SEQ, HEADS, HS)

def forward(params, inputs, key_ids, cosine_table, sine_table):
    entry, leave, shared, vector = params
    entry_split = low(entry).reshape(D, N_MP, PW)
    query_weight = entry_split[:, :, :QW].reshape(D, HEADS * HS)
    up_weight = entry_split[:, :, QW:].reshape(D, FF)
    leave_split = low(leave).reshape(N_MP, PW, D)
    attend_weight = leave_split[:, :QW].reshape(HEADS * HS, D)
    down_weight = leave_split[:, QW:].reshape(FF, D)
    pair_weight = low(shared)
    bias_split = vector[6 * D + 2 * HS:].reshape(N_MP, PW)
    query_bias = bias_split[:, :QW].reshape(HEADS * HS)
    up_bias = bias_split[:, QW:].reshape(FF)
    attn_input = low(layer_norm(inputs, vector[0:D], vector[D:2 * D]))
    ffn_input = low(layer_norm(inputs, vector[2 * D:3 * D], vector[3 * D:4 * D]))
    queries = low_back(product(attn_input, query_weight) + query_bias).reshape(SEQ, HEADS, HS)
    pairs = low_back(product(attn_input, pair_weight) + vector[6 * D:6 * D + 2 * HS])
    rotated_queries = low(rotate(queries, cosine_table, sine_table))
    rotated_keys = low(rotate(pairs[:, None, :HS], cosine_table, sine_table)[:, 0])
    values = low(pairs[:, HS:])
    mixed = attend(rotated_queries, rotated_keys, values, key_ids).reshape(SEQ, HEADS * HS)
    attended = low(low_back(mixed))
    hidden = low(jax.nn.gelu(low_back(product(ffn_input, up_weight) + up_bias), approximate=False))
    branches = product(attended, attend_weight) + product(hidden, down_weight)
    return inputs + branches + vector[4 * D:5 * D] + vector[5 * D:6 * D]

def adamw_update(weight, first, second, gradient, step_rate, decay):
    first_new = BETA_ONE * first + (1.0 - BETA_ONE) * gradient
    second_new = BETA_TWO * second + (1.0 - BETA_TWO) * gradient * gradient
    fix_first = 1.0 - BETA_ONE ** STEP
    fix_second = 1.0 - BETA_TWO ** STEP
    update = first_new / fix_first / (jnp.sqrt(second_new / fix_second) + ADAM_EPS)
    return (first_new, second_new, weight - step_rate * (update + decay * weight))

def outer_step(anchor, velocity, local_new):
    change = lax.optimization_barrier(jnp.mean(anchor[None] - local_new, 0))
    momentum = OUTER_BETA * velocity + change
    return (change, momentum, anchor - OUTER_RATE * (change + OUTER_BETA * momentum))

def reference(hidden_in, doc_ids, out_cotangent, entry_weight, entry_first, entry_second, entry_anchor, entry_velocity, exit_weight, exit_first, exit_second, exit_anchor, exit_velocity, shared_weight, shared_first, shared_second, shared_anchor, shared_velocity, vector_weight, vector_first, vector_second, vector_anchor, vector_velocity):
    cosine_table, sine_table = rotation_tables()
    per_group = N_DP * SEQ_DEV
    inputs = hidden_in.astype(jnp.float32).reshape(N_GROUP, per_group, SEQ, D)
    cotangents = out_cotangent.astype(jnp.float32).reshape(N_GROUP, per_group, SEQ, D)
    grouped_ids = doc_ids.reshape(N_GROUP, per_group, SEQ)
    params = (entry_weight, exit_weight, shared_weight, vector_weight)

    def group_pass(running, record):
        group_params, group_inputs, group_ids, group_cots = record
        blank_grads = jax.tree.map(jnp.zeros_like, group_params)

        def sequence_pass(summed, item):
            row_inputs, row_ids, row_cots = item
            result, pullback = jax.vjp(lambda p, v: forward(p, v, row_ids, cosine_table, sine_table), group_params, row_inputs)
            param_grads, input_grads = pullback(row_cots)
            return (jax.tree.map(jnp.add, summed, param_grads), (result, input_grads))
        grads, (results, input_grads) = lax.scan(sequence_pass, blank_grads, (group_inputs, group_ids, group_cots))
        return (running, (grads, results, input_grads))
    _, (grads, results, input_grads) = lax.scan(group_pass, jnp.zeros((), jnp.float32), (params, inputs, grouped_ids, cotangents))
    block_output = results.reshape(ROWS, SEQ, D)
    input_grad = input_grads.reshape(ROWS, SEQ, D)
    entry_m, entry_v, entry_new = adamw_update(entry_weight, entry_first, entry_second, grads[0], MATRIX_RATE, MATRIX_DECAY)
    exit_m, exit_v, exit_new = adamw_update(exit_weight, exit_first, exit_second, grads[1], MATRIX_RATE, MATRIX_DECAY)
    shared_m, shared_v, shared_new = adamw_update(shared_weight, shared_first, shared_second, grads[2], MATRIX_RATE, MATRIX_DECAY)
    vector_m, vector_v, vector_new = adamw_update(vector_weight, vector_first, vector_second, grads[3], VECTOR_RATE, 0.0)
    entry_c, entry_p, entry_g = outer_step(entry_anchor, entry_velocity, entry_new)
    exit_c, exit_p, exit_g = outer_step(exit_anchor, exit_velocity, exit_new)
    shared_c, shared_p, shared_g = outer_step(shared_anchor, shared_velocity, shared_new)
    vector_c, vector_p, vector_g = outer_step(vector_anchor, vector_velocity, vector_new)
    return (block_output, input_grad, entry_m, entry_v, entry_new, entry_c, entry_p, entry_g, exit_m, exit_v, exit_new, exit_c, exit_p, exit_g, shared_m, shared_v, shared_new, shared_c, shared_p, shared_g, vector_m, vector_v, vector_new, vector_c, vector_p, vector_g)
```

```python
import math

import jax
import jax.numpy as jnp
from jax import lax
from jax.experimental import pallas as pl
from jax.experimental.pallas import tpu as pltpu
from jax.sharding import PartitionSpec as P

D = 768
HEADS = 12
HS = 64
ROT = 16
STEP = 5
IN_COLS = 3840


NORM_EPS = 1e-05
BETA_ONE = 0.9
BETA_TWO = 0.95
ADAM_EPS = 1e-08
MATRIX_RATE = 0.03
MATRIX_DECAY = 0.1
VECTOR_RATE = 0.3
OUTER_RATE = 0.7
OUTER_BETA = 0.9

TILE = 256
F32 = jnp.float32
BF = jnp.bfloat16


def dot(left, right):
    return jnp.dot(left, right, preferred_element_type=F32)


def dot_nt(left, right):
    return lax.dot_general(left, right, (((1,), (1,)), ((), ())), preferred_element_type=F32)


def dot_tn(left, right):
    return lax.dot_general(left, right, (((0,), (0,)), ((), ())), preferred_element_type=F32)


def tile_at(rank, tile, per):
    return pl.multiple_of((jnp.bitwise_xor(tile // per, rank) * per + tile % per) * TILE, TILE)


def masked(scores, key_tile, query_tile, tiles, key_ids, query_ids):
    edge = key_tile == 0 or query_tile == tiles - 1
    if key_tile == query_tile:
        rows = lax.broadcasted_iota(jnp.int32, (TILE, TILE), 0)
        columns = lax.broadcasted_iota(jnp.int32, (TILE, TILE), 1)
        allowed = rows <= columns
        if edge:
            allowed = allowed & (key_ids == query_ids)
        return jnp.where(allowed, scores, -1e9)
    if edge:
        return jnp.where(key_ids == query_ids, scores, -1e9)
    return scores


def forward_kernel(rank_ref, q_ref, k_ref, vt_ref, row_ids, col_ids, o_ref, l_ref, s_ref):
    tiles = q_ref.shape[1] // TILE
    per = tiles // 4
    rank = rank_ref[0]
    for query in range(tiles):
        at_q = tile_at(rank, query, per)
        q = q_ref[:, pl.ds(at_q, TILE)]
        query_ids = row_ids[:, pl.ds(at_q, TILE)]
        highest = jnp.full((1, TILE), -jnp.inf, F32)
        for key in range(query + 1):
            at_k = tile_at(rank, key, per)
            scores = dot(k_ref[pl.ds(at_k, TILE), :], q)
            scores = masked(scores, key, query, tiles, col_ids[pl.ds(at_k, TILE), :], query_ids)
            s_ref[pl.ds(key * TILE, TILE), :] = scores
            highest = jnp.maximum(highest, jnp.max(scores, 0, keepdims=True))
        total = jnp.zeros((1, TILE), F32)
        for key in range(query + 1):
            exponent = jnp.exp(s_ref[pl.ds(key * TILE, TILE), :] - highest)
            s_ref[pl.ds(key * TILE, TILE), :] = exponent
            total = total + jnp.sum(exponent, 0, keepdims=True)
        inverse = 1.0 / total
        mixed = jnp.zeros((HS, TILE), F32)
        for key in range(query + 1):
            at_k = tile_at(rank, key, per)
            softmax = (s_ref[pl.ds(key * TILE, TILE), :] * inverse).astype(BF)
            mixed = mixed + dot(vt_ref[:, pl.ds(at_k, TILE)], softmax)
        o_ref[:, pl.ds(at_q, TILE)] = mixed.astype(BF)
        l_ref[:, :, pl.ds(at_q, TILE)] = jnp.broadcast_to(highest + jnp.log(total), (8, TILE))[None]


def attend_forward(rank, qt, k, vt, ids):
    length = qt.shape[1]
    heads = qt.shape[0] // HS
    by_head = lambda i, r: (i, 0)
    whole = lambda i, r: (0, 0)
    grid_spec = pltpu.PrefetchScalarGridSpec(
        num_scalar_prefetch=1,
        grid=(heads,),
        in_specs=[
            pl.BlockSpec((HS, length), by_head),
            pl.BlockSpec((length, HS), whole),
            pl.BlockSpec((HS, length), whole),
            pl.BlockSpec((1, length), whole),
            pl.BlockSpec((length, 1), whole),
        ],
        out_specs=[
            pl.BlockSpec((HS, length), by_head),
            pl.BlockSpec((1, 8, length), lambda i, r: (i, 0, 0)),
        ],
        scratch_shapes=[pltpu.VMEM((length, TILE), F32)],
    )
    work = heads * length * length * HS
    return pl.pallas_call(
        forward_kernel,
        grid_spec=grid_spec,
        out_shape=[
            jax.ShapeDtypeStruct((heads * HS, length), BF),
            jax.ShapeDtypeStruct((heads, 8, length), F32),
        ],
        compiler_params=pltpu.CompilerParams(vmem_limit_bytes=32 << 20),
        cost_estimate=pl.CostEstimate(
            flops=8 * work, bytes_accessed=4 << 20, transcendentals=heads * length * length // 2
        ),
        name="attend_rows",
    )(rank, qt, k, vt, ids.reshape(1, length), ids.reshape(length, 1))


def backward_kernel(
    rank_ref, q_ref, do_ref, l_ref, k_ref, v_ref, kt_ref, row_ids, col_ids,
    dq_ref, dk_ref, dv_ref, p_ref, d_ref,
):
    tiles = q_ref.shape[1] // TILE
    per = tiles // 4
    rank = rank_ref[0]

    @pl.when(pl.program_id(0) == 0)
    def _():
        dk_ref[...] = jnp.zeros_like(dk_ref)
        dv_ref[...] = jnp.zeros_like(dv_ref)

    for query in range(tiles):
        at_q = tile_at(rank, query, per)
        q = q_ref[:, pl.ds(at_q, TILE)]
        do = do_ref[:, pl.ds(at_q, TILE)]
        scaled = do * jnp.asarray(0.125, BF)
        query_ids = row_ids[:, pl.ds(at_q, TILE)]
        log_total = l_ref[0, 0:1, pl.ds(at_q, TILE)]
        inner = jnp.zeros((1, TILE), F32)
        for key in range(query + 1):
            at_k = tile_at(rank, key, per)
            scores = dot(k_ref[pl.ds(at_k, TILE), :], q)
            scores = masked(scores, key, query, tiles, col_ids[pl.ds(at_k, TILE), :], query_ids)
            softmax = jnp.exp(scores - log_total)
            prob_grad = dot(v_ref[pl.ds(at_k, TILE), :], scaled)
            p_ref[pl.ds(key * TILE, TILE), :] = softmax
            d_ref[pl.ds(key * TILE, TILE), :] = prob_grad
            inner = inner + jnp.sum(softmax * prob_grad, 0, keepdims=True)
        query_grad = jnp.zeros((HS, TILE), F32)
        for key in range(query + 1):
            at_k = tile_at(rank, key, per)
            softmax = p_ref[pl.ds(key * TILE, TILE), :]
            score_grad = (softmax * (d_ref[pl.ds(key * TILE, TILE), :] - inner)).astype(BF)
            query_grad = query_grad + dot(kt_ref[:, pl.ds(at_k, TILE)], score_grad)
            dk_ref[pl.ds(at_k, TILE), :] += dot_nt(score_grad, q)
            dv_ref[pl.ds(at_k, TILE), :] += dot_nt(softmax.astype(BF), do)
        dq_ref[:, pl.ds(at_q, TILE)] = query_grad


def attend_backward(rank, qt, dot_rows, log_total, k, v, kt, ids):
    length = qt.shape[1]
    heads = qt.shape[0] // HS
    by_head = lambda i, r: (i, 0)
    whole = lambda i, r: (0, 0)
    grid_spec = pltpu.PrefetchScalarGridSpec(
        num_scalar_prefetch=1,
        grid=(heads,),
        in_specs=[
            pl.BlockSpec((HS, length), by_head),
            pl.BlockSpec((HS, length), by_head),
            pl.BlockSpec((1, 8, length), lambda i, r: (i, 0, 0)),
            pl.BlockSpec((length, HS), whole),
            pl.BlockSpec((length, HS), whole),
            pl.BlockSpec((HS, length), whole),
            pl.BlockSpec((1, length), whole),
            pl.BlockSpec((length, 1), whole),
        ],
        out_specs=[
            pl.BlockSpec((HS, length), by_head),
            pl.BlockSpec((length, HS), whole),
            pl.BlockSpec((length, HS), whole),
        ],
        scratch_shapes=[pltpu.VMEM((length, TILE), F32), pltpu.VMEM((length, TILE), F32)],
    )
    work = heads * length * length * HS
    return pl.pallas_call(
        backward_kernel,
        grid_spec=grid_spec,
        out_shape=[
            jax.ShapeDtypeStruct((heads * HS, length), F32),
            jax.ShapeDtypeStruct((length, HS), F32),
            jax.ShapeDtypeStruct((length, HS), F32),
        ],
        compiler_params=pltpu.CompilerParams(vmem_limit_bytes=32 << 20),
        cost_estimate=pl.CostEstimate(
            flops=14 * work, bytes_accessed=6 << 20, transcendentals=heads * length * length // 2
        ),
        name="attend_rows_back",
    )(rank, qt, dot_rows, log_total, k, v, kt, ids.reshape(1, length), ids.reshape(length, 1))


def rotate(rows, cosine_table, sine_table):
    half = ROT // 2
    one, two = (rows[..., :half, :], rows[..., half:ROT, :])
    return jnp.concatenate(
        [
            one * cosine_table - two * sine_table,
            two * cosine_table + one * sine_table,
            rows[..., ROT:, :],
        ],
        -2,
    )


def adamw_update(weight, first, second, gradient, step_rate, decay):
    first_new = BETA_ONE * first + (1.0 - BETA_ONE) * gradient
    second_new = BETA_TWO * second + (1.0 - BETA_TWO) * gradient * gradient
    fix_first = 1.0 - BETA_ONE**STEP
    fix_second = 1.0 - BETA_TWO**STEP
    update = first_new / fix_first / (jnp.sqrt(second_new / fix_second) + ADAM_EPS)
    return (first_new, second_new, weight - step_rate * (update + decay * weight))


def pairs_of(size, bit):
    return [(at, at ^ bit) for at in range(size)]


def over_core(array):
    return lax.ppermute(array, "group", pairs_of(lax.axis_size("group"), 1))


def over_half(array):
    return lax.ppermute(array, "group", pairs_of(lax.axis_size("group"), 2))


def over_next(array):
    return lax.ppermute(array, "mp", pairs_of(lax.axis_size("mp"), 1))


def over_dp(array):
    return lax.ppermute(array, "dp", pairs_of(2, 1))


def swapped_parts(array):
    parts = lax.axis_size("mp")
    pairs = []
    for group in range(lax.axis_size("group")):
        for rank in range(parts):
            here = group * parts + rank
            there = (group ^ 1) * parts + (rank ^ 2)
            pairs.append((here, there if group % 2 != rank // 2 else here))
    return lax.ppermute(array, ("group", "mp"), pairs)


def gather_square(own):
    pair = jnp.stack([own, over_next(own)])
    return jnp.concatenate([pair, over_core(pair)], 0)


def scatter_square(slots, send_type):
    pair = slots[:2] + over_core(slots[2:].astype(send_type)).astype(F32)
    return pair[0] + over_next(pair[1].astype(send_type)).astype(F32)


def sum_square(array):
    array = array + over_core(array)
    return array + over_next(array)


def gather_dp(own, axis):
    if lax.axis_size("dp") == 2:
        other = over_dp(own)
        first = lax.axis_index("dp") == 0
        return jnp.concatenate(
            [jnp.where(first, own, other), jnp.where(first, other, own)], axis
        )
    return lax.all_gather(own, "dp", axis=axis, tiled=True)


def scatter_dp(array, axis, send_type):
    if lax.axis_size("dp") == 2:
        size = array.shape[axis] // 2
        mine = lax.axis_index("dp")
        kept = lax.dynamic_slice_in_dim(array, mine * size, size, axis)
        sent = lax.dynamic_slice_in_dim(array, (1 - mine) * size, size, axis)
        return kept + over_dp(sent.astype(send_type)).astype(F32)
    return lax.psum_scatter(array, "dp", scatter_dimension=axis, tiled=True)


def sum_dp(array):
    if lax.axis_size("dp") == 2:
        return array + over_dp(array)
    return lax.psum(array, "dp")


def sum_groups(array, send_type):
    size = array.shape[0] // 2
    core = lax.axis_index("group") % 2
    kept = lax.dynamic_slice_in_dim(array, core * size, size, 0)
    sent = lax.dynamic_slice_in_dim(array, (1 - core) * size, size, 0)
    part = (kept + over_core(sent)).astype(send_type)
    part = part.astype(F32) + over_half(part).astype(F32)
    other = over_core(part)
    low = core == 0
    return jnp.concatenate([jnp.where(low, part, other), jnp.where(low, other, part)], 0)


def shards(
    hidden_in,
    doc_ids,
    out_cotangent,
    entry_weight,
    entry_first,
    entry_second,
    entry_anchor,
    entry_velocity,
    exit_weight,
    exit_first,
    exit_second,
    exit_anchor,
    exit_velocity,
    shared_weight,
    shared_first,
    shared_second,
    shared_anchor,
    shared_velocity,
    vector_weight,
    vector_first,
    vector_second,
    vector_anchor,
    vector_velocity,
):
    batch, local_len = hidden_in.shape[:2]
    parts = lax.axis_size("mp")
    group, rank = (lax.axis_index("group"), lax.axis_index("mp"))
    is_swapped = (group % 2) != (rank // 2)
    rank = jnp.where(is_swapped, jnp.bitwise_xor(rank, 2), rank)
    length = local_len * parts
    part_width = entry_weight.shape[2]
    query_width = HEADS * HS // parts
    heads = query_width // HS

    home_vector = vector_weight[0]
    vector = jnp.where(is_swapped, over_core(home_vector), home_vector)
    gain_one, shift_one = (vector[0:D], vector[D : 2 * D])
    gain_two, shift_two = (vector[2 * D : 3 * D], vector[3 * D : 4 * D])
    home_bias = home_vector[4 * D : 5 * D] + home_vector[5 * D : 6 * D]
    pair_bias = vector[6 * D : 6 * D + 2 * HS]
    in_bias = lax.dynamic_slice_in_dim(vector, 6 * D + 2 * HS + rank * part_width, part_width, 0)
    query_bias = in_bias[:query_width]
    up_bias = in_bias[query_width:]

    inputs = gather_square(swapped_parts(hidden_in[0])).reshape(length, D)
    ids = gather_square(swapped_parts(doc_ids[0])).reshape(length)
    entry_rows = gather_dp(swapped_parts(entry_weight[0].astype(BF)), 0)
    exit_rows = gather_dp(swapped_parts(exit_weight[0].astype(BF)), 1)
    pieces = gather_square(swapped_parts(shared_weight[0].astype(BF)))
    order = jnp.bitwise_xor(jnp.arange(parts), rank)
    pieces = jnp.take(pieces, order, axis=0)
    pair_weight = gather_dp(pieces.reshape(-1, 2 * HS), 0)
    cots = gather_square(swapped_parts(out_cotangent[0])).reshape(length, D)

    query_weight = entry_rows[:, :query_width]
    up_weight = entry_rows[:, query_width:]
    attend_weight = exit_rows[:query_width]
    down_weight = exit_rows[query_width:]

    half = ROT // 2
    positions = (order[:, None] * local_len + jnp.arange(local_len)[None, :]).reshape(length)
    frequency = 10000.0 ** (-(jnp.arange(half).astype(F32) * 2.0 / ROT))
    angles = frequency[:, None] * positions.astype(F32)[None, :]
    cosine_table, sine_table = (jnp.cos(angles), jnp.sin(angles))

    wide = inputs.astype(F32)
    centered = wide - jnp.mean(wide, -1, keepdims=True)
    normal = centered * lax.rsqrt(jnp.mean(centered * centered, -1, keepdims=True) + NORM_EPS)
    attn_input = (normal * gain_one + shift_one).astype(BF)
    ffn_input = (normal * gain_two + shift_two).astype(BF)

    queries = lax.dot_general(
        query_weight, attn_input, (((0,), (1,)), ((), ())), preferred_element_type=F32
    )
    queries = (queries + query_bias[:, None]).reshape(heads, HS, length)
    rotated_queries = rotate(queries, cosine_table, sine_table).astype(BF) * jnp.asarray(
        1.0 / math.sqrt(HS), BF
    )
    rotated_queries = rotated_queries.reshape(query_width, length)
    pairs = lax.dot_general(
        pair_weight, attn_input, (((0,), (1,)), ((), ())), preferred_element_type=F32
    )
    pairs = pairs + pair_bias[:, None]
    key_rows = rotate(pairs[:HS], cosine_table, sine_table).astype(BF)
    value_rows = pairs[HS:].astype(BF)
    keys, values = (key_rows.T, value_rows.T)
    rank_scalar = rank.reshape(1).astype(jnp.int32)
    attended, log_total = attend_forward(rank_scalar, rotated_queries, keys, value_rows, ids)

    hidden_pre = dot(ffn_input, up_weight) + up_bias
    half_root = math.sqrt(0.5)
    below = 0.5 * (1.0 + lax.erf(hidden_pre * half_root))
    hidden = (hidden_pre * below).astype(BF)
    density = jnp.exp(-0.5 * hidden_pre * hidden_pre) * (1.0 / math.sqrt(2.0 * math.pi))
    slope = below + hidden_pre * density

    partial_sum = dot_tn(attended, attend_weight) + dot(hidden, down_weight)
    branch = scatter_square(partial_sum.reshape(parts, local_len, D), BF)
    block_output = (
        hidden_in[0].astype(F32) + swapped_parts(branch.astype(BF)).astype(F32) + home_bias
    )

    grad_attend = dot(attended, cots)
    grad_down = dot_tn(hidden, cots)
    mixed_grad = dot_nt(attend_weight, cots).astype(BF)
    pre_grad = (dot_nt(cots, down_weight) * slope).astype(BF)
    grad_up = dot_tn(ffn_input, pre_grad)
    ffn_input_grad = dot_nt(pre_grad, up_weight)
    up_bias_grad = jnp.sum(pre_grad.astype(F32), 0)
    query_rot_grad, key_rot_grad, value_grad = attend_backward(
        rank_scalar, rotated_queries, mixed_grad, log_total, keys, values, key_rows, ids
    )
    query_grad = rotate(query_rot_grad.reshape(heads, HS, length), cosine_table, -sine_table)
    query_grad = query_grad.astype(BF).reshape(query_width, length)
    key_grad = rotate(key_rot_grad.T * math.sqrt(HS), cosine_table, -sine_table).T
    pair_partial = jnp.concatenate([key_grad, value_grad], -1)
    grad_query = dot(query_grad, attn_input).T
    attn_input_grad = lax.dot_general(
        query_grad, query_weight, (((0,), (1,)), ((), ())), preferred_element_type=F32
    )
    query_bias_grad = jnp.sum(query_grad.astype(F32), 1)
    joined = attn_input_grad * gain_one + ffn_input_grad * gain_two
    joined_own = scatter_square(joined.reshape(parts, local_len, D), BF)
    pair_low = scatter_square(pair_partial.reshape(parts, local_len, 2 * HS), F32).astype(BF)
    pair_input_grad = dot_nt(pair_low, pair_weight)
    joined_own = joined_own + pair_input_grad * gain_one
    joined_home = swapped_parts(joined_own.astype(BF)).astype(F32)
    home_wide = hidden_in[0].astype(F32)
    home_centered = home_wide - jnp.mean(home_wide, -1, keepdims=True)
    home_scale = lax.rsqrt(jnp.mean(home_centered * home_centered, -1, keepdims=True) + NORM_EPS)
    home_normal = home_centered * home_scale
    input_grad = out_cotangent[0].astype(F32) + home_scale * (
        joined_home
        - jnp.mean(joined_home, -1, keepdims=True)
        - home_normal * jnp.mean(joined_home * home_normal, -1, keepdims=True)
    )

    own_normal = normal[:local_len]
    own_attn = attn_input[:local_len]
    grad_pair = dot_tn(own_attn, pair_low)
    out_bias_grad = jnp.sum(cots[:local_len].astype(F32), 0)
    leading_grads = jnp.concatenate(
        [
            jnp.sum(attn_input_grad * normal, 0) + jnp.sum(pair_input_grad * own_normal, 0),
            jnp.sum(attn_input_grad, 0) + jnp.sum(pair_input_grad, 0),
            jnp.sum(ffn_input_grad * normal, 0),
            jnp.sum(ffn_input_grad, 0),
            out_bias_grad,
            out_bias_grad,
            jnp.sum(pair_low.astype(F32), 0),
        ]
    )
    bias_tail = lax.dynamic_update_slice(
        jnp.zeros((IN_COLS,), F32),
        jnp.concatenate([query_bias_grad, up_bias_grad]),
        (rank * part_width,),
    )
    vector_grad = swapped_parts(
        sum_dp(sum_square(jnp.concatenate([leading_grads, bias_tail])))
    )
    entry_grad = scatter_dp(jnp.concatenate([grad_query, grad_up], 1), 0, BF)
    exit_grad = scatter_dp(jnp.concatenate([grad_attend, grad_down], 0), 1, BF)
    entry_grad = jnp.where(
        is_swapped, swapped_parts(entry_grad.astype(BF)).astype(F32), entry_grad
    )
    exit_grad = jnp.where(is_swapped, swapped_parts(exit_grad.astype(BF)).astype(F32), exit_grad)
    grad_pieces = grad_pair.reshape(lax.axis_size("dp"), parts, -1, 2 * HS)
    grad_pieces = jnp.take(grad_pieces, order, axis=1).swapaxes(0, 1)
    shared_grad = scatter_dp(scatter_square(grad_pieces, F32), 0, F32)
    shared_grad = swapped_parts(shared_grad.reshape(-1, 2 * HS))

    entry_m, entry_v, entry_new = adamw_update(
        entry_weight[0], entry_first[0], entry_second[0], entry_grad, MATRIX_RATE, MATRIX_DECAY
    )
    exit_m, exit_v, exit_new = adamw_update(
        exit_weight[0], exit_first[0], exit_second[0], exit_grad, MATRIX_RATE, MATRIX_DECAY
    )
    shared_m, shared_v, shared_new = adamw_update(
        shared_weight[0], shared_first[0], shared_second[0], shared_grad, MATRIX_RATE, MATRIX_DECAY
    )
    vector_m, vector_v, vector_new = adamw_update(
        home_vector, vector_first[0], vector_second[0], vector_grad, VECTOR_RATE, 0.0
    )
    group_count = lax.axis_size("group")
    vector_gap = vector_anchor - vector_new
    vector_gap = vector_gap + over_core(vector_gap)
    summed = (
        sum_groups(entry_anchor - entry_new, BF),
        sum_groups(exit_anchor - exit_new, BF),
        sum_groups(shared_anchor - shared_new, F32),
        vector_gap + over_half(vector_gap),
    )
    anchors = (entry_anchor, exit_anchor, shared_anchor, vector_anchor)
    velocities = (entry_velocity, exit_velocity, shared_velocity, vector_velocity)
    outer_parts = []
    for position in range(4):
        change = summed[position] / group_count
        momentum = OUTER_BETA * velocities[position] + change
        outer_parts.append(
            (change, momentum, anchors[position] - OUTER_RATE * (change + OUTER_BETA * momentum))
        )
    return (
        (block_output[None], input_grad[None], entry_m[None], entry_v[None], entry_new[None])
        + outer_parts[0]
        + (exit_m[None], exit_v[None], exit_new[None])
        + outer_parts[1]
        + (shared_m[None], shared_v[None], shared_new[None])
        + outer_parts[2]
        + (vector_m[None], vector_v[None], vector_new[None])
        + outer_parts[3]
    )


def solution(mesh):
    in_specs = (
        P(("group", "dp"), "mp", None),
        P(("group", "dp"), "mp"),
        P(("group", "dp"), "mp", None),
        P("group", "dp", "mp"),
        P("group", "dp", "mp"),
        P("group", "dp", "mp"),
        P("dp", "mp"),
        P("dp", "mp"),
        P("group", "mp", "dp"),
        P("group", "mp", "dp"),
        P("group", "mp", "dp"),
        P("mp", "dp"),
        P("mp", "dp"),
        P("group", ("dp", "mp"), None),
        P("group", ("dp", "mp"), None),
        P("group", ("dp", "mp"), None),
        P(("dp", "mp"), None),
        P(("dp", "mp"), None),
        P("group", None),
        P("group", None),
        P("group", None),
        P(),
        P(),
    )
    out_specs = (
        P(("group", "dp"), "mp", None),
        P(("group", "dp"), "mp", None),
        P("group", "dp", "mp"),
        P("group", "dp", "mp"),
        P("group", "dp", "mp"),
        P("dp", "mp"),
        P("dp", "mp"),
        P("dp", "mp"),
        P("group", "mp", "dp"),
        P("group", "mp", "dp"),
        P("group", "mp", "dp"),
        P("mp", "dp"),
        P("mp", "dp"),
        P("mp", "dp"),
        P("group", ("dp", "mp"), None),
        P("group", ("dp", "mp"), None),
        P("group", ("dp", "mp"), None),
        P(("dp", "mp"), None),
        P(("dp", "mp"), None),
        P(("dp", "mp"), None),
        P("group", None),
        P("group", None),
        P("group", None),
        P(),
        P(),
        P(),
    )
    return jax.shard_map(shards, mesh=mesh, in_specs=in_specs, out_specs=out_specs, check_vma=False)
```

```python
import functools
import math

import jax
import jax.numpy as jnp
import numpy as np
from jax import lax
from jax.experimental import pallas as pl
from jax.experimental.pallas import tpu as pltpu
from jax.sharding import PartitionSpec as P

D = 768
HEADS = 12
HS = 64
ROT = 16
STEP = 5
IN_COLS = 3840


NORM_EPS = 1e-05
BETA_ONE = 0.9
BETA_TWO = 0.95
ADAM_EPS = 1e-08
MATRIX_RATE = 0.03
MATRIX_DECAY = 0.1
VECTOR_RATE = 0.3
OUTER_RATE = 0.7
OUTER_BETA = 0.9

TILE = 256
F32 = jnp.float32
BF = jnp.bfloat16


def dot(left, right):
    return jnp.dot(left, right, preferred_element_type=F32)


def dot_nt(left, right):
    return lax.dot_general(left, right, (((1,), (1,)), ((), ())), preferred_element_type=F32)


def dot_tn(left, right):
    return lax.dot_general(left, right, (((0,), (0,)), ((), ())), preferred_element_type=F32)


def adamw_update(weight, first, second, gradient, step_rate, decay):
    first_new = BETA_ONE * first + (1.0 - BETA_ONE) * gradient
    second_new = BETA_TWO * second + (1.0 - BETA_TWO) * gradient * gradient
    fix_first = 1.0 - BETA_ONE**STEP
    fix_second = 1.0 - BETA_TWO**STEP
    update = first_new / fix_first / (jnp.sqrt(second_new / fix_second) + ADAM_EPS)
    return (first_new, second_new, weight - step_rate * (update + decay * weight))


def pairs_of(size, bit):
    return [(at, at ^ bit) for at in range(size)]


def over_core(array):
    return lax.ppermute(array, "group", pairs_of(lax.axis_size("group"), 1))


def over_half(array):
    return lax.ppermute(array, "group", pairs_of(lax.axis_size("group"), 2))


def over_next(array):
    return lax.ppermute(array, "mp", pairs_of(lax.axis_size("mp"), 1))


def over_dp(array):
    return lax.ppermute(array, "dp", pairs_of(2, 1))


def swapped_parts(array):
    parts = lax.axis_size("mp")
    pairs = []
    for group in range(lax.axis_size("group")):
        for rank in range(parts):
            here = group * parts + rank
            there = (group ^ 1) * parts + (rank ^ 2)
            pairs.append((here, there if group % 2 != rank // 2 else here))
    return lax.ppermute(array, ("group", "mp"), pairs)


def gather_square(own):
    pair = jnp.stack([own, over_next(own)])
    return jnp.concatenate([pair, over_core(pair)], 0)


def scatter_square(slots, send_type):
    pair = slots[:2] + over_core(slots[2:].astype(send_type)).astype(F32)
    return pair[0] + over_next(pair[1].astype(send_type)).astype(F32)


def sum_square(array):
    array = array + over_core(array)
    return array + over_next(array)


def gather_dp(own, axis):
    if lax.axis_size("dp") == 2:
        other = over_dp(own)
        first = lax.axis_index("dp") == 0
        return jnp.concatenate(
            [jnp.where(first, own, other), jnp.where(first, other, own)], axis
        )
    return lax.all_gather(own, "dp", axis=axis, tiled=True)


def scatter_dp(array, axis, send_type):
    if lax.axis_size("dp") == 2:
        size = array.shape[axis] // 2
        mine = lax.axis_index("dp")
        kept = lax.dynamic_slice_in_dim(array, mine * size, size, axis)
        sent = lax.dynamic_slice_in_dim(array, (1 - mine) * size, size, axis)
        return kept + over_dp(sent.astype(send_type)).astype(F32)
    return lax.psum_scatter(array, "dp", scatter_dimension=axis, tiled=True)


def sum_dp(array):
    if lax.axis_size("dp") == 2:
        return array + over_dp(array)
    return lax.psum(array, "dp")


def sum_groups(array, send_type):
    size = array.shape[0] // 2
    core = lax.axis_index("group") % 2
    kept = lax.dynamic_slice_in_dim(array, core * size, size, 0)
    sent = lax.dynamic_slice_in_dim(array, (1 - core) * size, size, 0)
    part = (kept + over_core(sent)).astype(send_type)
    part = part.astype(F32) + over_half(part).astype(F32)
    other = over_core(part)
    low = core == 0
    return jnp.concatenate([jnp.where(low, part, other), jnp.where(low, other, part)], 0)


def flip_one(index):
    return index + 1 - 2 * (index % 2)


def flip_two(index):
    return index + 2 - 4 * ((index // 2) % 2)


def at_slot(slot, rank):
    rank = flip_one(rank) if slot % 2 else rank
    return flip_two(rank) if slot // 2 else rank


class Copies:
    def __init__(self, send, receive):
        self.send, self.receive, self.used, self.sends = (send, receive, 0, [])

    def remote(self, source, target, device):
        at = self.used
        self.used += 1
        copy = pltpu.make_async_remote_copy(
            src_ref=source,
            dst_ref=target,
            send_sem=self.send.at[at],
            recv_sem=self.receive.at[at],
            device_id=device,
            device_id_type=pl.DeviceIdType.MESH,
        )
        copy.start()
        self.sends.append(copy)
        return copy

    def swapped(self, source, target, is_swapped, device):
        at = self.used
        self.used += 1
        far = pltpu.make_async_remote_copy(
            src_ref=source,
            dst_ref=target,
            send_sem=self.send.at[at],
            recv_sem=self.receive.at[at],
            device_id=device,
            device_id_type=pl.DeviceIdType.MESH,
        )
        near = pltpu.make_async_copy(source, target, self.receive.at[at])

        @pl.when(is_swapped)
        def _():
            far.start()

        @pl.when(jnp.logical_not(is_swapped))
        def _():
            near.start()

        def wait():
            @pl.when(is_swapped)
            def _():
                far.wait_send()
                far.wait_recv()

            @pl.when(jnp.logical_not(is_swapped))
            def _():
                near.wait()

        return wait

    def finish(self):
        for copy in self.sends:
            copy.wait_send()


class Place:
    def __init__(self, dp_size):
        group, self.dp, home = (lax.axis_index("group"), lax.axis_index("dp"), lax.axis_index("mp"))
        core, upper = (group % 2, home // 2)
        self.is_swapped = core != upper
        self.home = home
        self.rank = jnp.where(self.is_swapped, flip_two(home), home)
        self.swap = {"group": flip_one(group), "mp": flip_two(home)}
        self.core = {"group": flip_one(group)}
        self.next = {"mp": flip_one(home)}
        self.dp_peers = [{"dp": (self.dp + step) % dp_size} for step in range(1, dp_size)]

    def meet(self):
        barrier = pltpu.get_barrier_semaphore()
        peers = [self.core, self.next, self.swap] + self.dp_peers
        for peer in peers:
            pl.semaphore_signal(
                barrier, inc=1, device_id=peer, device_id_type=pl.DeviceIdType.MESH
            )
        pl.semaphore_wait(barrier, len(peers))


def rotate(rows, cosine, sine):
    half = ROT // 2
    one, two = (rows[:half], rows[half:ROT])
    return jnp.concatenate(
        [one * cosine - two * sine, two * cosine + one * sine, rows[ROT:]], 0
    )


def first_kernel(
    dp_size, x_ref, c_ref, small_ref, big_ref, pair_ref, ids_ref, norm_ref, qb_ref, kvb_ref, cos_ref, sin_ref,
    xg, cg, a1, a2, big, small, kvw, ot, dqt, pair_grad,
    smt, kvt, qt, dot_rows, kt, vt, k, v, dk, dv, s_ref, d_ref, idr, send, receive,
):
    place = Place(dp_size)
    rank, dp = (place.rank, place.dp)
    copies = Copies(send, receive)
    local = x_ref.shape[0]
    length = 4 * local
    rows = small_ref.shape[0]
    query_width = small_ref.shape[1] // 2
    heads = query_width // HS
    gathers_pair = pair_ref.shape[0] != D
    place.meet()

    def swapped(source, target):
        return copies.swapped(source, target, place.is_swapped, place.swap)

    def dp_rows(ref, start, size):
        return ref.at[pl.ds(pl.multiple_of(dp * rows + start, 16), size)]

    step = local // 2
    spans = [pl.ds(at * step, step) for at in range(2)]
    x_swaps = [swapped(x_ref.at[s], xg.at[0, s]) for s in spans]
    small_swap = swapped(small_ref, dp_rows(small, 0, rows))
    if gathers_pair:
        pair_swap = swapped(pair_ref, kvw.at[dp, place.home])
    ids_swap = swapped(ids_ref, idr.at[:, pl.ds(0, local)])
    c_swaps = [swapped(c_ref.at[s], cg.at[0, s]) for s in spans]
    chunk = rows // 4 if rows % 64 == 0 else rows
    big_swaps = [
        swapped(big_ref.at[pl.ds(at, chunk)], dp_rows(big, at, chunk)) for at in range(0, rows, chunk)
    ]

    def normalise(slot):
        def body(at, carry):
            span = pl.ds(pl.multiple_of(at * 128, 128), 128)
            wide = xg[slot, span, :].astype(F32)
            centered = wide - jnp.mean(wide, -1, keepdims=True)
            normal = centered * lax.rsqrt(
                jnp.mean(centered * centered, -1, keepdims=True) + NORM_EPS
            )
            a1[slot, span, :] = (normal * norm_ref[0:1, :] + norm_ref[1:2, :]).astype(BF)
            a2[slot, span, :] = (normal * norm_ref[2:3, :] + norm_ref[3:4, :]).astype(BF)
            return carry

        lax.fori_loop(0, local // 128, body, 0)

    def lanes(ref, slot):
        return ref.at[:, pl.ds(slot * local, local)]

    x_next, x_core, x_far = ([], [], [])
    for span, wait in zip(spans, x_swaps):
        wait()
        x_next.append(copies.remote(xg.at[0, span], xg.at[1, span], place.next))
        x_core.append(copies.remote(xg.at[0, span], xg.at[2, span], place.core))
    normalise(0)
    small_swap()
    small_dp = [copies.remote(dp_rows(small, 0, rows), dp_rows(small, 0, rows), peer) for peer in place.dp_peers]
    if gathers_pair:
        pair_swap()
        own_pair = kvw.at[dp, rank]
        pair_next = copies.remote(own_pair, own_pair, place.next)
        pair_core = copies.remote(own_pair, own_pair, place.core)
    ids_swap()
    ids_next = copies.remote(lanes(idr, 0), lanes(idr, 1), place.next)
    ids_core = copies.remote(lanes(idr, 0), lanes(idr, 2), place.core)
    for span, copy in zip(spans, x_next):
        copy.wait_recv()
        x_far.append(copies.remote(xg.at[1, span], xg.at[3, span], place.core))
    if gathers_pair:
        pair_next.wait_recv()
        next_pair = kvw.at[dp, flip_one(rank)]
        pair_far = copies.remote(next_pair, next_pair, place.core)
    ids_next.wait_recv()
    ids_far = copies.remote(lanes(idr, 1), lanes(idr, 3), place.core)
    if gathers_pair:
        pair_core.wait_recv()
        pair_far.wait_recv()
        pair_dp = [copies.remote(kvw.at[dp], kvw.at[dp], peer) for peer in place.dp_peers]
    for copy in x_core:
        copy.wait_recv()
    normalise(2)
    c_next, c_core, c_far = ([], [], [])
    for span, wait in zip(spans, c_swaps):
        wait()
        c_next.append(copies.remote(cg.at[0, span], cg.at[1, span], place.next))
        c_core.append(copies.remote(cg.at[0, span], cg.at[2, span], place.core))
    normalise(1)
    for copy in x_far:
        copy.wait_recv()
    normalise(3)
    for copy in small_dp:
        copy.wait_recv()
    smt[...] = small[...].T
    if gathers_pair:
        for copy in pair_dp:
            copy.wait_recv()
        kvt[...] = kvw[...].reshape(D, 2 * HS).T
    else:
        kvw[...] = pair_ref[...]
        kvt[...] = pair_ref[...].T
    for slot in range(4):
        block = at_slot(slot, rank)
        table = pl.ds(pl.multiple_of(block * local, local), local)
        cosine, sine = (cos_ref[:, table], sin_ref[:, table])
        tokens = pl.ds(slot * local, local)
        queries = dot_nt(smt[0:query_width, :], a1[slot]) + qb_ref[...]
        for head in range(heads):
            turned = rotate(queries[head * HS : (head + 1) * HS], cosine, sine).astype(BF)
            qt[head * HS : (head + 1) * HS, tokens] = turned * jnp.asarray(1.0 / math.sqrt(HS), BF)
        pairs = dot_nt(kvt[...], a1[slot]) + kvb_ref[...]
        turned = rotate(pairs[:HS], cosine, sine).astype(BF)
        kt[:, tokens] = turned
        k[tokens, :] = turned.T
        value = pairs[HS:].astype(BF)
        vt[:, tokens] = value
        v[tokens, :] = value.T
    for span, copy in zip(spans, c_next):
        copy.wait_recv()
        c_far.append(copies.remote(cg.at[1, span], cg.at[3, span], place.core))
    for copy in c_core + c_far:
        copy.wait_recv()
    for slot in range(4):
        tokens = pl.ds(slot * local, local)
        dot_rows[:, tokens] = dot_nt(smt[query_width:, :], cg[slot]).astype(BF)
    big_dp = []

    def big_send(at):
        big_swaps[at]()
        part = dp_rows(big, at * chunk, chunk)
        big_dp.extend(copies.remote(part, part, peer) for peer in place.dp_peers)

    for copy in (ids_core, ids_far):
        copy.wait_recv()
    ids = idr[...].astype(F32)
    first_end = jnp.sum(jnp.where(ids < 0.5, 1.0, 0.0), 1, keepdims=True)
    second_end = jnp.sum(jnp.where(ids < 1.5, 1.0, 0.0), 1, keepdims=True)

    def document(position):
        position = position.astype(F32)
        return jnp.where(position < first_end, 0.0, jnp.where(position < second_end, 1.0, 2.0))

    dk[...] = jnp.zeros_like(dk)
    dv[...] = jnp.zeros_like(dv)
    tiles = length // TILE
    per = tiles // 4

    def tile_at(tile):
        return pl.multiple_of(at_slot(tile // per, rank) * local + (tile % per) * TILE, TILE)

    def masked(scores, key, query):
        edge = key == 0 or query == tiles - 1
        allowed = None
        if key == query:
            down = lax.broadcasted_iota(jnp.int32, (TILE, TILE), 0)
            allowed = down <= lax.broadcasted_iota(jnp.int32, (TILE, TILE), 1)
        if edge:
            down = document(lax.broadcasted_iota(jnp.int32, (TILE, 1), 0) + key * TILE)
            along = document(lax.broadcasted_iota(jnp.int32, (1, TILE), 1) + query * TILE)
            same = down == along
            allowed = same if allowed is None else allowed & same
        return scores if allowed is None else jnp.where(allowed, scores, -1e9)

    def one_head(head, carry):
        own = pl.ds(pl.multiple_of(head * HS, HS), HS)
        for query in range(tiles):
            at_q = pl.ds(tile_at(query), TILE)
            q, do = (qt[own, at_q], dot_rows[own, at_q])
            scaled = do * jnp.asarray(1.0 / math.sqrt(HS), BF)
            highest = jnp.full((1, TILE), -jnp.inf, F32)
            for key in range(query + 1):
                at_k = pl.ds(tile_at(key), TILE)
                at_s = pl.ds(key * TILE, TILE)
                scores = masked(dot(k[at_k, :], q), key, query)
                s_ref[at_s, :] = scores
                highest = jnp.maximum(highest, jnp.max(scores, 0, keepdims=True))
                d_ref[at_s, :] = dot(v[at_k, :], scaled)
            total = jnp.zeros((1, TILE), F32)
            inner = jnp.zeros((1, TILE), F32)
            for key in range(query + 1):
                at_s = pl.ds(key * TILE, TILE)
                exponent = jnp.exp(s_ref[at_s, :] - highest)
                s_ref[at_s, :] = exponent
                total = total + jnp.sum(exponent, 0, keepdims=True)
                inner = inner + jnp.sum(exponent * d_ref[at_s, :], 0, keepdims=True)
            inverse = 1.0 / total
            inner = inner * inverse
            mixed = jnp.zeros((HS, TILE), F32)
            query_grad = jnp.zeros((HS, TILE), F32)
            for key in range(query + 1):
                at_k = pl.ds(tile_at(key), TILE)
                at_s = pl.ds(key * TILE, TILE)
                softmax = s_ref[at_s, :] * inverse
                low = softmax.astype(BF)
                score_grad = (softmax * (d_ref[at_s, :] - inner)).astype(BF)
                mixed = mixed + dot(vt[:, at_k], low)
                query_grad = query_grad + dot(kt[:, at_k], score_grad)
                dk[at_k, :] += dot_nt(score_grad, q)
                dv[at_k, :] += dot_nt(low, do)
            ot[own, at_q] = mixed.astype(BF)
            table = pl.ds(query * TILE, TILE)
            dqt[own, at_q] = rotate(query_grad, cos_ref[:, table], -sin_ref[:, table]).astype(BF)
        return carry

    lax.fori_loop(0, heads, one_head, 0)
    for at in range(len(big_swaps)):
        big_send(at)
    for slot in range(4):
        block = at_slot(slot, rank)
        table = pl.ds(pl.multiple_of(block * local, local), local)
        tokens = pl.ds(slot * local, local)
        key_grad = dk[tokens, :].T * math.sqrt(HS)
        pair_grad[0:HS, tokens] = rotate(key_grad, cos_ref[:, table], -sin_ref[:, table])
        pair_grad[HS:, tokens] = dv[tokens, :].T
    for copy in big_dp:
        copy.wait_recv()
    copies.finish()


def first_pass(dp_size, x, c, small, big, pair, ids, norms, qb, kvb, cosine, sine):
    local = x.shape[0]
    length = 4 * local
    width = small.shape[1]
    query_width = width // 2
    gathers_pair = pair.shape[0] != D
    outs = [
        ((4, local, D), BF),
        ((4, local, D), BF),
        ((4, local, D), BF),
        ((4, local, D), BF),
        ((D, big.shape[1]), BF),
        ((D, width), BF),
        ((dp_size, 4, pair.shape[0], 2 * HS) if gathers_pair else (D, 2 * HS), BF),
        ((query_width, length), BF),
        ((query_width, length), BF),
        ((2 * HS, length), F32),
    ]
    vmem = pl.BlockSpec(memory_space=pltpu.VMEM)
    copies = 40 + 8 * dp_size
    work = query_width * length * length
    return pl.pallas_call(
        functools.partial(first_kernel, dp_size),
        out_shape=[jax.ShapeDtypeStruct(shape, kind) for shape, kind in outs],
        in_specs=[vmem] * 11,
        out_specs=[vmem] * len(outs),
        scratch_shapes=[
            pltpu.VMEM((width, D), BF),
            pltpu.VMEM((2 * HS, D), BF),
            pltpu.VMEM((query_width, length), BF),
            pltpu.VMEM((query_width, length), BF),
            pltpu.VMEM((HS, length), BF),
            pltpu.VMEM((HS, length), BF),
            pltpu.VMEM((length, HS), BF),
            pltpu.VMEM((length, HS), BF),
            pltpu.VMEM((length, HS), F32),
            pltpu.VMEM((length, HS), F32),
            pltpu.VMEM((length, TILE), F32),
            pltpu.VMEM((length, TILE), F32),
            pltpu.VMEM((1, length), jnp.int32),
            pltpu.SemaphoreType.DMA((copies,)),
            pltpu.SemaphoreType.DMA((copies,)),
        ],
        compiler_params=pltpu.CompilerParams(
            collective_id=0, has_side_effects=True, vmem_limit_bytes=52 << 20
        ),
        cost_estimate=pl.CostEstimate(
            flops=40 * work, bytes_accessed=24 << 20, transcendentals=work // HS
        ),
        name="gather_attend",
    )(x, c, small, big, pair, ids, norms, qb, kvb, cosine, sine)

def shards(
    hidden_in,
    doc_ids,
    out_cotangent,
    entry_weight,
    entry_first,
    entry_second,
    entry_anchor,
    entry_velocity,
    exit_weight,
    exit_first,
    exit_second,
    exit_anchor,
    exit_velocity,
    shared_weight,
    shared_first,
    shared_second,
    shared_anchor,
    shared_velocity,
    vector_weight,
    vector_first,
    vector_second,
    vector_anchor,
    vector_velocity,
):
    batch, local_len = hidden_in.shape[:2]
    parts = lax.axis_size("mp")
    group, rank = (lax.axis_index("group"), lax.axis_index("mp"))
    is_swapped = (group % 2) != (rank // 2)
    rank = jnp.where(is_swapped, jnp.bitwise_xor(rank, 2), rank)
    length = local_len * parts
    part_width = entry_weight.shape[2]
    query_width = HEADS * HS // parts
    heads = query_width // HS

    home_vector = vector_weight[0]
    vector = jnp.where(is_swapped, over_core(home_vector), home_vector)
    gain_one, shift_one = (vector[0:D], vector[D : 2 * D])
    gain_two, shift_two = (vector[2 * D : 3 * D], vector[3 * D : 4 * D])
    home_bias = home_vector[4 * D : 5 * D] + home_vector[5 * D : 6 * D]
    pair_bias = vector[6 * D : 6 * D + 2 * HS]
    in_bias = lax.dynamic_slice_in_dim(vector, 6 * D + 2 * HS + rank * part_width, part_width, 0)
    query_bias = in_bias[:query_width]
    up_bias = in_bias[query_width:]

    dp_size = lax.axis_size("dp")
    order = jnp.bitwise_xor(jnp.arange(parts), rank)
    small = jnp.concatenate(
        [entry_weight[0, :, :query_width], exit_weight[0, :query_width].T], 1
    ).astype(BF)
    big = jnp.concatenate(
        [entry_weight[0, :, query_width:], exit_weight[0, query_width:].T], 1
    ).astype(BF)
    pair_piece = shared_weight[0].astype(BF)
    if pair_piece.shape[0] % 16:
        pieces = gather_square(swapped_parts(pair_piece))
        pieces = jnp.take(pieces, order, axis=0)
        pair_piece = gather_dp(pieces.reshape(-1, 2 * HS), 0)
    half = ROT // 2
    frequency = 10000.0 ** (-(np.arange(half) * 2.0 / ROT))
    angles = frequency.astype(np.float32)[:, None] * np.arange(length, dtype=np.float32)[None, :]
    cosine_table = jnp.asarray(np.cos(angles.astype(np.float64)).astype(np.float32))
    sine_table = jnp.asarray(np.sin(angles.astype(np.float64)).astype(np.float32))
    inputs, cots, attn_input, ffn_input, big, small, pair_weight, attended, query_grad, pair_rows = (
        first_pass(
            dp_size,
            hidden_in[0],
            out_cotangent[0],
            small,
            big,
            pair_piece,
            doc_ids,
            vector[: 4 * D].reshape(4, D),
            query_bias[:, None],
            pair_bias[:, None],
            cosine_table,
            sine_table,
        )
    )
    inputs, cots, attn_input, ffn_input = (
        a.reshape(length, D) for a in (inputs, cots, attn_input, ffn_input)
    )
    query_weight, attend_turned = (small[:, :query_width], small[:, query_width:])
    up_weight, down_turned = (big[:, : part_width - query_width], big[:, part_width - query_width :])
    pair_weight = pair_weight.reshape(D, 2 * HS)
    wide = inputs.astype(F32)
    centered = wide - jnp.mean(wide, -1, keepdims=True)
    normal = centered * lax.rsqrt(jnp.mean(centered * centered, -1, keepdims=True) + NORM_EPS)

    hidden_pre = dot(ffn_input, up_weight) + up_bias
    half_root = math.sqrt(0.5)
    below = 0.5 * (1.0 + lax.erf(hidden_pre * half_root))
    hidden = (hidden_pre * below).astype(BF)
    density = jnp.exp(-0.5 * hidden_pre * hidden_pre) * (1.0 / math.sqrt(2.0 * math.pi))
    slope = below + hidden_pre * density

    partial_sum = lax.dot_general(
        attended, attend_turned, (((0,), (1,)), ((), ())), preferred_element_type=F32
    ) + dot_nt(hidden, down_turned)
    branch = scatter_square(partial_sum.reshape(parts, local_len, D), BF)
    block_output = (
        hidden_in[0].astype(F32) + swapped_parts(branch.astype(BF)).astype(F32) + home_bias
    )

    grad_attend = dot(attended, cots)
    grad_down = dot_tn(hidden, cots)
    pre_grad = (dot(cots, down_turned) * slope).astype(BF)
    grad_up = dot_tn(ffn_input, pre_grad)
    ffn_input_grad = dot_nt(pre_grad, up_weight)
    up_bias_grad = jnp.sum(pre_grad.astype(F32), 0)
    pair_partial = pair_rows.T
    grad_query = dot(query_grad, attn_input).T
    attn_input_grad = lax.dot_general(
        query_grad, query_weight, (((0,), (1,)), ((), ())), preferred_element_type=F32
    )
    query_bias_grad = jnp.sum(query_grad.astype(F32), 1)
    joined = attn_input_grad * gain_one + ffn_input_grad * gain_two
    joined_own = scatter_square(joined.reshape(parts, local_len, D), BF)
    pair_low = scatter_square(pair_partial.reshape(parts, local_len, 2 * HS), F32).astype(BF)
    pair_input_grad = dot_nt(pair_low, pair_weight)
    joined_own = joined_own + pair_input_grad * gain_one
    joined_home = swapped_parts(joined_own.astype(BF)).astype(F32)
    home_wide = hidden_in[0].astype(F32)
    home_centered = home_wide - jnp.mean(home_wide, -1, keepdims=True)
    home_scale = lax.rsqrt(jnp.mean(home_centered * home_centered, -1, keepdims=True) + NORM_EPS)
    home_normal = home_centered * home_scale
    input_grad = out_cotangent[0].astype(F32) + home_scale * (
        joined_home
        - jnp.mean(joined_home, -1, keepdims=True)
        - home_normal * jnp.mean(joined_home * home_normal, -1, keepdims=True)
    )

    own_normal = normal[:local_len]
    own_attn = attn_input[:local_len]
    grad_pair = dot_tn(own_attn, pair_low)
    out_bias_grad = jnp.sum(cots[:local_len].astype(F32), 0)
    leading_grads = jnp.concatenate(
        [
            jnp.sum(attn_input_grad * normal, 0) + jnp.sum(pair_input_grad * own_normal, 0),
            jnp.sum(attn_input_grad, 0) + jnp.sum(pair_input_grad, 0),
            jnp.sum(ffn_input_grad * normal, 0),
            jnp.sum(ffn_input_grad, 0),
            out_bias_grad,
            out_bias_grad,
            jnp.sum(pair_low.astype(F32), 0),
        ]
    )
    bias_tail = lax.dynamic_update_slice(
        jnp.zeros((IN_COLS,), F32),
        jnp.concatenate([query_bias_grad, up_bias_grad]),
        (rank * part_width,),
    )
    vector_grad = swapped_parts(
        sum_dp(sum_square(jnp.concatenate([leading_grads, bias_tail])))
    )
    entry_grad = scatter_dp(jnp.concatenate([grad_query, grad_up], 1), 0, BF)
    exit_grad = scatter_dp(jnp.concatenate([grad_attend, grad_down], 0), 1, BF)
    entry_grad = jnp.where(
        is_swapped, swapped_parts(entry_grad.astype(BF)).astype(F32), entry_grad
    )
    exit_grad = jnp.where(is_swapped, swapped_parts(exit_grad.astype(BF)).astype(F32), exit_grad)
    grad_pieces = grad_pair.reshape(lax.axis_size("dp"), parts, -1, 2 * HS)
    grad_pieces = jnp.take(grad_pieces, order, axis=1).swapaxes(0, 1)
    shared_grad = scatter_dp(scatter_square(grad_pieces, F32), 0, F32)
    shared_grad = swapped_parts(shared_grad.reshape(-1, 2 * HS))

    entry_m, entry_v, entry_new = adamw_update(
        entry_weight[0], entry_first[0], entry_second[0], entry_grad, MATRIX_RATE, MATRIX_DECAY
    )
    exit_m, exit_v, exit_new = adamw_update(
        exit_weight[0], exit_first[0], exit_second[0], exit_grad, MATRIX_RATE, MATRIX_DECAY
    )
    shared_m, shared_v, shared_new = adamw_update(
        shared_weight[0], shared_first[0], shared_second[0], shared_grad, MATRIX_RATE, MATRIX_DECAY
    )
    vector_m, vector_v, vector_new = adamw_update(
        home_vector, vector_first[0], vector_second[0], vector_grad, VECTOR_RATE, 0.0
    )
    group_count = lax.axis_size("group")
    vector_gap = vector_anchor - vector_new
    vector_gap = vector_gap + over_core(vector_gap)
    summed = (
        sum_groups(entry_anchor - entry_new, BF),
        sum_groups(exit_anchor - exit_new, BF),
        sum_groups(shared_anchor - shared_new, F32),
        vector_gap + over_half(vector_gap),
    )
    anchors = (entry_anchor, exit_anchor, shared_anchor, vector_anchor)
    velocities = (entry_velocity, exit_velocity, shared_velocity, vector_velocity)
    outer_parts = []
    for position in range(4):
        change = summed[position] / group_count
        momentum = OUTER_BETA * velocities[position] + change
        outer_parts.append(
            (change, momentum, anchors[position] - OUTER_RATE * (change + OUTER_BETA * momentum))
        )
    return (
        (block_output[None], input_grad[None], entry_m[None], entry_v[None], entry_new[None])
        + outer_parts[0]
        + (exit_m[None], exit_v[None], exit_new[None])
        + outer_parts[1]
        + (shared_m[None], shared_v[None], shared_new[None])
        + outer_parts[2]
        + (vector_m[None], vector_v[None], vector_new[None])
        + outer_parts[3]
    )


def solution(mesh):
    in_specs = (
        P(("group", "dp"), "mp", None),
        P(("group", "dp"), "mp"),
        P(("group", "dp"), "mp", None),
        P("group", "dp", "mp"),
        P("group", "dp", "mp"),
        P("group", "dp", "mp"),
        P("dp", "mp"),
        P("dp", "mp"),
        P("group", "mp", "dp"),
        P("group", "mp", "dp"),
        P("group", "mp", "dp"),
        P("mp", "dp"),
        P("mp", "dp"),
        P("group", ("dp", "mp"), None),
        P("group", ("dp", "mp"), None),
        P("group", ("dp", "mp"), None),
        P(("dp", "mp"), None),
        P(("dp", "mp"), None),
        P("group", None),
        P("group", None),
        P("group", None),
        P(),
        P(),
    )
    out_specs = (
        P(("group", "dp"), "mp", None),
        P(("group", "dp"), "mp", None),
        P("group", "dp", "mp"),
        P("group", "dp", "mp"),
        P("group", "dp", "mp"),
        P("dp", "mp"),
        P("dp", "mp"),
        P("dp", "mp"),
        P("group", "mp", "dp"),
        P("group", "mp", "dp"),
        P("group", "mp", "dp"),
        P("mp", "dp"),
        P("mp", "dp"),
        P("mp", "dp"),
        P("group", ("dp", "mp"), None),
        P("group", ("dp", "mp"), None),
        P("group", ("dp", "mp"), None),
        P(("dp", "mp"), None),
        P(("dp", "mp"), None),
        P(("dp", "mp"), None),
        P("group", None),
        P("group", None),
        P("group", None),
        P(),
        P(),
        P(),
    )
    return jax.shard_map(shards, mesh=mesh, in_specs=in_specs, out_specs=out_specs, check_vma=False)
```

```python
import functools
import math

import jax
import jax.numpy as jnp
import numpy as np
from jax import lax
from jax.experimental import pallas as pl
from jax.experimental.pallas import tpu as pltpu
from jax.sharding import PartitionSpec as P

D = 768
HEADS = 12
HS = 64
ROT = 16
STEP = 5
IN_COLS = 3840


NORM_EPS = 1e-05
BETA_ONE = 0.9
BETA_TWO = 0.95
ADAM_EPS = 1e-08
MATRIX_RATE = 0.03
MATRIX_DECAY = 0.1
VECTOR_RATE = 0.3
OUTER_RATE = 0.7
OUTER_BETA = 0.9

TILE = 256
F32 = jnp.float32
BF = jnp.bfloat16


def dot(left, right):
    return jnp.dot(left, right, preferred_element_type=F32)


def dot_nt(left, right):
    return lax.dot_general(left, right, (((1,), (1,)), ((), ())), preferred_element_type=F32)


def dot_tn(left, right):
    return lax.dot_general(left, right, (((0,), (0,)), ((), ())), preferred_element_type=F32)


def adamw_update(weight, first, second, gradient, step_rate, decay):
    first_new = BETA_ONE * first + (1.0 - BETA_ONE) * gradient
    second_new = BETA_TWO * second + (1.0 - BETA_TWO) * gradient * gradient
    fix_first = 1.0 - BETA_ONE**STEP
    fix_second = 1.0 - BETA_TWO**STEP
    update = first_new / fix_first / (jnp.sqrt(second_new / fix_second) + ADAM_EPS)
    return (first_new, second_new, weight - step_rate * (update + decay * weight))


def pairs_of(size, bit):
    return [(at, at ^ bit) for at in range(size)]


def over_core(array):
    return lax.ppermute(array, "group", pairs_of(lax.axis_size("group"), 1))


def over_half(array):
    return lax.ppermute(array, "group", pairs_of(lax.axis_size("group"), 2))


def over_next(array):
    return lax.ppermute(array, "mp", pairs_of(lax.axis_size("mp"), 1))


def over_dp(array):
    return lax.ppermute(array, "dp", pairs_of(2, 1))


def swapped_parts(array):
    parts = lax.axis_size("mp")
    pairs = []
    for group in range(lax.axis_size("group")):
        for rank in range(parts):
            here = group * parts + rank
            there = (group ^ 1) * parts + (rank ^ 2)
            pairs.append((here, there if group % 2 != rank // 2 else here))
    return lax.ppermute(array, ("group", "mp"), pairs)


def gather_square(own):
    pair = jnp.stack([own, over_next(own)])
    return jnp.concatenate([pair, over_core(pair)], 0)


def scatter_square(slots, send_type):
    pair = slots[:2] + over_core(slots[2:].astype(send_type)).astype(F32)
    return pair[0] + over_next(pair[1].astype(send_type)).astype(F32)


def sum_square(array):
    array = array + over_core(array)
    return array + over_next(array)


def gather_dp(own, axis):
    if lax.axis_size("dp") == 2:
        other = over_dp(own)
        first = lax.axis_index("dp") == 0
        return jnp.concatenate(
            [jnp.where(first, own, other), jnp.where(first, other, own)], axis
        )
    return lax.all_gather(own, "dp", axis=axis, tiled=True)


def scatter_dp(array, axis, send_type):
    if lax.axis_size("dp") == 2:
        size = array.shape[axis] // 2
        mine = lax.axis_index("dp")
        kept = lax.dynamic_slice_in_dim(array, mine * size, size, axis)
        sent = lax.dynamic_slice_in_dim(array, (1 - mine) * size, size, axis)
        return kept + over_dp(sent.astype(send_type)).astype(F32)
    return lax.psum_scatter(array, "dp", scatter_dimension=axis, tiled=True)


def sum_dp(array):
    if lax.axis_size("dp") == 2:
        return array + over_dp(array)
    return lax.psum(array, "dp")


def sum_groups(array, send_type):
    size = array.shape[0] // 2
    core = lax.axis_index("group") % 2
    kept = lax.dynamic_slice_in_dim(array, core * size, size, 0)
    sent = lax.dynamic_slice_in_dim(array, (1 - core) * size, size, 0)
    part = (kept + over_core(sent)).astype(send_type)
    part = part.astype(F32) + over_half(part).astype(F32)
    other = over_core(part)
    low = core == 0
    return jnp.concatenate([jnp.where(low, part, other), jnp.where(low, other, part)], 0)


def flip_one(index):
    return index + 1 - 2 * (index % 2)


def flip_two(index):
    return index + 2 - 4 * ((index // 2) % 2)


def at_slot(slot, rank):
    rank = flip_one(rank) if slot % 2 else rank
    return flip_two(rank) if slot // 2 else rank


class Copies:
    def __init__(self, send, receive):
        self.send, self.receive, self.used, self.sends = (send, receive, 0, [])

    def remote(self, source, target, device, starts=True):
        at = self.used
        self.used += 1
        copy = pltpu.make_async_remote_copy(
            src_ref=source,
            dst_ref=target,
            send_sem=self.send.at[at],
            recv_sem=self.receive.at[at],
            device_id=device,
            device_id_type=pl.DeviceIdType.MESH,
        )
        if starts:
            copy.start()
        self.sends.append(copy)
        return copy

    def swapped(self, source, target, is_swapped, device):
        at = self.used
        self.used += 1
        far = pltpu.make_async_remote_copy(
            src_ref=source,
            dst_ref=target,
            send_sem=self.send.at[at],
            recv_sem=self.receive.at[at],
            device_id=device,
            device_id_type=pl.DeviceIdType.MESH,
        )
        near = pltpu.make_async_copy(source, target, self.receive.at[at])

        def start():
            @pl.when(is_swapped)
            def _():
                far.start()

            @pl.when(jnp.logical_not(is_swapped))
            def _():
                near.start()

        def wait():
            @pl.when(is_swapped)
            def _():
                far.wait_send()
                far.wait_recv()

            @pl.when(jnp.logical_not(is_swapped))
            def _():
                near.wait()

        return (start, wait)

    def homeward(self, source, target, device):
        at = self.used
        self.used += 1
        return pltpu.make_async_remote_copy(
            src_ref=source,
            dst_ref=target,
            send_sem=self.send.at[at],
            recv_sem=self.receive.at[at],
            device_id=device,
            device_id_type=pl.DeviceIdType.MESH,
        )

    def sent(self, copy):
        copy.wait_send()
        self.sends = [other for other in self.sends if other is not copy]

    def finish(self):
        for copy in self.sends:
            copy.wait_send()


class Place:
    def __init__(self, dp_size):
        group, self.dp, home = (lax.axis_index("group"), lax.axis_index("dp"), lax.axis_index("mp"))
        core, upper = (group % 2, home // 2)
        self.is_swapped = core != upper
        self.home = home
        self.rank = jnp.where(self.is_swapped, flip_two(home), home)
        self.swap = {"group": flip_one(group), "mp": flip_two(home)}
        self.core = {"group": flip_one(group)}
        self.next = {"mp": flip_one(home)}
        self.dp_peers = [{"dp": (self.dp + step) % dp_size} for step in range(1, dp_size)]

    def meet(self):
        barrier = pltpu.get_barrier_semaphore()
        peers = [self.core, self.next, self.swap] + self.dp_peers
        for peer in peers:
            pl.semaphore_signal(
                barrier, inc=1, device_id=peer, device_id_type=pl.DeviceIdType.MESH
            )
        pl.semaphore_wait(barrier, len(peers))


def column_of(row):
    size = row.shape[1]
    down = lax.broadcasted_iota(jnp.int32, (size, size), 0)
    along = lax.broadcasted_iota(jnp.int32, (size, size), 1)
    return jnp.sum(jnp.where(down == along, row, 0.0), 1, keepdims=True)


def rotate(rows, cosine, sine):
    half = ROT // 2
    one, two = (rows[:half], rows[half:ROT])
    return jnp.concatenate(
        [one * cosine - two * sine, two * cosine + one * sine, rows[ROT:]], 0
    )


def first_kernel(
    dp_size, x_ref, c_ref, entry_ref, exit_ref, shared_ref, ids_ref, vector_ref, cos_ref, sin_ref,
    xg, cg, a1, h, dh, big, small, kvw, ot, dqt, pair_grad, norm_ref, ub_grad, big_own,
    small_ref, big_ref, pair_ref, vector_other, qb_ref, kvb_ref, big_land, a2, smt, kvt, qt, dot_rows, kt, vt, k, v, dk, dv, s_ref, d_ref, l_ref, idr,
    g_send, g_recv, g_swap, send, receive,
):
    place = Place(dp_size)
    rank, dp = (place.rank, place.dp)
    copies = Copies(send, receive)
    local = x_ref.shape[0]
    length = 4 * local
    rows = entry_ref.shape[0]
    query_width = small_ref.shape[1] // 2
    heads = query_width // HS
    gathers_pair = shared_ref.shape[0] != D
    place.meet()
    vector_core = copies.remote(vector_ref, vector_other, place.core)

    def swapped(source, target):
        return copies.swapped(source, target, place.is_swapped, place.swap)

    def dp_rows(ref, start, size):
        return ref.at[pl.ds(pl.multiple_of(dp * rows + start, 16), size)]

    step = local // 2
    spans = [pl.ds(at * step, step) for at in range(2)]
    x_swaps = [swapped(x_ref.at[s], xg.at[0, s]) for s in spans]
    c_swaps = [swapped(c_ref.at[s], cg.at[0, s]) for s in spans]
    small_swap = swapped(small_ref, dp_rows(small, 0, rows))
    ids_swap = swapped(ids_ref, idr.at[:, pl.ds(0, local)])
    chunk = rows // 8 if rows % 128 == 0 else rows
    big_swaps = [
        swapped(big_ref.at[pl.ds(at, chunk)], dp_rows(big, at, chunk)) for at in range(0, rows, chunk)
    ]
    first = [ids_swap]
    if gathers_pair:
        pair_swap = swapped(pair_ref, kvw.at[dp, place.home])
        first.append(pair_swap)
    queue = iter([start for start, _ in x_swaps + [small_swap] + c_swaps])

    def start_next():
        start = next(queue, None)
        if start is not None:
            start()

    start_next()
    start_next()
    if gathers_pair:
        pair_ref[...] = shared_ref[...].astype(BF)
    for start, _ in first:
        start()
    small_ref[:, :query_width] = entry_ref[:, :query_width].astype(BF)
    small_ref[:, query_width:] = exit_ref[:query_width, :].T.astype(BF)
    wide = big_ref.shape[1] // 2
    big_ref[:, :wide] = entry_ref[:, query_width:].astype(BF)
    big_ref[:, wide:] = exit_ref[query_width:, :].T.astype(BF)
    vector_core.wait_recv()

    def role_vector(start, size):
        span = slice(start, start + size)
        return jnp.where(place.is_swapped, vector_other[:, span], vector_ref[:, span])

    for at in range(4):
        norm_ref[at : at + 1, :] = role_vector(at * D, D)
    kvb_ref[...] = column_of(role_vector(6 * D, 2 * HS))
    part = query_width + wide
    tail = 6 * D + 2 * HS
    in_bias = role_vector(tail, part)
    for at in range(1, 4):
        in_bias = jnp.where(rank == at, role_vector(tail + at * part, part), in_bias)
    qb_ref[...] = column_of(in_bias[:, :query_width])
    norm_ref[4:5, :] = in_bias[:, query_width:]

    def normalise(slot):
        def body(at, carry):
            span = pl.ds(pl.multiple_of(at * 128, 128), 128)
            wide = xg[slot, span, :].astype(F32)
            centered = wide - jnp.mean(wide, -1, keepdims=True)
            normal = centered * lax.rsqrt(
                jnp.mean(centered * centered, -1, keepdims=True) + NORM_EPS
            )
            a1[slot, span, :] = (normal * norm_ref[0:1, :] + norm_ref[1:2, :]).astype(BF)
            a2[slot, span, :] = (normal * norm_ref[2:3, :] + norm_ref[3:4, :]).astype(BF)
            return carry

        lax.fori_loop(0, local // 128, body, 0)

    def lanes(ref, slot):
        return ref.at[:, pl.ds(slot * local, local)]

    x_next, x_core, x_far = ([], [], [])
    for span, (_, wait) in zip(spans, x_swaps):
        wait()
        start_next()
        x_next.append(copies.remote(xg.at[0, span], xg.at[1, span], place.next))
        x_core.append(copies.remote(xg.at[0, span], xg.at[2, span], place.core))
    small_swap[1]()
    start_next()
    small_dp = [copies.remote(dp_rows(small, 0, rows), dp_rows(small, 0, rows), peer) for peer in place.dp_peers]
    ids_swap[1]()
    ids_next = copies.remote(lanes(idr, 0), lanes(idr, 1), place.next)
    ids_core = copies.remote(lanes(idr, 0), lanes(idr, 2), place.core)
    if gathers_pair:
        pair_swap[1]()
        own_pair = kvw.at[dp, rank]
        pair_next = copies.remote(own_pair, own_pair, place.next)
        pair_core = copies.remote(own_pair, own_pair, place.core)
    normalise(0)
    for span, copy in zip(spans, x_next):
        copy.wait_recv()
        x_far.append(copies.remote(xg.at[1, span], xg.at[3, span], place.core))
    ids_next.wait_recv()
    ids_far = copies.remote(lanes(idr, 1), lanes(idr, 3), place.core)
    if gathers_pair:
        pair_next.wait_recv()
        next_pair = kvw.at[dp, flip_one(rank)]
        pair_far = copies.remote(next_pair, next_pair, place.core)
        pair_core.wait_recv()
        pair_far.wait_recv()
        pair_dp = [copies.remote(kvw.at[dp], kvw.at[dp], peer) for peer in place.dp_peers]
    c_next, c_core, c_far, big_dp = ([], [], [], [])
    for span in spans:
        c_next.append(copies.remote(cg.at[0, span], cg.at[1, span], place.next, starts=False))
        c_core.append(copies.remote(cg.at[0, span], cg.at[2, span], place.core, starts=False))
        c_far.append(copies.remote(cg.at[1, span], cg.at[3, span], place.core, starts=False))
    for at in range(0, rows, chunk):
        part = dp_rows(big, at, chunk)
        big_dp.append([copies.remote(part, part, peer, starts=False) for peer in place.dp_peers])

    def c_arrives(at):
        c_swaps[at][1]()
        if at < len(big_swaps):
            big_swaps[at][0]()
        c_next[at].start()
        c_core[at].start()

    def c_passes(at):
        c_next[at].wait_recv()
        c_far[at].start()

    def big_arrives(at):
        big_swaps[at][1]()
        if at + 2 < len(big_swaps):
            big_swaps[at + 2][0]()
        for copy in big_dp[at]:
            copy.start()

    events = [functools.partial(big_arrives, at) for at in range(len(big_swaps))]
    events[2:2] = [functools.partial(c_passes, 0)]
    events[5:5] = [functools.partial(c_passes, 1)]
    for copy in x_core:
        copy.wait_recv()
    normalise(2)
    normalise(1)
    for copy in x_far:
        copy.wait_recv()
    normalise(3)
    for copy in small_dp:
        copy.wait_recv()
    smt[...] = small[...].T
    if gathers_pair:
        for copy in pair_dp:
            copy.wait_recv()
        kvt[...] = kvw[...].reshape(D, 2 * HS).T
    else:
        kvw[...] = shared_ref[...]
        kvt[...] = shared_ref[...].T
    c_arrives(0)
    for slot in range(4):
        block = at_slot(slot, rank)
        table = pl.ds(pl.multiple_of(block * local, local), local)
        cosine, sine = (cos_ref[:, table], sin_ref[:, table])
        tokens = pl.ds(slot * local, local)
        queries = dot_nt(smt[0:query_width, :], a1[slot]) + qb_ref[...]
        for head in range(heads):
            turned = rotate(queries[head * HS : (head + 1) * HS], cosine, sine).astype(BF)
            qt[head * HS : (head + 1) * HS, tokens] = turned * jnp.asarray(1.0 / math.sqrt(HS), BF)
        pairs = dot_nt(kvt[...], a1[slot]) + kvb_ref[...]
        turned = rotate(pairs[:HS], cosine, sine).astype(BF)
        kt[:, tokens] = turned
        k[tokens, :] = turned.T
        value = pairs[HS:].astype(BF)
        vt[:, tokens] = value
        v[tokens, :] = value.T
    c_arrives(1)
    for copy in (ids_core, ids_far):
        copy.wait_recv()
    ids = idr[...].astype(F32)
    first_end = jnp.sum(jnp.where(ids < 0.5, 1.0, 0.0), 1, keepdims=True)
    second_end = jnp.sum(jnp.where(ids < 1.5, 1.0, 0.0), 1, keepdims=True)

    def document(position):
        position = position.astype(F32)
        return jnp.where(position < first_end, 0.0, jnp.where(position < second_end, 1.0, 2.0))

    tiles = length // TILE
    per = tiles // 4

    def tile_at(tile):
        return pl.multiple_of(at_slot(tile // per, rank) * local + (tile % per) * TILE, TILE)

    def masked(scores, key, query):
        edge = key == 0 or query == tiles - 1
        allowed = None
        if key == query:
            down = lax.broadcasted_iota(jnp.int32, (TILE, TILE), 0)
            allowed = down <= lax.broadcasted_iota(jnp.int32, (TILE, TILE), 1)
        if edge:
            down = document(lax.broadcasted_iota(jnp.int32, (TILE, 1), 0) + key * TILE)
            along = document(lax.broadcasted_iota(jnp.int32, (1, TILE), 1) + query * TILE)
            same = down == along
            allowed = same if allowed is None else allowed & same
        return scores if allowed is None else jnp.where(allowed, scores, -1e9)

    def hooks(head, query, todo, first):
        for at, event in enumerate(todo):
            if query == first + at % (tiles - first):

                @pl.when(head == at // (tiles - first))
                def _():
                    event()

    def forward_head(head, carry):
        own = pl.ds(pl.multiple_of(head * HS, HS), HS)
        for query in range(tiles):
            hooks(head, query, events, 3)
            at_q = pl.ds(tile_at(query), TILE)
            q = qt[own, at_q]
            highest = jnp.full((1, TILE), -jnp.inf, F32)
            for key in range(query + 1):
                scores = masked(dot(k[pl.ds(tile_at(key), TILE), :], q), key, query)
                s_ref[pl.ds(key * TILE, TILE), :] = scores
                highest = jnp.maximum(highest, jnp.max(scores, 0, keepdims=True))
            total = jnp.zeros((1, TILE), F32)
            for key in range(query + 1):
                exponent = jnp.exp(s_ref[pl.ds(key * TILE, TILE), :] - highest)
                s_ref[pl.ds(key * TILE, TILE), :] = exponent
                total = total + jnp.sum(exponent, 0, keepdims=True)
            inverse = 1.0 / total
            mixed = jnp.zeros((HS, TILE), F32)
            for key in range(query + 1):
                softmax = (s_ref[pl.ds(key * TILE, TILE), :] * inverse).astype(BF)
                mixed = mixed + dot(vt[:, pl.ds(tile_at(key), TILE)], softmax)
            ot[own, at_q] = mixed.astype(BF)
            l_ref[head, :, at_q] = jnp.broadcast_to(highest + jnp.log(total), (8, TILE))
        return carry

    lax.fori_loop(0, heads, forward_head, 0)
    for event in events[heads * (tiles - 3) :]:
        event()

    for copy in c_core + c_far:
        copy.wait_recv()
    for copy in sum(big_dp, []):
        copy.wait_recv()
    ub_grad[...] = jnp.zeros_like(ub_grad)

    def perceptron(slot, carry):
        for at in range(0, local, TILE):
            span = pl.ds(at, TILE)
            pre = dot(a2[slot, span, :], big[:, :wide]) + norm_ref[4:5, :]
            below = 0.5 * (1.0 + lax.erf(pre * math.sqrt(0.5)))
            h[slot, span, :] = (pre * below).astype(BF)
            density = jnp.exp(-0.5 * pre * pre) * (1.0 / math.sqrt(2.0 * math.pi))
            grad = dot(cg[slot, span, :], big[:, wide:]) * (below + pre * density)
            grad = grad.astype(BF)
            dh[slot, span, :] = grad
            ub_grad[0:1, :] += jnp.sum(grad.astype(F32), 0, keepdims=True)
        tokens = pl.ds(pl.multiple_of(slot * local, local), local)
        dot_rows[:, tokens] = dot_nt(smt[query_width:, :], cg[slot]).astype(BF)
        return carry

    lax.fori_loop(0, 4, perceptron, 0)

    def big_grad(at):
        columns = pl.ds(pl.multiple_of(at, 128), 128)
        up, down = (0.0, 0.0)
        for slot in range(4):
            up = up + dot_tn(a2[slot, :, columns], dh[slot])
            down = down + dot_tn(cg[slot, :, columns], h[slot])
        return (up, down)

    shares = dp_size == 2 and rows % 128 == 0
    sums = []
    if shares:
        pieces = rows // 128
        for at in range(pieces):
            up, down = big_grad((1 - dp) * rows + at * 128)
            span = pl.ds(at * 128, 128)
            g_send[span, :wide] = up.astype(BF)
            g_send[span, wide:] = down.astype(BF)
            sums.append(copies.remote(g_send.at[span], g_recv.at[span], place.dp_peers[0]))
        for at in range(pieces):
            up, down = big_grad(dp * rows + at * 128)
            span = pl.ds(at * 128, 128)
            big_own[span, :wide] = up
            big_own[span, wide:] = down
        homes = [
            copies.homeward(g_swap.at[pl.ds(at * 128, 128)], big_land.at[pl.ds(at * 128, 128)], place.swap)
            for at in range(pieces)
        ]

        def sum_arrives(at):
            span = pl.ds(at * 128, 128)
            sums[at].wait_recv()
            total = big_own[span, :] + g_recv[span, :].astype(F32)
            big_own[span, :] = total

            @pl.when(place.is_swapped)
            def _():
                g_swap[span, :] = total.astype(BF)
                homes[at].start()

        later = [functools.partial(sum_arrives, at) for at in range(pieces)]
    else:

        def big_grad_rows(at, carry):
            up, down = big_grad(at * 128)
            span = pl.ds(pl.multiple_of(at * 128, 128), 128)
            big_own[span, :wide] = up
            big_own[span, wide:] = down
            return carry

        lax.fori_loop(0, D // 128, big_grad_rows, 0)
        later, homes = ([], [])

    dk[...] = jnp.zeros_like(dk)
    dv[...] = jnp.zeros_like(dv)

    def backward_head(head, carry):
        own = pl.ds(pl.multiple_of(head * HS, HS), HS)
        for query in range(tiles):
            hooks(head, query, later, 6)
            at_q = pl.ds(tile_at(query), TILE)
            q, do = (qt[own, at_q], dot_rows[own, at_q])
            scaled = do * jnp.asarray(1.0 / math.sqrt(HS), BF)
            log_total = l_ref[head, 0:1, at_q]
            inner = jnp.zeros((1, TILE), F32)
            for key in range(query + 1):
                at_k = pl.ds(tile_at(key), TILE)
                at_s = pl.ds(key * TILE, TILE)
                softmax = jnp.exp(masked(dot(k[at_k, :], q), key, query) - log_total)
                prob_grad = dot(v[at_k, :], scaled)
                s_ref[at_s, :] = softmax
                d_ref[at_s, :] = prob_grad
                inner = inner + jnp.sum(softmax * prob_grad, 0, keepdims=True)
            query_grad = jnp.zeros((HS, TILE), F32)
            for key in range(query + 1):
                at_k = pl.ds(tile_at(key), TILE)
                at_s = pl.ds(key * TILE, TILE)
                softmax = s_ref[at_s, :]
                score_grad = (softmax * (d_ref[at_s, :] - inner)).astype(BF)
                query_grad = query_grad + dot(kt[:, at_k], score_grad)
                dk[at_k, :] += dot_nt(score_grad, q)
                dv[at_k, :] += dot_nt(softmax.astype(BF), do)
            table = pl.ds(query * TILE, TILE)
            dqt[own, at_q] = rotate(query_grad, cos_ref[:, table], -sin_ref[:, table]).astype(BF)
        return carry

    lax.fori_loop(0, heads, backward_head, 0)
    for event in later[heads * (tiles - 6) :]:
        event()
    for slot in range(4):
        block = at_slot(slot, rank)
        table = pl.ds(pl.multiple_of(block * local, local), local)
        tokens = pl.ds(slot * local, local)
        key_grad = dk[tokens, :].T * math.sqrt(HS)
        pair_grad[0:HS, tokens] = rotate(key_grad, cos_ref[:, table], -sin_ref[:, table])
        pair_grad[HS:, tokens] = dv[tokens, :].T

    @pl.when(place.is_swapped)
    def _():
        for copy in homes:
            copy.wait_send()
            copy.wait_recv()
        if shares:
            big_own[...] = big_land[...].astype(F32)

    copies.finish()


def first_pass(dp_size, x, c, entry, leave, shared, ids, vector, cosine, sine):
    local = x.shape[0]
    length = 4 * local
    rows, part = entry.shape
    query_width = HEADS * HS // 4
    width = 2 * query_width
    wide = 2 * (part - query_width)
    heads = query_width // HS
    gathers_pair = shared.shape[0] != D
    shares = dp_size == 2 and rows % 128 == 0
    held = (rows if shares else 128, wide)
    tokens = ((4, local, D), BF)
    hidden = ((4, local, wide // 2), BF)
    outs = [
        tokens,
        tokens,
        tokens,
        hidden,
        hidden,
        ((D, wide), BF),
        ((D, width), BF),
        ((dp_size, 4, shared.shape[0], 2 * HS) if gathers_pair else (D, 2 * HS), BF),
        ((query_width, length), BF),
        ((query_width, length), BF),
        ((2 * HS, length), F32),
        ((8, D), F32),
        ((8, wide // 2), F32),
        ((rows if shares else D, wide), F32),
    ]
    vmem = pl.BlockSpec(memory_space=pltpu.VMEM)
    copies = 48 + 12 * dp_size
    work = query_width * length * length
    return pl.pallas_call(
        functools.partial(first_kernel, dp_size),
        out_shape=[jax.ShapeDtypeStruct(shape, kind) for shape, kind in outs],
        in_specs=[vmem] * 9,
        out_specs=[vmem] * len(outs),
        scratch_shapes=[
            pltpu.VMEM((rows, width), BF),
            pltpu.VMEM((rows, wide), BF),
            pltpu.VMEM((shared.shape[0] if gathers_pair else 16, 2 * HS), BF),
            pltpu.VMEM(vector.shape, F32),
            pltpu.VMEM((query_width, 1), F32),
            pltpu.VMEM((2 * HS, 1), F32),
            pltpu.VMEM(held, BF),
            pltpu.VMEM((4, local, D), BF),
            pltpu.VMEM((width, D), BF),
            pltpu.VMEM((2 * HS, D), BF),
            pltpu.VMEM((query_width, length), BF),
            pltpu.VMEM((query_width, length), BF),
            pltpu.VMEM((HS, length), BF),
            pltpu.VMEM((HS, length), BF),
            pltpu.VMEM((length, HS), BF),
            pltpu.VMEM((length, HS), BF),
            pltpu.VMEM((length, HS), F32),
            pltpu.VMEM((length, HS), F32),
            pltpu.VMEM((length, TILE), F32),
            pltpu.VMEM((length, TILE), F32),
            pltpu.VMEM((heads, 8, length), F32),
            pltpu.VMEM((1, length), jnp.int32),
            pltpu.VMEM(held, BF),
            pltpu.VMEM(held, BF),
            pltpu.VMEM(held, BF),
            pltpu.SemaphoreType.DMA((copies,)),
            pltpu.SemaphoreType.DMA((copies,)),
        ],
        compiler_params=pltpu.CompilerParams(
            collective_id=0, has_side_effects=True, vmem_limit_bytes=59 << 20
        ),
        cost_estimate=pl.CostEstimate(
            flops=60 * work, bytes_accessed=30 << 20, transcendentals=work // HS
        ),
        name="gather_attend",
    )(x, c, entry, leave, shared, ids, vector, cosine, sine)


def second_kernel(
    dp_size, sums_pair, x_ref, c_ref, bias_ref, xg, cg, a1, h, dh, big, small, kvw, ot, dqt, pair_grad,
    norm_ref, ub_grad,
    out_ref, grad_ref, small_own, vector_home, shared_home, pair_parts,
    y_land, u_land, small_land, stats, v_next, v_core, v_dp, s_core, s_next, s_dp,
    y_core, y_from, y_next, y_got, y_keep, y_home, u_core, u_from, u_next, u_got, u_keep, u_home,
    p_from, p_next, p_got, full, g_send, g_recv, g_swap, send, receive,
):
    place = Place(dp_size)
    copies = Copies(send, receive)
    local = xg.shape[1]
    wide = dh.shape[2]
    rows = small_own.shape[0]
    query_width = ot.shape[0]
    place.meet()
    pair_core = copies.remote(pair_grad.at[:, pl.ds(2 * local, 2 * local)], p_from, place.core)
    stats[...] = jnp.zeros_like(stats)

    def normal_of(slot):
        inputs = xg[slot].astype(F32)
        centered = inputs - jnp.mean(inputs, -1, keepdims=True)
        return centered * lax.rsqrt(jnp.mean(centered * centered, -1, keepdims=True) + NORM_EPS)

    def column_sum(rows_of):
        return jnp.sum(rows_of, 0, keepdims=True)

    def row_of(column):
        size = column.shape[0]
        down = lax.broadcasted_iota(jnp.int32, (size, size), 0)
        along = lax.broadcasted_iota(jnp.int32, (size, size), 1)
        return column_sum(jnp.where(down == along, column, 0.0))

    stats[4:5, :D] = column_sum(cg[0].astype(F32))
    tail = pl.ds(8 + place.rank, 1)
    stats[tail, :query_width] = row_of(jnp.sum(dqt[...].astype(F32), 1, keepdims=True))
    stats[tail, query_width : query_width + dh.shape[2]] = ub_grad[0:1, :]

    def both(slot):
        tokens = pl.ds(slot * local, local)
        branch = dot_nt(h[slot], big[:, wide:])
        branch = branch + dot_nt(ot[:, tokens].T, small[:, query_width:])
        first = dot_nt(dqt[:, tokens].T, small[:, :query_width])
        second = dot_nt(dh[slot], big[:, :wide])
        normal = normal_of(slot)
        stats[0:1, :D] += column_sum(first * normal)
        stats[1:2, :D] += column_sum(first)
        stats[2:3, :D] += column_sum(second * normal)
        stats[3:4, :D] += column_sum(second)
        return (branch, first * norm_ref[0:1, :] + second * norm_ref[2:3, :])

    step = local // 2
    spans = [pl.ds(at * step, step) for at in range(2)]
    y_cores, u_cores = ({}, {})
    for slot in (3, 2):
        branch, joined = both(slot)
        at = slot - 2
        u_core[at] = joined.astype(BF)
        u_cores[at] = copies.remote(u_core.at[at], u_from.at[at], place.core)
        y_core[at] = branch.astype(BF)
        y_cores[at] = copies.remote(y_core.at[at], y_from.at[at], place.core)
    pair_core.wait_recv()
    p_next[...] = pair_grad[:, local : 2 * local] + p_from[:, local:]
    pair_next = copies.remote(p_next, p_got, place.next)
    branch, joined = both(1)
    u_cores[1].wait_recv()
    u_next[...] = (joined + u_from[1].astype(F32)).astype(BF)
    u_nexts = [copies.remote(u_next.at[s], u_got.at[s], place.next) for s in spans]
    y_cores[1].wait_recv()
    y_next[...] = (branch + y_from[1].astype(F32)).astype(BF)

    turned = 0.0
    turned_out = 0.0
    for slot in range(4):
        tokens = pl.ds(slot * local, local)
        turned = turned + dot(dqt[:, tokens], a1[slot])
        turned_out = turned_out + dot(ot[:, tokens], cg[slot])
    full[:, :query_width] = turned.T
    full[:, query_width:] = turned_out.T
    shares = dp_size == 2 and rows < D
    if shares:
        g_send[...] = full[pl.ds(pl.multiple_of((1 - place.dp) * rows, 128), rows), :].astype(BF)
        small_sum = copies.remote(g_send, g_recv, place.dp_peers[0])
        small_home = copies.homeward(g_swap, small_land, place.swap)
        small_own[...] = full[pl.ds(pl.multiple_of(place.dp * rows, 128), rows), :]
    else:
        small_own[...] = full[...]

    branch, joined = both(0)
    u_cores[0].wait_recv()
    y_cores[0].wait_recv()
    y_keep[...] = branch + y_from[0].astype(F32)
    pair_next.wait_recv()
    pair_sum = (pair_grad[:, :local] + p_from[:, :local] + p_got[...]).astype(BF)
    stats[5:6, : 2 * HS] = row_of(jnp.sum(pair_sum.astype(F32), 1, keepdims=True))
    through_pair = dot_nt(pair_sum.T, kvw[...])
    stats[0:1, :D] += column_sum(through_pair * normal_of(0))
    stats[1:2, :D] += column_sum(through_pair)
    u_keep[...] = joined + u_from[0].astype(F32) + through_pair * norm_ref[0:1, :]
    pair_parts[...] = dot(pair_sum, a1[0]).T.reshape(pair_parts.shape)
    vector_core = copies.remote(stats, v_core, place.core)
    if sums_pair:
        shared_core = copies.remote(pair_parts, s_core, place.core)

    def sent_home(source, target):
        return copies.swapped(source, target, place.is_swapped, place.swap)

    homes = []
    if shares:
        small_sum.wait_recv()
        total = small_own[...] + g_recv[...].astype(F32)
        small_own[...] = total

        @pl.when(place.is_swapped)
        def _():
            g_swap[...] = total.astype(BF)
            small_home.start()

    vector_core.wait_recv()
    copies.sent(vector_core)
    stats[...] = stats[...] + v_core[...]
    vector_next = copies.remote(stats, v_next, place.next)
    if sums_pair:
        shared_core.wait_recv()
        copies.sent(shared_core)
        pair_parts[...] = pair_parts[...] + s_core[...]
        shared_next = [
            copies.remote(pair_parts.at[at * 4 + flip_one(place.rank)], s_next.at[at], place.next)
            for at in range(dp_size)
        ]
    vector_next.wait_recv()
    copies.sent(vector_next)
    stats[...] = stats[...] + v_next[...]
    vector_dp = [
        copies.remote(stats, v_dp.at[at], peer) for at, peer in enumerate(place.dp_peers)
    ]
    if sums_pair:
        for at, copy in enumerate(shared_next):
            copy.wait_recv()
            s_next[at] = s_next[at] + pair_parts[at * 4 + place.rank]
        shared_dp = [
            copies.remote(s_next.at[(place.dp + at + 1) % dp_size], s_dp.at[at], peer)
            for at, peer in enumerate(place.dp_peers)
        ]
    for copy in vector_dp:
        copy.wait_recv()
        copies.sent(copy)
    total = stats[...]
    for at in range(dp_size - 1):
        total = total + v_dp[at]
    stats[...] = total
    small_homes = [sent_home(stats, vector_home)]
    if sums_pair:
        for copy in shared_dp:
            copy.wait_recv()
        total = s_next[place.dp]
        for at in range(dp_size - 1):
            total = total + s_dp[at]
        s_core[0] = total
        small_homes.append(sent_home(s_core.at[0], shared_home))
    for start, _ in small_homes:
        start()
    y_nexts = []
    for span, copy in zip(spans, u_nexts):
        copy.wait_recv()
        y_nexts.append(copies.remote(y_next.at[span], y_got.at[span], place.next))
        u_home[span, :] = (u_keep[span, :] + u_got[span, :].astype(F32)).astype(BF)
        homes.append(sent_home(u_home.at[span], u_land.at[span]))
        homes[-1][0]()
    for span, copy in zip(spans, y_nexts):
        copy.wait_recv()
        y_home[span, :] = (y_keep[span, :] + y_got[span, :].astype(F32)).astype(BF)
        homes.append(sent_home(y_home.at[span], y_land.at[span]))
        homes[-1][0]()
    for span, (_, wait) in zip(spans, homes):
        wait()
        inputs = x_ref[span, :].astype(F32)
        centered = inputs - jnp.mean(inputs, -1, keepdims=True)
        scale = lax.rsqrt(jnp.mean(centered * centered, -1, keepdims=True) + NORM_EPS)
        normal = centered * scale
        joined = u_land[span, :].astype(F32)
        grad_ref[span, :] = c_ref[span, :].astype(F32) + scale * (
            joined
            - jnp.mean(joined, -1, keepdims=True)
            - normal * jnp.mean(joined * normal, -1, keepdims=True)
        )
    bias = bias_ref[:, 4 * D : 5 * D] + bias_ref[:, 5 * D : 6 * D]
    for span, (_, wait) in zip(spans, homes[2:]):
        wait()
        out_ref[span, :] = x_ref[span, :].astype(F32) + y_land[span, :].astype(F32) + bias
    for _, wait in small_homes:
        wait()
    if shares:

        @pl.when(place.is_swapped)
        def _():
            small_home.wait_send()
            small_home.wait_recv()
            small_own[...] = small_land[...].astype(F32)

    copies.finish()


def second_pass(
    dp_size, x, c, vector, xg, cg, a1, h, dh, big, small, kvw, ot, dqt, pair_grad, norms, ub_grad, piece
):
    local = xg.shape[1]
    length = 4 * local
    width = small.shape[1]
    rows = D // dp_size
    shares = dp_size == 2 and rows % 128 == 0
    sums_pair = piece % 16 == 0
    held = (rows if shares else 8, width)
    parts = (4 * dp_size, piece, 2 * HS) if sums_pair else (1, D, 2 * HS)
    own = (piece if sums_pair else 8, 2 * HS)
    outs = [
        (local, D),
        (local, D),
        (rows if shares else D, width),
        (16, 1024),
        own,
        parts,
    ]
    vmem = pl.BlockSpec(memory_space=pltpu.VMEM)
    branch = [
        pltpu.VMEM((2, local, D), BF),
        pltpu.VMEM((2, local, D), BF),
        pltpu.VMEM((local, D), BF),
        pltpu.VMEM((local, D), BF),
        pltpu.VMEM((local, D), F32),
        pltpu.VMEM((local, D), BF),
    ]
    work = length * D * D
    return pl.pallas_call(
        functools.partial(second_kernel, dp_size, sums_pair),
        out_shape=[jax.ShapeDtypeStruct(shape, F32) for shape in outs],
        in_specs=[vmem] * 16,
        out_specs=[vmem] * len(outs),
        scratch_shapes=[
            pltpu.VMEM((local, D), BF),
            pltpu.VMEM((local, D), BF),
            pltpu.VMEM(held, BF),
            pltpu.VMEM((16, 1024), F32),
            pltpu.VMEM((16, 1024), F32),
            pltpu.VMEM((16, 1024), F32),
            pltpu.VMEM((dp_size - 1, 16, 1024), F32),
            pltpu.VMEM(parts, F32),
            pltpu.VMEM((dp_size,) + own, F32),
            pltpu.VMEM((dp_size - 1,) + own, F32),
        ]
        + branch
        + branch
        + [
            pltpu.VMEM((2 * HS, 2 * local), F32),
            pltpu.VMEM((2 * HS, local), F32),
            pltpu.VMEM((2 * HS, local), F32),
            pltpu.VMEM((D, width), F32),
            pltpu.VMEM(held, BF),
            pltpu.VMEM(held, BF),
            pltpu.VMEM(held, BF),
            pltpu.SemaphoreType.DMA((32 + 3 * dp_size,)),
            pltpu.SemaphoreType.DMA((32 + 3 * dp_size,)),
        ],
        compiler_params=pltpu.CompilerParams(
            collective_id=1, has_side_effects=True, vmem_limit_bytes=59 << 20
        ),
        cost_estimate=pl.CostEstimate(flops=8 * work, bytes_accessed=30 << 20, transcendentals=0),
        name="sum_branches",
    )(x, c, vector, xg, cg, a1, h, dh, big, small, kvw, ot, dqt, pair_grad, norms, ub_grad)


def outer_step(total, groups, anchor, velocity):
    change = total / groups
    momentum = OUTER_BETA * velocity + change
    return (change, momentum, anchor - OUTER_RATE * (change + OUTER_BETA * momentum))


def third_kernel(
    groups, big_grad, small_grad, vector_grad, shared_grad,
    ew, em, ev, ea, eu, xw, xm, xv, xa, xu, sw, sm, sv, sa, su, vw, vm, vv, va, vu,
    em2, ev2, ew2, ec, ep, eg, xm2, xv2, xw2, xc, xp, xg, sm2, sv2, sw2, sc, sp, sg, vm2, vv2, vw2, vc, vp, vg,
    entry_grad, exit_grad, e_send, e_from, e_low, e_got, e_sum, e_back,
    x_send, x_from, x_low, x_got, x_sum, x_back, s_gap, s_core, s_part, s_half, v_gap, v_core, v_part, v_half,
    send, receive,
):
    group = lax.axis_index("group")
    core = group % 2
    mate, across = ({"group": flip_one(group)}, {"group": flip_two(group)})
    copies = Copies(send, receive)
    barrier = pltpu.get_barrier_semaphore()
    for peer in (mate, across):
        pl.semaphore_signal(barrier, inc=1, device_id=peer, device_id_type=pl.DeviceIdType.MESH)
    pl.semaphore_wait(barrier, 2)
    query_width = small_grad.shape[1] // 2
    wide = big_grad.shape[1] // 2

    def halves(ref):
        size = ref.shape[0] // 2
        return [pl.ds(pl.multiple_of(at * size, 8), size) for at in (core, 1 - core)]

    def update(span, grad, olds, news, rate, decay):
        weight, first, second, anchor = (ref[span, :] for ref in olds)
        first, second, new = adamw_update(weight, first, second, grad, rate, decay)
        news[0][span, :] = first
        news[1][span, :] = second
        news[2][span, :] = new
        return anchor - new

    entry_grad[:, :query_width] = small_grad[:, :query_width]
    entry_grad[:, query_width:] = big_grad[:, :wide]
    entry = ((ew, em, ev, ea), (em2, ev2, ew2))
    leave = ((xw, xm, xv, xa), (xm2, xv2, xw2))
    e_own, e_other = halves(ew)
    x_own, x_other = halves(xw)
    e_send[...] = update(e_other, entry_grad[e_other, :], *entry, MATRIX_RATE, MATRIX_DECAY)
    e_core = copies.remote(e_send, e_from, mate)
    e_sum[...] = update(e_own, entry_grad[e_own, :], *entry, MATRIX_RATE, MATRIX_DECAY)
    e_core.wait_recv()
    e_low[...] = (e_sum[...] + e_from[...]).astype(BF)
    e_across = copies.remote(e_low, e_got, across)
    exit_grad[:query_width, :] = small_grad[:, query_width:].T
    exit_grad[query_width:, :] = big_grad[:, wide:].T
    x_send[...] = update(x_other, exit_grad[x_other, :], *leave, MATRIX_RATE, MATRIX_DECAY)
    x_core = copies.remote(x_send, x_from, mate)
    x_sum[...] = update(x_own, exit_grad[x_own, :], *leave, MATRIX_RATE, MATRIX_DECAY)
    x_core.wait_recv()
    x_low[...] = (x_sum[...] + x_from[...]).astype(BF)
    x_across = copies.remote(x_low, x_got, across)
    every = slice(None)
    s_gap[...] = update(
        every, shared_grad[...], (sw, sm, sv, sa), (sm2, sv2, sw2), MATRIX_RATE, MATRIX_DECAY
    )
    shared_core = copies.remote(s_gap, s_core, mate)
    part = query_width + wide
    rows = [vector_grad[at : at + 1, :D] for at in (0, 1, 2, 3, 4, 4)]
    rows.append(vector_grad[5:6, : 2 * HS])
    rows += [vector_grad[8 + at : 9 + at, :part] for at in range(4)]
    v_gap[...] = update(
        every, jnp.concatenate(rows, 1), (vw, vm, vv, va), (vm2, vv2, vw2), VECTOR_RATE, 0.0
    )
    vector_core = copies.remote(v_gap, v_core, mate)
    shared_core.wait_recv()
    s_part[...] = s_gap[...] + s_core[...]
    shared_across = copies.remote(s_part, s_half, across)
    vector_core.wait_recv()
    v_part[...] = v_gap[...] + v_core[...]
    vector_across = copies.remote(v_part, v_half, across)

    def finish(span, total, anchor, velocity, outs):
        for ref, value in zip(outs, outer_step(total, groups, anchor[span, :], velocity[span, :])):
            ref[span, :] = value

    backs = []
    for across_copy, low, got, total, back, own, anchor, velocity, outs in (
        (e_across, e_low, e_got, e_sum, e_back, e_own, ea, eu, (ec, ep, eg)),
        (x_across, x_low, x_got, x_sum, x_back, x_own, xa, xu, (xc, xp, xg)),
    ):
        across_copy.wait_recv()
        total[...] = low[...].astype(F32) + got[...].astype(F32)
        backs.append(copies.remote(total, back, mate))
        finish(own, total[...], anchor, velocity, outs)
    shared_across.wait_recv()
    finish(every, s_part[...] + s_half[...], sa, su, (sc, sp, sg))
    vector_across.wait_recv()
    finish(every, v_part[...] + v_half[...], va, vu, (vc, vp, vg))
    backs[0].wait_recv()
    finish(e_other, e_back[...], ea, eu, (ec, ep, eg))
    backs[1].wait_recv()
    finish(x_other, x_back[...], xa, xu, (xc, xp, xg))
    copies.finish()


def third_pass(groups, grads, entry, leave, shared, vector):
    vmem = pl.BlockSpec(memory_space=pltpu.VMEM)
    outs = [array[0] for array in (entry, leave, shared, vector) for _ in range(6)]

    def half(array, kind):
        return pltpu.VMEM((array.shape[0] // 2, array.shape[1]), kind)

    def whole(array):
        return [pltpu.VMEM(array.shape, F32)] * 4

    def sums(array):
        return [half(array, kind) for kind in (F32, F32, BF, BF, F32, F32)]

    arrays = list(grads) + [array for arrays in (entry, leave, shared, vector) for array in arrays]
    return pl.pallas_call(
        functools.partial(third_kernel, groups),
        out_shape=[jax.ShapeDtypeStruct(array.shape, F32) for array in outs],
        in_specs=[vmem] * len(arrays),
        out_specs=[vmem] * len(outs),
        scratch_shapes=[pltpu.VMEM(entry[0].shape, F32), pltpu.VMEM(leave[0].shape, F32)]
        + sums(entry[0])
        + sums(leave[0])
        + whole(shared[0])
        + whole(vector[0])
        + [pltpu.SemaphoreType.DMA((16,)), pltpu.SemaphoreType.DMA((16,))],
        compiler_params=pltpu.CompilerParams(
            collective_id=2, has_side_effects=True, vmem_limit_bytes=59 << 20
        ),
        cost_estimate=pl.CostEstimate(flops=1 << 26, bytes_accessed=40 << 20, transcendentals=1 << 20),
        name="update_weights",
    )(*arrays)

def shards(
    hidden_in,
    doc_ids,
    out_cotangent,
    entry_weight,
    entry_first,
    entry_second,
    entry_anchor,
    entry_velocity,
    exit_weight,
    exit_first,
    exit_second,
    exit_anchor,
    exit_velocity,
    shared_weight,
    shared_first,
    shared_second,
    shared_anchor,
    shared_velocity,
    vector_weight,
    vector_first,
    vector_second,
    vector_anchor,
    vector_velocity,
):
    batch, local_len = hidden_in.shape[:2]
    parts = lax.axis_size("mp")
    group, rank = (lax.axis_index("group"), lax.axis_index("mp"))
    is_swapped = (group % 2) != (rank // 2)
    rank = jnp.where(is_swapped, jnp.bitwise_xor(rank, 2), rank)
    length = local_len * parts
    part_width = entry_weight.shape[2]
    query_width = HEADS * HS // parts
    heads = query_width // HS

    dp_size = lax.axis_size("dp")
    order = jnp.bitwise_xor(jnp.arange(parts), rank)
    piece = shared_weight.shape[1]
    shared_piece = shared_weight[0]
    if piece % 16:
        pieces = gather_square(swapped_parts(shared_piece.astype(BF)))
        pieces = jnp.take(pieces, order, axis=0)
        shared_piece = gather_dp(pieces.reshape(-1, 2 * HS), 0)
    half = ROT // 2
    frequency = 10000.0 ** (-(np.arange(half) * 2.0 / ROT))
    angles = frequency.astype(np.float32)[:, None] * np.arange(length, dtype=np.float32)[None, :]
    cosine_table = jnp.asarray(np.cos(angles.astype(np.float64)).astype(np.float32))
    sine_table = jnp.asarray(np.sin(angles.astype(np.float64)).astype(np.float32))
    (
        inputs, cots, attn_input, hidden, hidden_grad, big, small, pair_weight, attended, query_grad,
        pair_rows, norms, up_bias_rows, big_grad,
    ) = first_pass(
        dp_size,
        hidden_in[0],
        out_cotangent[0],
        entry_weight[0],
        exit_weight[0],
        shared_piece,
        doc_ids,
        vector_weight,
        cosine_table,
        sine_table,
    )
    block_output, input_grad, small_grad, vector_grad, shared_grad, pair_parts = second_pass(
        dp_size, hidden_in[0], out_cotangent[0], vector_weight, inputs, cots, attn_input, hidden,
        hidden_grad, big, small, pair_weight.reshape(D, 2 * HS), attended, query_grad, pair_rows, norms,
        up_bias_rows, piece,
    )
    if big_grad.shape[0] == D:
        big_grad, small_grad = (scatter_dp(array, 0, F32) for array in (big_grad, small_grad))
        big_grad, small_grad = (swapped_parts(array) for array in (big_grad, small_grad))
    if piece % 16:
        grad_pieces = pair_parts.reshape(dp_size, parts, -1, 2 * HS)
        grad_pieces = jnp.take(grad_pieces, order, axis=1).swapaxes(0, 1)
        shared_grad = scatter_dp(scatter_square(grad_pieces, F32), 0, F32)
        shared_grad = swapped_parts(shared_grad.reshape(-1, 2 * HS))
    updated = third_pass(
        lax.axis_size("group"),
        (big_grad, small_grad, vector_grad, shared_grad),
        (entry_weight[0], entry_first[0], entry_second[0], entry_anchor, entry_velocity),
        (exit_weight[0], exit_first[0], exit_second[0], exit_anchor, exit_velocity),
        (shared_weight[0], shared_first[0], shared_second[0], shared_anchor, shared_velocity),
        (vector_weight, vector_first, vector_second, vector_anchor[None], vector_velocity[None]),
    )
    updated = list(updated)
    results = [block_output[None], input_grad[None]]
    for at in range(3):
        results += [array[None] for array in updated[6 * at : 6 * at + 3]]
        results += updated[6 * at + 3 : 6 * at + 6]
    results += updated[18:21] + [array[0] for array in updated[21:24]]
    return tuple(results)


def solution(mesh):
    in_specs = (
        P(("group", "dp"), "mp", None),
        P(("group", "dp"), "mp"),
        P(("group", "dp"), "mp", None),
        P("group", "dp", "mp"),
        P("group", "dp", "mp"),
        P("group", "dp", "mp"),
        P("dp", "mp"),
        P("dp", "mp"),
        P("group", "mp", "dp"),
        P("group", "mp", "dp"),
        P("group", "mp", "dp"),
        P("mp", "dp"),
        P("mp", "dp"),
        P("group", ("dp", "mp"), None),
        P("group", ("dp", "mp"), None),
        P("group", ("dp", "mp"), None),
        P(("dp", "mp"), None),
        P(("dp", "mp"), None),
        P("group", None),
        P("group", None),
        P("group", None),
        P(),
        P(),
    )
    out_specs = (
        P(("group", "dp"), "mp", None),
        P(("group", "dp"), "mp", None),
        P("group", "dp", "mp"),
        P("group", "dp", "mp"),
        P("group", "dp", "mp"),
        P("dp", "mp"),
        P("dp", "mp"),
        P("dp", "mp"),
        P("group", "mp", "dp"),
        P("group", "mp", "dp"),
        P("group", "mp", "dp"),
        P("mp", "dp"),
        P("mp", "dp"),
        P("mp", "dp"),
        P("group", ("dp", "mp"), None),
        P("group", ("dp", "mp"), None),
        P("group", ("dp", "mp"), None),
        P(("dp", "mp"), None),
        P(("dp", "mp"), None),
        P(("dp", "mp"), None),
        P("group", None),
        P("group", None),
        P("group", None),
        P(),
        P(),
        P(),
    )
    return jax.shard_map(shards, mesh=mesh, in_specs=in_specs, out_specs=out_specs, check_vma=False)
```

```python
import functools
import math

import jax
import jax.numpy as jnp
import numpy as np
from jax import lax
from jax.experimental import pallas as pl
from jax.experimental.pallas import tpu as pltpu
from jax.sharding import PartitionSpec as P

D = 768
HEADS = 12
HS = 64
ROT = 16
STEP = 5
IN_COLS = 3840


NORM_EPS = 1e-05
BETA_ONE = 0.9
BETA_TWO = 0.95
ADAM_EPS = 1e-08
MATRIX_RATE = 0.03
MATRIX_DECAY = 0.1
VECTOR_RATE = 0.3
OUTER_RATE = 0.7
OUTER_BETA = 0.9

TILE = 256
F32 = jnp.float32
BF = jnp.bfloat16


def dot(left, right):
    return jnp.dot(left, right, preferred_element_type=F32)


def dot_nt(left, right):
    return lax.dot_general(left, right, (((1,), (1,)), ((), ())), preferred_element_type=F32)


def dot_tn(left, right):
    return lax.dot_general(left, right, (((0,), (0,)), ((), ())), preferred_element_type=F32)


def adamw_update(weight, first, second, gradient, step_rate, decay):
    first_new = BETA_ONE * first + (1.0 - BETA_ONE) * gradient
    second_new = BETA_TWO * second + (1.0 - BETA_TWO) * gradient * gradient
    fix_first = 1.0 - BETA_ONE**STEP
    fix_second = 1.0 - BETA_TWO**STEP
    update = first_new / fix_first / (jnp.sqrt(second_new / fix_second) + ADAM_EPS)
    return (first_new, second_new, weight - step_rate * (update + decay * weight))


def pairs_of(size, bit):
    return [(at, at ^ bit) for at in range(size)]


def over_core(array):
    return lax.ppermute(array, "group", pairs_of(lax.axis_size("group"), 1))


def over_next(array):
    return lax.ppermute(array, "mp", pairs_of(lax.axis_size("mp"), 1))


def over_dp(array):
    return lax.ppermute(array, "dp", pairs_of(2, 1))


def swapped_parts(array):
    parts = lax.axis_size("mp")
    pairs = []
    for group in range(lax.axis_size("group")):
        for rank in range(parts):
            here = group * parts + rank
            there = (group ^ 1) * parts + (rank ^ 2)
            pairs.append((here, there if group % 2 != rank // 2 else here))
    return lax.ppermute(array, ("group", "mp"), pairs)


def gather_square(own):
    pair = jnp.stack([own, over_next(own)])
    return jnp.concatenate([pair, over_core(pair)], 0)


def scatter_square(slots, send_type):
    pair = slots[:2] + over_core(slots[2:].astype(send_type)).astype(F32)
    return pair[0] + over_next(pair[1].astype(send_type)).astype(F32)


def gather_dp(own, axis):
    if lax.axis_size("dp") == 2:
        other = over_dp(own)
        first = lax.axis_index("dp") == 0
        return jnp.concatenate(
            [jnp.where(first, own, other), jnp.where(first, other, own)], axis
        )
    return lax.all_gather(own, "dp", axis=axis, tiled=True)


def scatter_dp(array, axis, send_type):
    if lax.axis_size("dp") == 2:
        size = array.shape[axis] // 2
        mine = lax.axis_index("dp")
        kept = lax.dynamic_slice_in_dim(array, mine * size, size, axis)
        sent = lax.dynamic_slice_in_dim(array, (1 - mine) * size, size, axis)
        return kept + over_dp(sent.astype(send_type)).astype(F32)
    return lax.psum_scatter(array, "dp", scatter_dimension=axis, tiled=True)


def flip_one(index):
    return index + 1 - 2 * (index % 2)


def flip_two(index):
    return index + 2 - 4 * ((index // 2) % 2)


def at_slot(slot, rank):
    rank = flip_one(rank) if slot % 2 else rank
    return flip_two(rank) if slot // 2 else rank


class Copies:
    def __init__(self, send, receive):
        self.send, self.receive, self.used, self.sends = (send, receive, 0, [])

    def remote(self, source, target, device, starts=True):
        at = self.used
        self.used += 1
        copy = pltpu.make_async_remote_copy(
            src_ref=source,
            dst_ref=target,
            send_sem=self.send.at[at],
            recv_sem=self.receive.at[at],
            device_id=device,
            device_id_type=pl.DeviceIdType.MESH,
        )
        if starts:
            copy.start()
        self.sends.append(copy)
        return copy

    def swapped(self, source, target, is_swapped, device):
        at = self.used
        self.used += 1
        far = pltpu.make_async_remote_copy(
            src_ref=source,
            dst_ref=target,
            send_sem=self.send.at[at],
            recv_sem=self.receive.at[at],
            device_id=device,
            device_id_type=pl.DeviceIdType.MESH,
        )
        near = pltpu.make_async_copy(source, target, self.receive.at[at])

        def start():
            @pl.when(is_swapped)
            def _():
                far.start()

            @pl.when(jnp.logical_not(is_swapped))
            def _():
                near.start()

        def wait():
            @pl.when(is_swapped)
            def _():
                far.wait_send()
                far.wait_recv()

            @pl.when(jnp.logical_not(is_swapped))
            def _():
                near.wait()

        return (start, wait)

    def homeward(self, source, target, device):
        at = self.used
        self.used += 1
        return pltpu.make_async_remote_copy(
            src_ref=source,
            dst_ref=target,
            send_sem=self.send.at[at],
            recv_sem=self.receive.at[at],
            device_id=device,
            device_id_type=pl.DeviceIdType.MESH,
        )

    def local(self, source, target):
        at = self.used
        self.used += 1
        copy = pltpu.make_async_copy(source, target, self.receive.at[at])
        copy.start()
        return copy

    def sent(self, copy):
        copy.wait_send()
        self.sends = [other for other in self.sends if other is not copy]

    def finish(self):
        for copy in self.sends:
            copy.wait_send()


class Place:
    def __init__(self, dp_size):
        group, self.dp, home = (lax.axis_index("group"), lax.axis_index("dp"), lax.axis_index("mp"))
        core, upper = (group % 2, home // 2)
        self.is_swapped = core != upper
        self.home = home
        self.rank = jnp.where(self.is_swapped, flip_two(home), home)
        self.swap = {"group": flip_one(group), "mp": flip_two(home)}
        self.core = {"group": flip_one(group)}
        self.across = {"group": flip_two(group)}
        self.half = core
        self.next = {"mp": flip_one(home)}
        self.dp_peers = [{"dp": (self.dp + step) % dp_size} for step in range(1, dp_size)]

    def meet(self, others=()):
        barrier = pltpu.get_barrier_semaphore()
        peers = [self.core, self.next, self.swap] + self.dp_peers + list(others)
        for peer in peers:
            pl.semaphore_signal(
                barrier, inc=1, device_id=peer, device_id_type=pl.DeviceIdType.MESH
            )
        pl.semaphore_wait(barrier, len(peers))


def column_of(row):
    size = row.shape[1]
    down = lax.broadcasted_iota(jnp.int32, (size, size), 0)
    along = lax.broadcasted_iota(jnp.int32, (size, size), 1)
    return jnp.sum(jnp.where(down == along, row, 0.0), 1, keepdims=True)


def rotate(rows, cosine, sine):
    half = ROT // 2
    one, two = (rows[:half], rows[half:ROT])
    return jnp.concatenate(
        [one * cosine - two * sine, two * cosine + one * sine, rows[ROT:]], 0
    )


def first_kernel(
    dp_size, x_ref, c_ref, entry_ref, exit_ref, shared_ref, ids_ref, vector_ref, cos_ref, sin_ref,
    xg_out, cg_out, a1_out, dh_out, up_out, small_out, kvw_out, ot_out,
    dqt, pair_grad, norm_ref, ub_grad, big_own, y_land,
    xg, cg, a1, dh, up_w, small, kvw, ot, h, down_w, small_ref, up_ref, down_ref, pair_ref, vector_other, qb_ref, kvb_ref, big_land, a2,
    kvt, qt, dot_rows, kt, vt, k, v, dk, dv, s_ref, d_ref, l_ref, idr, tmp,
    y_from, y_got, y_keep, g_send, g_recv, send, receive,
):
    place = Place(dp_size)
    rank, dp = (place.rank, place.dp)
    copies = Copies(send, receive)
    local = x_ref.shape[0]
    length = 4 * local
    columns = entry_ref.shape[1]
    shares = columns != D
    query_width = small.shape[0] // 2
    wide = up_w.shape[0]
    heads = query_width // HS
    gathers_pair = shared_ref.shape[0] != D
    kept = (xg, cg, a1, dh, up_w, small, kvw, ot)
    kept_outs = (xg_out, cg_out, a1_out, dh_out, up_out, small_out, kvw_out, ot_out)
    place.meet()
    vector_core = copies.remote(vector_ref, vector_other, place.core)

    def swapped(source, target):
        return copies.swapped(source, target, place.is_swapped, place.swap)

    def dp_part(ref, start, size):
        return ref.at[pl.ds(start, size), pl.ds(pl.multiple_of(dp * columns, 128), columns)]

    step = local // 2
    spans = [pl.ds(at * step, step) for at in range(2)]
    x_swaps = [swapped(x_ref.at[s], xg.at[0, s]) for s in spans]
    c_swaps = [swapped(c_ref.at[s], cg.at[0, s]) for s in spans]
    ids_swap = swapped(ids_ref, idr.at[:, pl.ds(0, local)])
    small_swaps, big_swaps, big_parts = ([], [], [])
    if shares:
        small_part = dp_part(small, 0, 2 * query_width)
        small_swaps = [swapped(small_ref, small_part)]
        for at in range(0, wide, TILE):
            for source, target in ((up_ref, up_w), (down_ref, down_w)):
                big_parts.append(dp_part(target, at, TILE))
                big_swaps.append(swapped(source.at[pl.ds(at, TILE)], big_parts[-1]))
    first = [ids_swap]
    if gathers_pair:
        pair_swap = swapped(pair_ref, kvw.at[dp, place.home])
        first.append(pair_swap)
    queue = iter([start for start, _ in x_swaps + small_swaps + c_swaps])

    def start_next():
        start = next(queue, None)
        if start is not None:
            start()

    start_next()
    start_next()
    if gathers_pair:
        pair_ref[...] = shared_ref[...].astype(BF)
    for start, _ in first:
        start()
    if shares:
        small_ref[:query_width, :] = entry_ref[:query_width, :].astype(BF)
        small_ref[query_width:, :] = exit_ref[:query_width, :].astype(BF)
        up_ref[...] = entry_ref[query_width:, :].astype(BF)
        down_ref[...] = exit_ref[query_width:, :].astype(BF)
    else:
        small[:query_width, :] = entry_ref[:query_width, :]
        small[query_width:, :] = exit_ref[:query_width, :]
        up_w[...] = entry_ref[query_width:, :]
        down_w[...] = exit_ref[query_width:, :]
    vector_core.wait_recv()

    def role_vector(start, size):
        span = slice(start, start + size)
        return jnp.where(place.is_swapped, vector_other[:, span], vector_ref[:, span])

    for at in range(4):
        norm_ref[at : at + 1, :] = role_vector(at * D, D)
    kvb_ref[...] = column_of(role_vector(6 * D, 2 * HS))
    part = query_width + wide
    tail = 6 * D + 2 * HS
    in_bias = role_vector(tail, part)
    for at in range(1, 4):
        in_bias = jnp.where(rank == at, role_vector(tail + at * part, part), in_bias)
    qb_ref[...] = column_of(in_bias[:, :query_width])
    norm_ref[4:5, :] = in_bias[:, query_width:]

    def normalise(slot):
        def body(at, carry):
            span = pl.ds(pl.multiple_of(at * 128, 128), 128)
            wide = xg[slot, span, :].astype(F32)
            centered = wide - jnp.mean(wide, -1, keepdims=True)
            normal = centered * lax.rsqrt(
                jnp.mean(centered * centered, -1, keepdims=True) + NORM_EPS
            )
            a1[slot, span, :] = (normal * norm_ref[0:1, :] + norm_ref[1:2, :]).astype(BF)
            a2[slot, span, :] = (normal * norm_ref[2:3, :] + norm_ref[3:4, :]).astype(BF)
            return carry

        lax.fori_loop(0, local // 128, body, 0)

    def lanes(ref, slot):
        return ref.at[:, pl.ds(slot * local, local)]

    x_next, x_core, x_far = ([], [], [])
    for span, (_, wait) in zip(spans, x_swaps):
        wait()
        start_next()
        x_next.append(copies.remote(xg.at[0, span], xg.at[1, span], place.next))
        x_core.append(copies.remote(xg.at[0, span], xg.at[2, span], place.core))
    small_dp = []
    for _, wait in small_swaps:
        wait()
        start_next()
        small_dp += [copies.remote(small_part, small_part, peer) for peer in place.dp_peers]
    ids_swap[1]()
    ids_next = copies.remote(lanes(idr, 0), lanes(idr, 1), place.next)
    ids_core = copies.remote(lanes(idr, 0), lanes(idr, 2), place.core)
    if gathers_pair:
        pair_swap[1]()
        own_pair = kvw.at[dp, rank]
        pair_next = copies.remote(own_pair, own_pair, place.next)
        pair_core = copies.remote(own_pair, own_pair, place.core)
    c_next, c_core, c_far, big_dp = ([], [], [], [])
    for span in spans:
        c_next.append(copies.remote(cg.at[0, span], cg.at[1, span], place.next, starts=False))
        c_core.append(copies.remote(cg.at[0, span], cg.at[2, span], place.core, starts=False))
        c_far.append(copies.remote(cg.at[1, span], cg.at[3, span], place.core, starts=False))
    for part in big_parts:
        big_dp.append([copies.remote(part, part, peer, starts=False) for peer in place.dp_peers])

    def c_sends(at):
        c_next[at].start()
        c_core[at].start()

    def c_arrives(at):
        @pl.when(place.is_swapped)
        def _():
            c_swaps[at][1]()
            c_sends(at)

        if at < len(big_swaps):
            big_swaps[at][0]()

    def c_passes(at):
        c_next[at].wait_recv()
        c_far[at].start()

    def big_arrives(at):
        big_swaps[at][1]()
        if at + 2 < len(big_swaps):
            big_swaps[at + 2][0]()
        for copy in big_dp[at]:
            copy.start()

    normalise(0)
    for span, copy in zip(spans, x_next):
        copy.wait_recv()
        x_far.append(copies.remote(xg.at[1, span], xg.at[3, span], place.core))
    for at in range(2):

        @pl.when(jnp.logical_not(place.is_swapped))
        def _():
            c_swaps[at][1]()
            c_sends(at)

    ids_next.wait_recv()
    ids_far = copies.remote(lanes(idr, 1), lanes(idr, 3), place.core)
    if gathers_pair:
        pair_next.wait_recv()
        next_pair = kvw.at[dp, flip_one(rank)]
        pair_far = copies.remote(next_pair, next_pair, place.core)
        pair_core.wait_recv()
        pair_far.wait_recv()
        pair_dp = [copies.remote(kvw.at[dp], kvw.at[dp], peer) for peer in place.dp_peers]
    events = [((0, 6), c_passes, 0), ((1, 5), c_passes, 1)]
    if shares:
        places = ((0, 5), (0, 7), (1, 6), (2, 3))
        events += [(place, big_arrives, at) for at, place in enumerate(places)]
    for copy in x_core:
        copy.wait_recv()
    normalise(2)
    normalise(1)
    for copy in x_far:
        copy.wait_recv()
    normalise(3)
    for copy in small_dp:
        copy.wait_recv()
    if gathers_pair:
        for copy in pair_dp:
            copy.wait_recv()
        kvt[...] = kvw[...].reshape(D, 2 * HS).T
    else:
        kvw[...] = shared_ref[...]
        kvt[...] = shared_ref[...].T
    c_arrives(0)
    for slot in range(4):
        block = at_slot(slot, rank)
        table = pl.ds(pl.multiple_of(block * local, local), local)
        cosine, sine = (cos_ref[:, table], sin_ref[:, table])
        tokens = pl.ds(slot * local, local)
        queries = dot_nt(small[0:query_width, :], a1[slot]) + qb_ref[...]
        for head in range(heads):
            turned = rotate(queries[head * HS : (head + 1) * HS], cosine, sine).astype(BF)
            qt[head * HS : (head + 1) * HS, tokens] = turned * jnp.asarray(1.0 / math.sqrt(HS), BF)
        pairs = dot_nt(kvt[...], a1[slot]) + kvb_ref[...]
        turned = rotate(pairs[:HS], cosine, sine).astype(BF)
        kt[:, tokens] = turned
        k[tokens, :] = turned.T
        value = pairs[HS:].astype(BF)
        vt[:, tokens] = value
        v[tokens, :] = value.T
    c_arrives(1)
    for copy in (ids_core, ids_far):
        copy.wait_recv()
    ids = idr[...].astype(F32)
    first_end = jnp.sum(jnp.where(ids < 0.5, 1.0, 0.0), 1, keepdims=True)
    second_end = jnp.sum(jnp.where(ids < 1.5, 1.0, 0.0), 1, keepdims=True)

    def document(position):
        position = position.astype(F32)
        return jnp.where(position < first_end, 0.0, jnp.where(position < second_end, 1.0, 2.0))

    tiles = length // TILE
    per = tiles // 4

    def tile_at(tile):
        return pl.multiple_of(at_slot(tile // per, rank) * local + (tile % per) * TILE, TILE)

    def masked(scores, key, query):
        edge = key == 0 or query == tiles - 1
        allowed = None
        if key == query:
            down = lax.broadcasted_iota(jnp.int32, (TILE, TILE), 0)
            allowed = down <= lax.broadcasted_iota(jnp.int32, (TILE, TILE), 1)
        if edge:
            down = document(lax.broadcasted_iota(jnp.int32, (TILE, 1), 0) + key * TILE)
            along = document(lax.broadcasted_iota(jnp.int32, (1, TILE), 1) + query * TILE)
            same = down == along
            allowed = same if allowed is None else allowed & same
        return scores if allowed is None else jnp.where(allowed, scores, -1e9)

    def hooks(head, query, todo):
        for (at_head, at_query), event, at in todo:
            if query == at_query:

                @pl.when(head == at_head)
                def _():
                    event(at)

    def forward_head(head, carry):
        own = pl.ds(pl.multiple_of(head * HS, HS), HS)
        for query in range(tiles):
            hooks(head, query, events)
            at_q = pl.ds(tile_at(query), TILE)
            q = qt[own, at_q]
            highest = jnp.full((1, TILE), -jnp.inf, F32)
            for key in range(query + 1):
                scores = masked(dot(k[pl.ds(tile_at(key), TILE), :], q), key, query)
                s_ref[pl.ds(key * TILE, TILE), :] = scores
                highest = jnp.maximum(highest, jnp.max(scores, 0, keepdims=True))
            total = jnp.zeros((1, TILE), F32)
            for key in range(query + 1):
                exponent = jnp.exp(s_ref[pl.ds(key * TILE, TILE), :] - highest)
                s_ref[pl.ds(key * TILE, TILE), :] = exponent
                total = total + jnp.sum(exponent, 0, keepdims=True)
            inverse = 1.0 / total
            mixed = jnp.zeros((HS, TILE), F32)
            for key in range(query + 1):
                softmax = (s_ref[pl.ds(key * TILE, TILE), :] * inverse).astype(BF)
                mixed = mixed + dot(vt[:, pl.ds(tile_at(key), TILE)], softmax)
            ot[own, at_q] = mixed.astype(BF)
            l_ref[head, :, at_q] = jnp.broadcast_to(highest + jnp.log(total), (8, TILE))
        return carry

    lax.fori_loop(0, heads, forward_head, 0)
    for copy in c_core + c_far:
        copy.wait_recv()
    ub_grad[...] = jnp.zeros_like(ub_grad)

    def attention_grad(slot, carry):
        tokens = pl.ds(pl.multiple_of(slot * local, local), local)
        dot_rows[:, tokens] = dot_nt(small[query_width:, :], cg[slot]).astype(BF)
        return carry

    lax.fori_loop(0, 4, attention_grad, 0)
    other = pl.ds(pl.multiple_of((1 - dp) * columns, 128), columns) if shares else None
    own_part = pl.ds(pl.multiple_of(dp * columns, 128), columns) if shares else None
    sums, homes = ({}, {})

    def sum_arrives(at):
        span = pl.ds(at * TILE, TILE)
        sums[at].wait_recv()
        sums[at].wait_send()
        total = big_own[span, :] + g_recv[span, :].astype(F32)
        big_own[span, :] = total

        @pl.when(place.is_swapped)
        def _():
            g_send[span, :] = total.astype(BF)
            homes[at].start()

    pieces = wide // TILE
    for piece in range(pieces):
        units = slice(piece * TILE, (piece + 1) * TILE)
        if shares:
            for copy in big_dp[2 * piece] + big_dp[2 * piece + 1]:
                copy.wait_recv()

        def perceptron(slot, carry):
            pre = dot_nt(a2[slot], up_w[units, :]) + norm_ref[4:5, units]
            below = 0.5 * (1.0 + lax.erf(pre * math.sqrt(0.5)))
            h[slot, :, units] = (pre * below).astype(BF)
            density = jnp.exp(-0.5 * pre * pre) * (1.0 / math.sqrt(2.0 * math.pi))
            grad = dot_nt(cg[slot], down_w[units, :]) * (below + pre * density)
            grad = grad.astype(BF)
            dh[slot, :, units] = grad
            ub_grad[0:1, units] += jnp.sum(grad.astype(F32), 0, keepdims=True)
            return carry

        lax.fori_loop(0, 4, perceptron, 0)
        if piece == 0:
            for at in range(4, len(big_swaps)):
                big_arrives(at)
        if shares and piece >= 2:
            sum_arrives(piece - 2)
            sum_arrives(pieces + piece - 2)
        for at, left, right in ((piece, dh, a2), (pieces + piece, h, cg)):
            span = pl.ds(at * TILE, TILE)
            total = 0.0
            for slot in range(4):
                total = total + dot_tn(left[slot, :, units], right[slot])
            if shares:
                tmp[...] = total
                g_send[span, :] = tmp[:, other].astype(BF)
                sums[at] = copies.remote(g_send.at[span], g_recv.at[span], place.dp_peers[0])
                big_own[span, :] = tmp[:, own_part]
                homes[at] = copies.homeward(g_send.at[span], big_land.at[span], place.swap)
            else:
                big_own[span, :] = total
    copies.sends = [
        copy for copy in copies.sends if not any(copy is other for other in sums.values())
    ]
    leaving = [copies.local(held, out) for held, out in zip(kept, kept_outs)]

    def branches(slot):
        tokens = pl.ds(slot * local, local)
        return dot(h[slot], down_w[...]) + dot_tn(ot[:, tokens], small[query_width:, :])

    y_cores = {}
    for slot in (3, 2):
        at = slot - 2
        a2[at] = branches(slot).astype(BF)
        y_cores[at] = copies.remote(a2.at[at], y_from.at[at], place.core)
    if shares:
        sum_arrives(pieces - 2)
        sum_arrives(2 * pieces - 2)
    branch = branches(1)
    y_cores[1].wait_recv()
    a2[2] = (branch + y_from[1].astype(F32)).astype(BF)
    y_nexts = [
        copies.remote(a2.at[2, span], y_got.at[span], place.next)
        for at, span in enumerate(spans)
    ]
    branch = branches(0)
    y_cores[0].wait_recv()
    y_keep[...] = branch + y_from[0].astype(F32)
    y_homes = [swapped(a2.at[3, span], y_land.at[span]) for span in spans]

    def y_arrives(at):
        y_nexts[at].wait_recv()
        span = spans[at]
        a2[3, span, :] = (y_keep[span, :] + y_got[span, :].astype(F32)).astype(BF)
        y_homes[at][0]()

    later = [((0, 7), y_arrives, 0), ((1, 7), y_arrives, 1)]
    if shares:
        later += [((0, 5), sum_arrives, at) for at in (pieces - 1, 2 * pieces - 1)]

    dk[...] = jnp.zeros_like(dk)
    dv[...] = jnp.zeros_like(dv)

    def backward_head(head, carry):
        own = pl.ds(pl.multiple_of(head * HS, HS), HS)
        for query in range(tiles):
            hooks(head, query, later)
            at_q = pl.ds(tile_at(query), TILE)
            q, do = (qt[own, at_q], dot_rows[own, at_q])
            scaled = do * jnp.asarray(1.0 / math.sqrt(HS), BF)
            log_total = l_ref[head, 0:1, at_q]
            inner = jnp.zeros((1, TILE), F32)
            for key in range(query + 1):
                at_k = pl.ds(tile_at(key), TILE)
                at_s = pl.ds(key * TILE, TILE)
                softmax = jnp.exp(masked(dot(k[at_k, :], q), key, query) - log_total)
                prob_grad = dot(v[at_k, :], scaled)
                s_ref[at_s, :] = softmax
                d_ref[at_s, :] = prob_grad
                inner = inner + jnp.sum(softmax * prob_grad, 0, keepdims=True)
            query_grad = jnp.zeros((HS, TILE), F32)
            for key in range(query + 1):
                at_k = pl.ds(tile_at(key), TILE)
                at_s = pl.ds(key * TILE, TILE)
                softmax = s_ref[at_s, :]
                score_grad = (softmax * (d_ref[at_s, :] - inner)).astype(BF)
                query_grad = query_grad + dot(kt[:, at_k], score_grad)
                dk[at_k, :] += dot_nt(score_grad, q)
                dv[at_k, :] += dot_nt(softmax.astype(BF), do)
            table = pl.ds(query * TILE, TILE)
            dqt[own, at_q] = rotate(query_grad, cos_ref[:, table], -sin_ref[:, table]).astype(BF)
        return carry

    lax.fori_loop(0, heads, backward_head, 0)
    for slot in range(4):
        block = at_slot(slot, rank)
        table = pl.ds(pl.multiple_of(block * local, local), local)
        tokens = pl.ds(slot * local, local)
        key_grad = dk[tokens, :].T * math.sqrt(HS)
        pair_grad[0:HS, tokens] = rotate(key_grad, cos_ref[:, table], -sin_ref[:, table])
        pair_grad[HS:, tokens] = dv[tokens, :].T

    for _, wait in y_homes:
        wait()
    for copy in leaving:
        copy.wait()

    @pl.when(place.is_swapped)
    def _():
        for at, copy in homes.items():
            copy.wait_send()
            copy.wait_recv()
            span = pl.ds(at * TILE, TILE)
            big_own[span, :] = big_land[span, :].astype(F32)

    copies.finish()


def first_pass(dp_size, x, c, entry, leave, shared, ids, vector, cosine, sine):
    local = x.shape[0]
    length = 4 * local
    part, columns = entry.shape
    query_width = HEADS * HS // 4
    width = 2 * query_width
    wide = part - query_width
    heads = query_width // HS
    gathers_pair = shared.shape[0] != D
    shares = columns != D
    held = (2 * wide if shares else 16, columns)
    tokens = ((4, local, D), BF)
    hidden = ((4, local, wide), BF)
    outs = [
        tokens,
        tokens,
        tokens,
        hidden,
        ((wide, D), BF),
        ((width, D), BF),
        ((dp_size, 4, shared.shape[0], 2 * HS) if gathers_pair else (D, 2 * HS), BF),
        ((query_width, length), BF),
        ((query_width, length), BF),
        ((2 * HS, length), F32),
        ((8, D), F32),
        ((8, wide), F32),
        ((2 * wide, columns), F32),
        ((local, D), BF),
    ]
    vmem = pl.BlockSpec(memory_space=pltpu.VMEM)
    copies = 64 + 12 * dp_size
    work = query_width * length * length
    return pl.pallas_call(
        functools.partial(first_kernel, dp_size),
        out_shape=[jax.ShapeDtypeStruct(shape, kind) for shape, kind in outs],
        in_specs=[vmem] * 9,
        out_specs=[pl.BlockSpec(memory_space=pl.ANY)] * 8 + [vmem] * (len(outs) - 8),
        scratch_shapes=[pltpu.VMEM(shape, kind) for shape, kind in outs[:8]]
        + [
            pltpu.VMEM(hidden[0], BF),
            pltpu.VMEM((wide, D), BF),
            pltpu.VMEM((width, columns), BF),
            pltpu.VMEM((wide, columns), BF),
            pltpu.VMEM((wide, columns), BF),
            pltpu.VMEM((shared.shape[0] if gathers_pair else 16, 2 * HS), BF),
            pltpu.VMEM(vector.shape, F32),
            pltpu.VMEM((query_width, 1), F32),
            pltpu.VMEM((2 * HS, 1), F32),
            pltpu.VMEM(held, BF),
            pltpu.VMEM((4, local, D), BF),
            pltpu.VMEM((2 * HS, D), BF),
            pltpu.VMEM((query_width, length), BF),
            pltpu.VMEM((query_width, length), BF),
            pltpu.VMEM((HS, length), BF),
            pltpu.VMEM((HS, length), BF),
            pltpu.VMEM((length, HS), BF),
            pltpu.VMEM((length, HS), BF),
            pltpu.VMEM((length, HS), F32),
            pltpu.VMEM((length, HS), F32),
            pltpu.VMEM((length, TILE), F32),
            pltpu.VMEM((length, TILE), F32),
            pltpu.VMEM((heads, 8, length), F32),
            pltpu.VMEM((1, length), jnp.int32),
            pltpu.VMEM((TILE, D), F32),
            pltpu.VMEM((2, local, D), BF),
            pltpu.VMEM((local, D), BF),
            pltpu.VMEM((local, D), F32),
            pltpu.VMEM(held, BF),
            pltpu.VMEM(held, BF),
            pltpu.SemaphoreType.DMA((copies,)),
            pltpu.SemaphoreType.DMA((copies,)),
        ],
        compiler_params=pltpu.CompilerParams(
            collective_id=0, has_side_effects=True, vmem_limit_bytes=59 << 20
        ),
        cost_estimate=pl.CostEstimate(
            flops=60 * work, bytes_accessed=30 << 20, transcendentals=work // HS
        ),
        name="gather_attend",
    )(x, c, entry, leave, shared, ids, vector, cosine, sine)


def column_sum(rows):
    return jnp.sum(rows, 0, keepdims=True)


def row_of(column):
    size = column.shape[0]
    down = lax.broadcasted_iota(jnp.int32, (size, size), 0)
    along = lax.broadcasted_iota(jnp.int32, (size, size), 1)
    return column_sum(jnp.where(down == along, column, 0.0))


def gap_of(grad, weight, first, second, anchor, rate, decay):
    return anchor - adamw_update(weight, first, second, grad, rate, decay)[2]


def second_kernel(dp_size, sums_pair, shares, *refs):
    refs = iter(refs)

    def take(number):
        return [next(refs) for _ in range(number)]

    late = take(5 + (8 if shares else 0))
    xg, dh, up_w, small, kvw, ot, dqt, pair_grad, norm_ref, ub_grad = take(10)
    if shares:
        shared, vector = (take(4) for _ in range(2))
    grad_ref, small_own, vector_row, shared_home, pair_parts = take(5)
    if shares:
        entry_sum, exit_sum, shared_sum, vector_sum = take(4)
    u_land, small_land, vector_home, stats, v_next, v_core, v_dp, s_core, s_next, s_dp = take(10)
    u_core, u_from, u_next, u_got, u_keep, u_home, p_from, p_next, p_got, full, g_send, g_recv = take(12)
    if shares:
        wide_buffers = [take(4), take(4)]
        small_buffers = [take(4), take(4)]
        shared_buffers, vector_buffers = (take(4), take(4))
    held = take(len(late))
    x_ref, c_ref, cg, a1, big_g = held[:5]
    entry, leave = (held[5:9], held[9:])
    send, receive = take(2)

    place = Place(dp_size)
    copies = Copies(send, receive)
    local = xg.shape[1]
    wide = dh.shape[2]
    columns = small_own.shape[1]
    query_width = ot.shape[0]
    place.meet([place.across])
    loads = [copies.local(source, target) for source, target in zip(late, held)]
    pair_core = copies.remote(pair_grad.at[:, pl.ds(2 * local, 2 * local)], p_from, place.core)
    stats[...] = jnp.zeros_like(stats)

    def normal_of(slot):
        inputs = xg[slot].astype(F32)
        centered = inputs - jnp.mean(inputs, -1, keepdims=True)
        return centered * lax.rsqrt(jnp.mean(centered * centered, -1, keepdims=True) + NORM_EPS)

    def joined_of(slot):
        tokens = pl.ds(slot * local, local)
        first = dot_tn(dqt[:, tokens], small[:query_width, :])
        second = dot(dh[slot], up_w[...])
        normal = normal_of(slot)
        stats[0:1, :D] += column_sum(first * normal)
        stats[1:2, :D] += column_sum(first)
        stats[2:3, :D] += column_sum(second * normal)
        stats[3:4, :D] += column_sum(second)
        return first * norm_ref[0:1, :] + second * norm_ref[2:3, :]

    def sent_home(source, target):
        return copies.swapped(source, target, place.is_swapped, place.swap)

    class GroupSum:
        def __init__(self, olds, grads, total, start, grad_start, size, buffers):
            self.olds, self.grads, self.total, self.buffers = (olds, grads, total, buffers)
            self.own, self.other = (
                pl.ds(pl.multiple_of(start + at * size, 8), size) for at in (place.half, 1 - place.half)
            )
            self.grad_own, self.grad_other = (
                pl.ds(pl.multiple_of(grad_start + at * size, 8), size)
                for at in (place.half, 1 - place.half)
            )

        def gap(self, span, grad_span):
            olds = (ref[span, :] for ref in self.olds)
            return gap_of(self.grads[grad_span, :], *olds, MATRIX_RATE, MATRIX_DECAY)

        def to_core(self):
            sent, got = self.buffers[:2]
            sent[...] = self.gap(self.other, self.grad_other)
            self.copy = copies.remote(sent, got, place.core)
            self.total[self.own, :] = self.gap(self.own, self.grad_own)

        def to_chip(self):
            self.copy.wait_recv()
            low, far = self.buffers[2:]
            low[...] = (self.total[self.own, :] + self.buffers[1][...]).astype(BF)
            self.copy = copies.remote(low, far, place.across)

        def back(self):
            self.copy.wait_recv()
            low, far = self.buffers[2:]
            self.total[self.own, :] = low[...].astype(F32) + far[...].astype(F32)
            part = self.total.at[self.own]
            self.copy = copies.remote(part, part, place.core)

    step = local // 2
    spans = [pl.ds(at * step, step) for at in range(2)]
    u_cores = {}
    for slot in (3, 2):
        at = slot - 2
        u_core[at] = joined_of(slot).astype(BF)
        u_cores[at] = copies.remote(u_core.at[at], u_from.at[at], place.core)
    pair_core.wait_recv()
    p_next[...] = pair_grad[:, local : 2 * local] + p_from[:, local:]
    pair_next = copies.remote(p_next, p_got, place.next)
    joined = joined_of(1)
    u_cores[1].wait_recv()
    u_next[...] = (joined + u_from[1].astype(F32)).astype(BF)
    u_nexts = [
        copies.remote(u_next.at[span], u_got.at[span], place.next, starts=at == 0)
        for at, span in enumerate(spans)
    ]
    wide_sums, small_sums = ([], [])
    if shares:
        half = wide // 2
        for copy in loads[4:]:
            copy.wait()
        for olds, start, total, buffers in (
            (entry, 0, entry_sum, wide_buffers[0]),
            (leave, wide, exit_sum, wide_buffers[1]),
        ):
            wide_sums.append(GroupSum(olds, big_g, total, query_width, start, half, buffers))
            wide_sums[-1].to_core()

    if not shares:
        loads[4].wait()
    loads[2].wait()
    loads[3].wait()
    turned = 0.0
    turned_out = 0.0
    for slot in range(4):
        tokens = pl.ds(slot * local, local)
        turned = turned + dot(dqt[:, tokens], a1[slot])
        turned_out = turned_out + dot(ot[:, tokens], cg[slot])
    if shares:
        full[:query_width, :] = turned
        full[query_width:, :] = turned_out
        other = pl.ds(pl.multiple_of((1 - place.dp) * columns, 128), columns)
        g_send[...] = full[:, other].astype(BF)
        small_sum = copies.remote(g_send, g_recv, place.dp_peers[0])
        small_home = copies.homeward(g_send, small_land, place.swap)
        small_own[...] = full[:, pl.ds(pl.multiple_of(place.dp * columns, 128), columns)]
        for part in wide_sums:
            part.to_chip()
    else:
        small_own[:query_width, :] = turned
        small_own[query_width:, :] = turned_out

    joined = joined_of(0)
    u_cores[0].wait_recv()
    pair_next.wait_recv()
    pair_sum = (pair_grad[:, :local] + p_from[:, :local] + p_got[...]).astype(BF)
    through_pair = dot_nt(pair_sum.T, kvw[...])
    u_keep[...] = joined + u_from[0].astype(F32) + through_pair * norm_ref[0:1, :]
    u_homes = [sent_home(u_home.at[span], u_land.at[span]) for span in spans]

    def u_arrives(at):
        u_nexts[at].wait_recv()
        if at == 0:
            u_nexts[1].start()
        span = spans[at]
        u_home[span, :] = (u_keep[span, :] + u_got[span, :].astype(F32)).astype(BF)
        u_homes[at][0]()

    stats[0:1, :D] += column_sum(through_pair * normal_of(0))
    stats[1:2, :D] += column_sum(through_pair)
    stats[4:5, :D] = column_sum(cg[0].astype(F32))
    stats[5:6, : 2 * HS] = row_of(jnp.sum(pair_sum.astype(F32), 1, keepdims=True))
    tail = pl.ds(8 + place.rank, 1)
    stats[tail, :query_width] = row_of(jnp.sum(dqt[...].astype(F32), 1, keepdims=True))
    stats[tail, query_width : query_width + wide] = ub_grad[0:1, :]
    vector_core = copies.remote(stats, v_core, place.core)
    pair_parts[...] = dot(pair_sum, a1[0]).T.reshape(pair_parts.shape)
    if sums_pair:
        shared_core = copies.remote(pair_parts, s_core, place.core)
    u_arrives(0)
    if shares:
        small_sum.wait_recv()
        copies.sent(small_sum)
        total = small_own[...] + g_recv[...].astype(F32)
        small_own[...] = total

        @pl.when(place.is_swapped)
        def _():
            g_send[...] = total.astype(BF)
            small_home.start()

    vector_core.wait_recv()
    copies.sent(vector_core)
    stats[...] = stats[...] + v_core[...]
    vector_next = copies.remote(stats, v_next, place.next)
    if sums_pair:
        shared_core.wait_recv()
        copies.sent(shared_core)
        pair_parts[...] = pair_parts[...] + s_core[...]
        shared_next = [
            copies.remote(pair_parts.at[at * 4 + flip_one(place.rank)], s_next.at[at], place.next)
            for at in range(dp_size)
        ]
    for part in wide_sums:
        part.back()
    u_arrives(1)
    vector_next.wait_recv()
    copies.sent(vector_next)
    stats[...] = stats[...] + v_next[...]
    vector_dp = [
        copies.remote(stats, v_dp.at[at], peer) for at, peer in enumerate(place.dp_peers)
    ]
    if sums_pair:
        for at, copy in enumerate(shared_next):
            copy.wait_recv()
            s_next[at] = s_next[at] + pair_parts[at * 4 + place.rank]
        shared_dp = [
            copies.remote(s_next.at[(place.dp + at + 1) % dp_size], s_dp.at[at], peer)
            for at, peer in enumerate(place.dp_peers)
        ]
    for copy in vector_dp:
        copy.wait_recv()
        copies.sent(copy)
    total = stats[...]
    for at in range(dp_size - 1):
        total = total + v_dp[at]
    stats[...] = total
    late_homes = [sent_home(stats, vector_home)]
    if sums_pair:
        for copy in shared_dp:
            copy.wait_recv()
        total = s_next[place.dp]
        for at in range(dp_size - 1):
            total = total + s_dp[at]
        s_core[0] = total
        late_homes.append(sent_home(s_core.at[0], shared_home))
    for start, _ in late_homes:
        start()

    if shares:

        @pl.when(place.is_swapped)
        def _():
            small_home.wait_send()
            small_home.wait_recv()
            small_own[...] = small_land[...].astype(F32)

        size = query_width // 2
        for olds, start, total, buffers in (
            (entry, 0, entry_sum, small_buffers[0]),
            (leave, query_width, exit_sum, small_buffers[1]),
        ):
            small_sums.append(GroupSum(olds, small_own, total, 0, start, size, buffers))
            small_sums[-1].to_core()
        for part in small_sums:
            part.to_chip()

    loads[0].wait()
    loads[1].wait()

    def end_rows(at):
        u_homes[at][1]()
        span = spans[at]
        inputs = x_ref[span, :].astype(F32)
        centered = inputs - jnp.mean(inputs, -1, keepdims=True)
        scale = lax.rsqrt(jnp.mean(centered * centered, -1, keepdims=True) + NORM_EPS)
        normal = centered * scale
        joined = u_land[span, :].astype(F32)
        grad_ref[span, :] = c_ref[span, :].astype(F32) + scale * (
            joined
            - jnp.mean(joined, -1, keepdims=True)
            - normal * jnp.mean(joined * normal, -1, keepdims=True)
        )

    end_rows(0)
    for _, wait in late_homes:
        wait()
    part = query_width + wide
    rows = [vector_home[at : at + 1, :D] for at in (0, 1, 2, 3, 4, 4)]
    rows.append(vector_home[5:6, : 2 * HS])
    rows += [vector_home[8 + at : 9 + at, :part] for at in range(4)]
    vector_row[...] = jnp.concatenate(rows, 1)
    if shares:
        whole_sums = []
        for olds, grads, buffers, rate, decay in (
            (vector, vector_row, vector_buffers, VECTOR_RATE, 0.0),
            (shared, shared_home, shared_buffers, MATRIX_RATE, MATRIX_DECAY),
        ):
            buffers[0][...] = gap_of(grads[...], *(ref[...] for ref in olds), rate, decay)
            whole_sums.append(copies.remote(buffers[0], buffers[1], place.core))
        for at, buffers in enumerate((vector_buffers, shared_buffers)):
            whole_sums[at].wait_recv()
            buffers[2][...] = buffers[0][...] + buffers[1][...]
            whole_sums[at] = copies.remote(buffers[2], buffers[3], place.across)
    end_rows(1)
    if shares:
        for part in small_sums:
            part.back()
        for copy, buffers, total in (
            (whole_sums[0], vector_buffers, vector_sum),
            (whole_sums[1], shared_buffers, shared_sum),
        ):
            copy.wait_recv()
            total[...] = buffers[2][...] + buffers[3][...]
        for part in wide_sums + small_sums:
            part.copy.wait_recv()
    copies.finish()


def second_pass(dp_size, late, arrays, olds, piece):
    x = late[0]
    up_w, small = arrays[2:4]
    local = x.shape[0]
    width = small.shape[0]
    query_width = width // 2
    wide = up_w.shape[0]
    shares = len(olds) > 0
    columns = olds[0].shape[1] if shares else D
    sums_pair = piece % 16 == 0
    held = (width if shares else 16, columns)
    parts = (4 * dp_size, piece, 2 * HS) if sums_pair else (1, D, 2 * HS)
    own = (piece if sums_pair else 8, 2 * HS)
    vector = (1, 6 * D + 2 * HS + 4 * (query_width + wide))
    outs = [(local, D), (width, columns), vector, own, parts]
    scratch = [
        ((local, D), BF),
        (held, BF),
        ((16, 1024), F32),
        ((16, 1024), F32),
        ((16, 1024), F32),
        ((16, 1024), F32),
        ((dp_size - 1, 16, 1024), F32),
        (parts, F32),
        ((dp_size,) + own, F32),
        ((dp_size - 1,) + own, F32),
        ((2, local, D), BF),
        ((2, local, D), BF),
        ((local, D), BF),
        ((local, D), BF),
        ((local, D), F32),
        ((local, D), BF),
        ((2 * HS, 2 * local), F32),
        ((2 * HS, local), F32),
        ((2 * HS, local), F32),
        ((width, D), F32),
        (held, BF),
        (held, BF),
    ]
    if shares:
        outs += [olds[0].shape, olds[4].shape, own, vector]
        for size in (wide // 2, wide // 2, query_width // 2, query_width // 2):
            scratch += [((size, columns), kind) for kind in (F32, F32, BF, BF)]
        scratch += [(own, F32)] * 4 + [(vector, F32)] * 4
    late = list(late) + list(olds[:8])
    scratch += [(array.shape, array.dtype) for array in late]
    arrays = late + list(arrays) + list(olds[8:])
    vmem = pl.BlockSpec(memory_space=pltpu.VMEM)
    work = 4 * local * D * D
    semaphores = pltpu.SemaphoreType.DMA((72 + 3 * dp_size,))
    return pl.pallas_call(
        functools.partial(second_kernel, dp_size, sums_pair, shares),
        out_shape=[jax.ShapeDtypeStruct(shape, F32) for shape in outs],
        in_specs=[pl.BlockSpec(memory_space=pl.ANY)] * len(late) + [vmem] * (len(arrays) - len(late)),
        out_specs=[vmem] * len(outs),
        scratch_shapes=[pltpu.VMEM(shape, kind) for shape, kind in scratch] + [semaphores] * 2,
        compiler_params=pltpu.CompilerParams(
            collective_id=1, has_side_effects=True, vmem_limit_bytes=60 << 20
        ),
        cost_estimate=pl.CostEstimate(flops=8 * work, bytes_accessed=30 << 20, transcendentals=0),
        name="sum_branches",
    )(*arrays)


def third_kernel(groups, *refs):
    refs = iter(refs)

    def take(number):
        return [next(refs) for _ in range(number)]

    grads = [take(2), take(2), take(1), take(1)]
    olds = [take(6) for _ in range(4)]
    news = [take(6) for _ in range(4)]
    step = pl.program_id(0)

    def update(at, grad, rate, decay):
        weight, first, second, anchor, velocity, total = (ref[...] for ref in olds[at])
        first, second, weight = adamw_update(weight, first, second, grad, rate, decay)
        change = total / groups
        momentum = OUTER_BETA * velocity + change
        outer = anchor - OUTER_RATE * (change + OUTER_BETA * momentum)
        for ref, value in zip(news[at], (first, second, weight, change, momentum, outer)):
            ref[...] = value

    for at in range(2):
        head, rest = grads[at]
        update(at, jnp.where(step == 0, head[...], rest[...]), MATRIX_RATE, MATRIX_DECAY)

    @pl.when(step == 0)
    def _():
        update(2, grads[2][0][...], MATRIX_RATE, MATRIX_DECAY)
        update(3, grads[3][0][...], VECTOR_RATE, 0.0)


def third_pass(groups, big, small, shared_grad, vector_grad, entry, leave, shared, vector):
    rows, columns = entry[0].shape
    size = small.shape[0] // 2
    wide = rows // size - 1

    def block(index):
        return pl.BlockSpec((size, columns), index)

    def all_of(array):
        return pl.BlockSpec(array.shape, lambda i: (0, 0))

    here = block(lambda i: (i, 0))
    grad_specs = [
        block(lambda i: (0, 0)),
        block(lambda i: (jnp.maximum(i - 1, 0), 0)),
        block(lambda i: (1, 0)),
        block(lambda i: (wide + jnp.maximum(i - 1, 0), 0)),
        all_of(shared_grad),
        all_of(vector_grad),
    ]
    specs = [here] * 12 + [all_of(array) for array in shared + vector]
    out_specs = [here] * 12 + [all_of(shared[0])] * 6 + [all_of(vector[0])] * 6
    outs = [array for array in (entry[0], leave[0], shared[0], vector[0]) for _ in range(6)]
    return pl.pallas_call(
        functools.partial(third_kernel, groups),
        grid=(rows // size,),
        out_shape=[jax.ShapeDtypeStruct(array.shape, F32) for array in outs],
        in_specs=grad_specs + specs,
        out_specs=out_specs,
        compiler_params=pltpu.CompilerParams(vmem_limit_bytes=60 << 20),
        cost_estimate=pl.CostEstimate(flops=1 << 26, bytes_accessed=40 << 20, transcendentals=1 << 20),
        name="update_weights",
    )(small, big, small, big, shared_grad, vector_grad, *entry, *leave, *shared, *vector)


def shards(
    hidden_in,
    doc_ids,
    out_cotangent,
    entry_weight,
    entry_first,
    entry_second,
    entry_anchor,
    entry_velocity,
    exit_weight,
    exit_first,
    exit_second,
    exit_anchor,
    exit_velocity,
    shared_weight,
    shared_first,
    shared_second,
    shared_anchor,
    shared_velocity,
    vector_weight,
    vector_first,
    vector_second,
    vector_anchor,
    vector_velocity,
):
    batch, local_len = hidden_in.shape[:2]
    parts = lax.axis_size("mp")
    group, rank = (lax.axis_index("group"), lax.axis_index("mp"))
    is_swapped = (group % 2) != (rank // 2)
    rank = jnp.where(is_swapped, jnp.bitwise_xor(rank, 2), rank)
    length = local_len * parts
    part_width = entry_weight.shape[2]
    query_width = HEADS * HS // parts
    heads = query_width // HS

    dp_size = lax.axis_size("dp")
    groups = lax.axis_size("group")
    order = jnp.bitwise_xor(jnp.arange(parts), rank)
    piece = shared_weight.shape[1]
    shared_piece = shared_weight[0]
    if piece % 16:
        pieces = gather_square(swapped_parts(shared_piece.astype(BF)))
        pieces = jnp.take(pieces, order, axis=0)
        shared_piece = gather_dp(pieces.reshape(-1, 2 * HS), 0)
    half = ROT // 2
    frequency = 10000.0 ** (-(np.arange(half) * 2.0 / ROT))
    angles = frequency.astype(np.float32)[:, None] * np.arange(length, dtype=np.float32)[None, :]
    cosine_table = jnp.asarray(np.cos(angles.astype(np.float64)).astype(np.float32))
    sine_table = jnp.asarray(np.sin(angles.astype(np.float64)).astype(np.float32))
    entry = [array[0].T for array in (entry_weight, entry_first, entry_second)]
    entry += [array.T for array in (entry_anchor, entry_velocity)]
    leave = [array[0] for array in (exit_weight, exit_first, exit_second)]
    leave += [exit_anchor, exit_velocity]
    shared = [array[0] for array in (shared_weight, shared_first, shared_second)]
    shared += [shared_anchor, shared_velocity]
    vector = [vector_weight, vector_first, vector_second, vector_anchor[None], vector_velocity[None]]
    shares = dp_size == 2 and leave[0].shape[1] % 128 == 0 and piece % 16 == 0
    weights = [entry[0], leave[0]]
    if not shares:
        weights = [gather_dp(swapped_parts(array.astype(BF)), 1) for array in weights]
    (
        inputs, cots, attn_input, hidden_grad, up_w, small, pair_weight, attended, query_grad,
        pair_rows, norms, up_bias_rows, big_grad, branch_home,
    ) = first_pass(
        dp_size,
        hidden_in[0],
        out_cotangent[0],
        *weights,
        shared_piece,
        doc_ids,
        vector_weight,
        cosine_table,
        sine_table,
    )
    home_bias = vector_weight[0, 4 * D : 5 * D] + vector_weight[0, 5 * D : 6 * D]
    block_output = hidden_in[0].astype(F32) + branch_home.astype(F32) + home_bias
    late = (hidden_in[0], out_cotangent[0], cots, attn_input, big_grad)
    arrays = (
        inputs, hidden_grad, up_w, small, pair_weight.reshape(D, 2 * HS), attended, query_grad,
        pair_rows, norms, up_bias_rows,
    )
    olds = [array for arrays in (entry, leave, shared, vector) for array in arrays[:4]]
    input_grad, small_grad, vector_grad, shared_grad, pair_parts, *totals = second_pass(
        dp_size, late, arrays, olds if shares else [], piece
    )
    if not shares:
        big_grad, small_grad = (
            swapped_parts(scatter_dp(array, 1, F32)) for array in (big_grad, small_grad)
        )
        if piece % 16:
            grad_pieces = pair_parts.reshape(dp_size, parts, -1, 2 * HS)
            grad_pieces = jnp.take(grad_pieces, order, axis=1).swapaxes(0, 1)
            shared_grad = scatter_dp(scatter_square(grad_pieces, F32), 0, F32)
            shared_grad = swapped_parts(shared_grad.reshape(-1, 2 * HS))
        size, wide = (small_grad.shape[0] // 2, big_grad.shape[0] // 2)
        gaps = (
            gap_of(
                jnp.concatenate([small_grad[:size], big_grad[:wide]]),
                *entry[:4], MATRIX_RATE, MATRIX_DECAY,
            ),
            gap_of(
                jnp.concatenate([small_grad[size:], big_grad[wide:]]),
                *leave[:4], MATRIX_RATE, MATRIX_DECAY,
            ),
            gap_of(shared_grad, *shared[:4], MATRIX_RATE, MATRIX_DECAY),
            gap_of(vector_grad, *vector[:4], VECTOR_RATE, 0.0),
        )
        totals = lax.psum(gaps, "group")
    updated = third_pass(
        groups, big_grad, small_grad, shared_grad, vector_grad,
        *(arrays + [total] for arrays, total in zip((entry, leave, shared, vector), totals)),
    )
    updated = list(updated)
    results = [block_output[None], input_grad[None]]
    for at in range(3):
        own = updated[6 * at : 6 * at + 6]
        if at == 0:
            own = [array.T for array in own]
        results += [array[None] for array in own[:3]] + own[3:]
    results += updated[18:21] + [array[0] for array in updated[21:24]]
    return tuple(results)


def solution(mesh):
    in_specs = (
        P(("group", "dp"), "mp", None),
        P(("group", "dp"), "mp"),
        P(("group", "dp"), "mp", None),
        P("group", "dp", "mp"),
        P("group", "dp", "mp"),
        P("group", "dp", "mp"),
        P("dp", "mp"),
        P("dp", "mp"),
        P("group", "mp", "dp"),
        P("group", "mp", "dp"),
        P("group", "mp", "dp"),
        P("mp", "dp"),
        P("mp", "dp"),
        P("group", ("dp", "mp"), None),
        P("group", ("dp", "mp"), None),
        P("group", ("dp", "mp"), None),
        P(("dp", "mp"), None),
        P(("dp", "mp"), None),
        P("group", None),
        P("group", None),
        P("group", None),
        P(),
        P(),
    )
    out_specs = (
        P(("group", "dp"), "mp", None),
        P(("group", "dp"), "mp", None),
        P("group", "dp", "mp"),
        P("group", "dp", "mp"),
        P("group", "dp", "mp"),
        P("dp", "mp"),
        P("dp", "mp"),
        P("dp", "mp"),
        P("group", "mp", "dp"),
        P("group", "mp", "dp"),
        P("group", "mp", "dp"),
        P("mp", "dp"),
        P("mp", "dp"),
        P("mp", "dp"),
        P("group", ("dp", "mp"), None),
        P("group", ("dp", "mp"), None),
        P("group", ("dp", "mp"), None),
        P(("dp", "mp"), None),
        P(("dp", "mp"), None),
        P(("dp", "mp"), None),
        P("group", None),
        P("group", None),
        P("group", None),
        P(),
        P(),
        P(),
    )
    return jax.shard_map(shards, mesh=mesh, in_specs=in_specs, out_specs=out_specs, check_vma=False)
```

```python
import functools
import math

import jax
import jax.numpy as jnp
import numpy as np
from jax import lax
from jax.experimental import pallas as pl
from jax.experimental.pallas import tpu as pltpu
from jax.sharding import PartitionSpec as P

D = 768
HEADS = 12
HS = 64
ROT = 16
STEP = 5
IN_COLS = 3840


NORM_EPS = 1e-05
BETA_ONE = 0.9
BETA_TWO = 0.95
ADAM_EPS = 1e-08
MATRIX_RATE = 0.03
MATRIX_DECAY = 0.1
VECTOR_RATE = 0.3
OUTER_RATE = 0.7
OUTER_BETA = 0.9

TILE = 256
F32 = jnp.float32
BF = jnp.bfloat16


def dot(left, right):
    return jnp.dot(left, right, preferred_element_type=F32)


def dot_nt(left, right):
    return lax.dot_general(left, right, (((1,), (1,)), ((), ())), preferred_element_type=F32)


def dot_tn(left, right):
    return lax.dot_general(left, right, (((0,), (0,)), ((), ())), preferred_element_type=F32)


def adamw_update(weight, first, second, gradient, step_rate, decay):
    first_new = BETA_ONE * first + (1.0 - BETA_ONE) * gradient
    second_new = BETA_TWO * second + (1.0 - BETA_TWO) * gradient * gradient
    fix_first = 1.0 - BETA_ONE**STEP
    fix_second = 1.0 - BETA_TWO**STEP
    update = first_new / fix_first / (jnp.sqrt(second_new / fix_second) + ADAM_EPS)
    return (first_new, second_new, weight - step_rate * (update + decay * weight))


def pairs_of(size, bit):
    return [(at, at ^ bit) for at in range(size)]


def over_core(array):
    return lax.ppermute(array, "group", pairs_of(lax.axis_size("group"), 1))


def over_next(array):
    return lax.ppermute(array, "mp", pairs_of(lax.axis_size("mp"), 1))


def over_dp(array):
    return lax.ppermute(array, "dp", pairs_of(2, 1))


def swapped_parts(array):
    parts = lax.axis_size("mp")
    pairs = []
    for group in range(lax.axis_size("group")):
        for rank in range(parts):
            here = group * parts + rank
            there = (group ^ 1) * parts + (rank ^ 2)
            pairs.append((here, there if group % 2 != rank // 2 else here))
    return lax.ppermute(array, ("group", "mp"), pairs)


def gather_square(own):
    pair = jnp.stack([own, over_next(own)])
    return jnp.concatenate([pair, over_core(pair)], 0)


def scatter_square(slots, send_type):
    pair = slots[:2] + over_core(slots[2:].astype(send_type)).astype(F32)
    return pair[0] + over_next(pair[1].astype(send_type)).astype(F32)


def gather_dp(own, axis):
    if lax.axis_size("dp") == 2:
        other = over_dp(own)
        first = lax.axis_index("dp") == 0
        return jnp.concatenate(
            [jnp.where(first, own, other), jnp.where(first, other, own)], axis
        )
    return lax.all_gather(own, "dp", axis=axis, tiled=True)


def scatter_dp(array, axis, send_type):
    if lax.axis_size("dp") == 2:
        size = array.shape[axis] // 2
        mine = lax.axis_index("dp")
        kept = lax.dynamic_slice_in_dim(array, mine * size, size, axis)
        sent = lax.dynamic_slice_in_dim(array, (1 - mine) * size, size, axis)
        return kept + over_dp(sent.astype(send_type)).astype(F32)
    return lax.psum_scatter(array, "dp", scatter_dimension=axis, tiled=True)


def flip_one(index):
    return index + 1 - 2 * (index % 2)


def flip_two(index):
    return index + 2 - 4 * ((index // 2) % 2)


def at_slot(slot, rank):
    rank = flip_one(rank) if slot % 2 else rank
    return flip_two(rank) if slot // 2 else rank


class Copies:
    def __init__(self, send, receive):
        self.send, self.receive, self.used, self.sends = (send, receive, 0, [])

    def remote(self, source, target, device, starts=True):
        at = self.used
        self.used += 1
        copy = pltpu.make_async_remote_copy(
            src_ref=source,
            dst_ref=target,
            send_sem=self.send.at[at],
            recv_sem=self.receive.at[at],
            device_id=device,
            device_id_type=pl.DeviceIdType.MESH,
        )
        if starts:
            copy.start()
        self.sends.append(copy)
        return copy

    def swapped(self, source, target, is_swapped, device):
        at = self.used
        self.used += 1
        far = pltpu.make_async_remote_copy(
            src_ref=source,
            dst_ref=target,
            send_sem=self.send.at[at],
            recv_sem=self.receive.at[at],
            device_id=device,
            device_id_type=pl.DeviceIdType.MESH,
        )
        near = pltpu.make_async_copy(source, target, self.receive.at[at])

        def start():
            @pl.when(is_swapped)
            def _():
                far.start()

            @pl.when(jnp.logical_not(is_swapped))
            def _():
                near.start()

        def wait():
            @pl.when(is_swapped)
            def _():
                far.wait_send()
                far.wait_recv()

            @pl.when(jnp.logical_not(is_swapped))
            def _():
                near.wait()

        return (start, wait)

    def homeward(self, source, target, device):
        at = self.used
        self.used += 1
        return pltpu.make_async_remote_copy(
            src_ref=source,
            dst_ref=target,
            send_sem=self.send.at[at],
            recv_sem=self.receive.at[at],
            device_id=device,
            device_id_type=pl.DeviceIdType.MESH,
        )

    def local(self, source, target):
        at = self.used
        self.used += 1
        copy = pltpu.make_async_copy(source, target, self.receive.at[at])
        copy.start()
        return copy

    def sent(self, copy):
        copy.wait_send()
        self.sends = [other for other in self.sends if other is not copy]

    def finish(self):
        for copy in self.sends:
            copy.wait_send()


class Place:
    def __init__(self, dp_size):
        group, self.dp, home = (lax.axis_index("group"), lax.axis_index("dp"), lax.axis_index("mp"))
        core, upper = (group % 2, home // 2)
        self.is_swapped = core != upper
        self.home = home
        self.rank = jnp.where(self.is_swapped, flip_two(home), home)
        self.swap = {"group": flip_one(group), "mp": flip_two(home)}
        self.core = {"group": flip_one(group)}
        self.across = {"group": flip_two(group)}
        self.half = core
        self.next = {"mp": flip_one(home)}
        self.dp_peers = [{"dp": (self.dp + step) % dp_size} for step in range(1, dp_size)]

    def meet(self, others=()):
        barrier = pltpu.get_barrier_semaphore()
        peers = [self.core, self.next, self.swap] + self.dp_peers + list(others)
        for peer in peers:
            pl.semaphore_signal(
                barrier, inc=1, device_id=peer, device_id_type=pl.DeviceIdType.MESH
            )
        pl.semaphore_wait(barrier, len(peers))


def column_of(row):
    size = row.shape[1]
    down = lax.broadcasted_iota(jnp.int32, (size, size), 0)
    along = lax.broadcasted_iota(jnp.int32, (size, size), 1)
    return jnp.sum(jnp.where(down == along, row, 0.0), 1, keepdims=True)


def rotate(rows, cosine, sine):
    half = ROT // 2
    one, two = (rows[:half], rows[half:ROT])
    return jnp.concatenate(
        [one * cosine - two * sine, two * cosine + one * sine, rows[ROT:]], 0
    )


def first_kernel(
    dp_size, x_ref, c_ref, entry_far, exit_far, shared_ref, ids_ref, vector_ref, cos_ref, sin_ref,
    xg_out, cg_out, a1_out, dh_out, up_out, small_out, kvw_out, ot_out,
    dqt, pair_grad, norm_ref, ub_grad, big_own, y_sum,
    xg, cg, a1, dh, up_w, small, kvw, ot, h, down_w, small_ref, up_ref, down_ref, pair_ref, vector_other, qb_ref, kvb_ref, big_land, a2,
    kvt, qt, dot_rows, kt, vt, k, v, dk, dv, s_ref, d_ref, l_ref, idr, tmp,
    y_from, y_got, y_keep, g_send, g_recv, entry_ref, exit_ref, send, receive,
):
    place = Place(dp_size)
    rank, dp = (place.rank, place.dp)
    copies = Copies(send, receive)
    local = x_ref.shape[0]
    length = 4 * local
    columns = entry_ref.shape[1]
    shares = columns != D
    query_width = small.shape[0] // 2
    wide = up_w.shape[0]
    heads = query_width // HS
    gathers_pair = shared_ref.shape[0] != D
    kept = (xg, cg, a1, dh, up_w, small, kvw, ot)
    kept_outs = (xg_out, cg_out, a1_out, dh_out, up_out, small_out, kvw_out, ot_out)
    place.meet()
    vector_core = copies.remote(vector_ref, vector_other, place.core)
    weight_loads = [copies.local(entry_far, entry_ref), copies.local(exit_far, exit_ref)]

    def swapped(source, target):
        return copies.swapped(source, target, place.is_swapped, place.swap)

    def dp_part(ref, start, size):
        return ref.at[pl.ds(start, size), pl.ds(pl.multiple_of(dp * columns, 128), columns)]

    step = local // 2
    spans = [pl.ds(at * step, step) for at in range(2)]
    x_swaps = [swapped(x_ref.at[s], xg.at[0, s]) for s in spans]
    c_swaps = [swapped(c_ref.at[s], cg.at[0, s]) for s in spans]
    ids_swap = swapped(ids_ref, idr.at[:, pl.ds(0, local)])
    small_swaps, big_swaps, big_parts = ([], [], [])
    if shares:
        small_part = dp_part(small, 0, 2 * query_width)
        small_swaps = [swapped(small_ref, small_part)]
        for at in range(0, wide, TILE):
            for source, target in ((up_ref, up_w), (down_ref, down_w)):
                big_parts.append(dp_part(target, at, TILE))
                big_swaps.append(swapped(source.at[pl.ds(at, TILE)], big_parts[-1]))
    first = [ids_swap]
    if gathers_pair:
        pair_swap = swapped(pair_ref, kvw.at[dp, place.home])
        first.append(pair_swap)
    queue = iter([start for start, _ in x_swaps + small_swaps + c_swaps])

    def start_next():
        start = next(queue, None)
        if start is not None:
            start()

    start_next()
    start_next()
    if gathers_pair:
        pair_ref[...] = shared_ref[...].astype(BF)
    for start, _ in first:
        start()
    for copy in weight_loads:
        copy.wait()
    if shares:
        small_ref[:query_width, :] = entry_ref[:query_width, :].astype(BF)
        small_ref[query_width:, :] = exit_ref[:query_width, :].astype(BF)
        up_ref[...] = entry_ref[query_width:, :].astype(BF)
        down_ref[...] = exit_ref[query_width:, :].astype(BF)
    else:
        small[:query_width, :] = entry_ref[:query_width, :]
        small[query_width:, :] = exit_ref[:query_width, :]
        up_w[...] = entry_ref[query_width:, :]
        down_w[...] = exit_ref[query_width:, :]
    vector_core.wait_recv()

    def role_vector(start, size):
        span = slice(start, start + size)
        return jnp.where(place.is_swapped, vector_other[:, span], vector_ref[:, span])

    for at in range(4):
        norm_ref[at : at + 1, :] = role_vector(at * D, D)
    kvb_ref[...] = column_of(role_vector(6 * D, 2 * HS))
    part = query_width + wide
    tail = 6 * D + 2 * HS
    in_bias = role_vector(tail, part)
    for at in range(1, 4):
        in_bias = jnp.where(rank == at, role_vector(tail + at * part, part), in_bias)
    qb_ref[...] = column_of(in_bias[:, :query_width])
    norm_ref[4:5, :] = in_bias[:, query_width:]

    def normalise(slot):
        def body(at, carry):
            span = pl.ds(pl.multiple_of(at * 128, 128), 128)
            wide = xg[slot, span, :].astype(F32)
            centered = wide - jnp.mean(wide, -1, keepdims=True)
            normal = centered * lax.rsqrt(
                jnp.mean(centered * centered, -1, keepdims=True) + NORM_EPS
            )
            a1[slot, span, :] = (normal * norm_ref[0:1, :] + norm_ref[1:2, :]).astype(BF)
            a2[slot, span, :] = (normal * norm_ref[2:3, :] + norm_ref[3:4, :]).astype(BF)
            return carry

        lax.fori_loop(0, local // 128, body, 0)

    def lanes(ref, slot):
        return ref.at[:, pl.ds(slot * local, local)]

    x_next, x_core, x_far = ([], [], [])
    for span, (_, wait) in zip(spans, x_swaps):
        wait()
        start_next()
        x_next.append(copies.remote(xg.at[0, span], xg.at[1, span], place.next))
        x_core.append(copies.remote(xg.at[0, span], xg.at[2, span], place.core))
    small_dp = []
    for _, wait in small_swaps:
        wait()
        start_next()
        small_dp += [copies.remote(small_part, small_part, peer) for peer in place.dp_peers]
    ids_swap[1]()
    ids_next = copies.remote(lanes(idr, 0), lanes(idr, 1), place.next)
    ids_core = copies.remote(lanes(idr, 0), lanes(idr, 2), place.core)
    if gathers_pair:
        pair_swap[1]()
        own_pair = kvw.at[dp, rank]
        pair_next = copies.remote(own_pair, own_pair, place.next)
        pair_core = copies.remote(own_pair, own_pair, place.core)
    c_next, c_core, c_far, big_dp = ([], [], [], [])
    for span in spans:
        c_next.append(copies.remote(cg.at[0, span], cg.at[1, span], place.next, starts=False))
        c_core.append(copies.remote(cg.at[0, span], cg.at[2, span], place.core, starts=False))
        c_far.append(copies.remote(cg.at[1, span], cg.at[3, span], place.core, starts=False))
    for part in big_parts:
        big_dp.append([copies.remote(part, part, peer, starts=False) for peer in place.dp_peers])

    def c_sends(at):
        c_next[at].start()
        c_core[at].start()

    def c_arrives(at):
        @pl.when(place.is_swapped)
        def _():
            c_swaps[at][1]()
            c_sends(at)

        if at < len(big_swaps):
            big_swaps[at][0]()

    def c_passes(at):
        c_next[at].wait_recv()
        c_far[at].start()

    def big_arrives(at):
        big_swaps[at][1]()
        if at + 2 < len(big_swaps):
            big_swaps[at + 2][0]()
        for copy in big_dp[at]:
            copy.start()

    normalise(0)
    for span, copy in zip(spans, x_next):
        copy.wait_recv()
        x_far.append(copies.remote(xg.at[1, span], xg.at[3, span], place.core))
    for at in range(2):

        @pl.when(jnp.logical_not(place.is_swapped))
        def _():
            c_swaps[at][1]()
            c_sends(at)

    ids_next.wait_recv()
    ids_far = copies.remote(lanes(idr, 1), lanes(idr, 3), place.core)
    if gathers_pair:
        pair_next.wait_recv()
        next_pair = kvw.at[dp, flip_one(rank)]
        pair_far = copies.remote(next_pair, next_pair, place.core)
        pair_core.wait_recv()
        pair_far.wait_recv()
        pair_dp = [copies.remote(kvw.at[dp], kvw.at[dp], peer) for peer in place.dp_peers]
    events = [((0, 6), c_passes, 0), ((1, 5), c_passes, 1)]
    if shares:
        places = ((0, 5), (0, 7), (1, 6), (2, 3))
        events += [(place, big_arrives, at) for at, place in enumerate(places)]
    for copy in x_core:
        copy.wait_recv()
    normalise(2)
    normalise(1)
    for copy in x_far:
        copy.wait_recv()
    normalise(3)
    for copy in small_dp:
        copy.wait_recv()
    if gathers_pair:
        for copy in pair_dp:
            copy.wait_recv()
        kvt[...] = kvw[...].reshape(D, 2 * HS).T
    else:
        kvw[...] = shared_ref[...]
        kvt[...] = shared_ref[...].T
    c_arrives(0)
    for slot in range(4):
        block = at_slot(slot, rank)
        table = pl.ds(pl.multiple_of(block * local, local), local)
        cosine, sine = (cos_ref[:, table], sin_ref[:, table])
        tokens = pl.ds(slot * local, local)
        queries = dot_nt(small[0:query_width, :], a1[slot]) + qb_ref[...]
        for head in range(heads):
            turned = rotate(queries[head * HS : (head + 1) * HS], cosine, sine).astype(BF)
            qt[head * HS : (head + 1) * HS, tokens] = turned * jnp.asarray(1.0 / math.sqrt(HS), BF)
        pairs = dot_nt(kvt[...], a1[slot]) + kvb_ref[...]
        turned = rotate(pairs[:HS], cosine, sine).astype(BF)
        kt[:, tokens] = turned
        k[tokens, :] = turned.T
        value = pairs[HS:].astype(BF)
        vt[:, tokens] = value
        v[tokens, :] = value.T
    c_arrives(1)
    for copy in (ids_core, ids_far):
        copy.wait_recv()
    ids = idr[...].astype(F32)
    first_end = jnp.sum(jnp.where(ids < 0.5, 1.0, 0.0), 1, keepdims=True)
    second_end = jnp.sum(jnp.where(ids < 1.5, 1.0, 0.0), 1, keepdims=True)

    def document(position):
        position = position.astype(F32)
        return jnp.where(position < first_end, 0.0, jnp.where(position < second_end, 1.0, 2.0))

    tiles = length // TILE
    per = tiles // 4

    def tile_at(tile):
        return pl.multiple_of(at_slot(tile // per, rank) * local + (tile % per) * TILE, TILE)

    def masked(scores, key, query):
        edge = key == 0 or query == tiles - 1
        allowed = None
        if key == query:
            down = lax.broadcasted_iota(jnp.int32, (TILE, TILE), 0)
            allowed = down <= lax.broadcasted_iota(jnp.int32, (TILE, TILE), 1)
        if edge:
            down = document(lax.broadcasted_iota(jnp.int32, (TILE, 1), 0) + key * TILE)
            along = document(lax.broadcasted_iota(jnp.int32, (1, TILE), 1) + query * TILE)
            same = down == along
            allowed = same if allowed is None else allowed & same
        return scores if allowed is None else jnp.where(allowed, scores, -1e9)

    def hooks(head, query, todo):
        for (at_head, at_query), event, at in todo:
            if query == at_query:

                @pl.when(head == at_head)
                def _():
                    event(at)

    def forward_head(head, carry):
        own = pl.ds(pl.multiple_of(head * HS, HS), HS)
        for query in range(tiles):
            hooks(head, query, events)
            at_q = pl.ds(tile_at(query), TILE)
            q = qt[own, at_q]
            highest = jnp.full((1, TILE), -jnp.inf, F32)
            for key in range(query + 1):
                scores = masked(dot(k[pl.ds(tile_at(key), TILE), :], q), key, query)
                s_ref[pl.ds(key * TILE, TILE), :] = scores
                highest = jnp.maximum(highest, jnp.max(scores, 0, keepdims=True))
            total = jnp.zeros((1, TILE), F32)
            for key in range(query + 1):
                exponent = jnp.exp(s_ref[pl.ds(key * TILE, TILE), :] - highest)
                s_ref[pl.ds(key * TILE, TILE), :] = exponent
                total = total + jnp.sum(exponent, 0, keepdims=True)
            inverse = 1.0 / total
            mixed = jnp.zeros((HS, TILE), F32)
            for key in range(query + 1):
                softmax = (s_ref[pl.ds(key * TILE, TILE), :] * inverse).astype(BF)
                mixed = mixed + dot(vt[:, pl.ds(tile_at(key), TILE)], softmax)
            ot[own, at_q] = mixed.astype(BF)
            l_ref[head, :, at_q] = jnp.broadcast_to(highest + jnp.log(total), (8, TILE))
        return carry

    lax.fori_loop(0, heads, forward_head, 0)
    for copy in c_core + c_far:
        copy.wait_recv()
    ub_grad[...] = jnp.zeros_like(ub_grad)

    def attention_grad(slot, carry):
        tokens = pl.ds(pl.multiple_of(slot * local, local), local)
        dot_rows[:, tokens] = dot_nt(small[query_width:, :], cg[slot]).astype(BF)
        return carry

    lax.fori_loop(0, 4, attention_grad, 0)
    other = pl.ds(pl.multiple_of((1 - dp) * columns, 128), columns) if shares else None
    own_part = pl.ds(pl.multiple_of(dp * columns, 128), columns) if shares else None
    sums, homes = ({}, {})

    def sum_arrives(at):
        span = pl.ds(at * TILE, TILE)
        sums[at].wait_recv()
        sums[at].wait_send()
        total = big_own[span, :] + g_recv[span, :].astype(F32)
        big_own[span, :] = total

        @pl.when(place.is_swapped)
        def _():
            g_send[span, :] = total.astype(BF)
            homes[at].start()

    pieces = wide // TILE
    for piece in range(pieces):
        units = slice(piece * TILE, (piece + 1) * TILE)
        if shares:
            for copy in big_dp[2 * piece] + big_dp[2 * piece + 1]:
                copy.wait_recv()

        def perceptron(slot, carry):
            pre = dot_nt(a2[slot], up_w[units, :]) + norm_ref[4:5, units]
            below = 0.5 * (1.0 + lax.erf(pre * math.sqrt(0.5)))
            h[slot, :, units] = (pre * below).astype(BF)
            density = jnp.exp(-0.5 * pre * pre) * (1.0 / math.sqrt(2.0 * math.pi))
            grad = dot_nt(cg[slot], down_w[units, :]) * (below + pre * density)
            grad = grad.astype(BF)
            dh[slot, :, units] = grad
            ub_grad[0:1, units] += jnp.sum(grad.astype(F32), 0, keepdims=True)
            return carry

        lax.fori_loop(0, 4, perceptron, 0)
        if piece == 0:
            for at in range(4, len(big_swaps)):
                big_arrives(at)
        if shares and piece >= 2:
            sum_arrives(piece - 2)
            sum_arrives(pieces + piece - 2)
        for at, left, right in ((piece, dh, a2), (pieces + piece, h, cg)):
            span = pl.ds(at * TILE, TILE)
            total = 0.0
            for slot in range(4):
                total = total + dot_tn(left[slot, :, units], right[slot])
            if shares:
                tmp[...] = total
                g_send[span, :] = tmp[:, other].astype(BF)
                sums[at] = copies.remote(g_send.at[span], g_recv.at[span], place.dp_peers[0])
                big_own[span, :] = tmp[:, own_part]
                homes[at] = copies.homeward(g_send.at[span], big_land.at[span], place.swap)
            else:
                big_own[span, :] = total
    copies.sends = [
        copy for copy in copies.sends if not any(copy is other for other in sums.values())
    ]
    leaving = [copies.local(held, out) for held, out in zip(kept, kept_outs)]

    def branches(slot):
        tokens = pl.ds(slot * local, local)
        return dot(h[slot], down_w[...]) + dot_tn(ot[:, tokens], small[query_width:, :])

    y_cores = {}
    for slot in (3, 2):
        at = slot - 2
        a2[at] = branches(slot).astype(BF)
        y_cores[at] = copies.remote(a2.at[at], y_from.at[at], place.core)
    branch = branches(1)
    y_cores[1].wait_recv()
    a2[2] = (branch + y_from[1].astype(F32)).astype(BF)
    y_next = copies.remote(a2.at[2], y_got, place.next)
    branch = branches(0)
    y_cores[0].wait_recv()
    y_keep[...] = branch + y_from[0].astype(F32)
    later = []
    if shares:
        for place_of, piece in (((0, 3), pieces - 2), ((0, 7), pieces - 1)):
            later += [(place_of, sum_arrives, at) for at in (piece, pieces + piece)]

    dk[...] = jnp.zeros_like(dk)
    dv[...] = jnp.zeros_like(dv)

    def backward_head(head, carry):
        own = pl.ds(pl.multiple_of(head * HS, HS), HS)
        for query in range(tiles):
            hooks(head, query, later)
            at_q = pl.ds(tile_at(query), TILE)
            q, do = (qt[own, at_q], dot_rows[own, at_q])
            scaled = do * jnp.asarray(1.0 / math.sqrt(HS), BF)
            log_total = l_ref[head, 0:1, at_q]
            inner = jnp.zeros((1, TILE), F32)
            for key in range(query + 1):
                at_k = pl.ds(tile_at(key), TILE)
                at_s = pl.ds(key * TILE, TILE)
                softmax = jnp.exp(masked(dot(k[at_k, :], q), key, query) - log_total)
                prob_grad = dot(v[at_k, :], scaled)
                s_ref[at_s, :] = softmax
                d_ref[at_s, :] = prob_grad
                inner = inner + jnp.sum(softmax * prob_grad, 0, keepdims=True)
            query_grad = jnp.zeros((HS, TILE), F32)
            for key in range(query + 1):
                at_k = pl.ds(tile_at(key), TILE)
                at_s = pl.ds(key * TILE, TILE)
                softmax = s_ref[at_s, :]
                score_grad = (softmax * (d_ref[at_s, :] - inner)).astype(BF)
                query_grad = query_grad + dot(kt[:, at_k], score_grad)
                dk[at_k, :] += dot_nt(score_grad, q)
                dv[at_k, :] += dot_nt(softmax.astype(BF), do)
            table = pl.ds(query * TILE, TILE)
            dqt[own, at_q] = rotate(query_grad, cos_ref[:, table], -sin_ref[:, table]).astype(BF)
        return carry

    lax.fori_loop(0, heads, backward_head, 0)
    for slot in range(4):
        block = at_slot(slot, rank)
        table = pl.ds(pl.multiple_of(block * local, local), local)
        tokens = pl.ds(slot * local, local)
        key_grad = dk[tokens, :].T * math.sqrt(HS)
        pair_grad[0:HS, tokens] = rotate(key_grad, cos_ref[:, table], -sin_ref[:, table])
        pair_grad[HS:, tokens] = dv[tokens, :].T

    y_next.wait_recv()
    y_sum[...] = (y_keep[...] + y_got[...].astype(F32)).astype(BF)
    for copy in leaving:
        copy.wait()

    @pl.when(place.is_swapped)
    def _():
        for at, copy in homes.items():
            copy.wait_send()
            copy.wait_recv()
            span = pl.ds(at * TILE, TILE)
            big_own[span, :] = big_land[span, :].astype(F32)

    copies.finish()


def first_pass(dp_size, x, c, entry, leave, shared, ids, vector, cosine, sine):
    local = x.shape[0]
    length = 4 * local
    part, columns = entry.shape
    query_width = HEADS * HS // 4
    width = 2 * query_width
    wide = part - query_width
    heads = query_width // HS
    gathers_pair = shared.shape[0] != D
    shares = columns != D
    held = (2 * wide if shares else 16, columns)
    tokens = ((4, local, D), BF)
    hidden = ((4, local, wide), BF)
    outs = [
        tokens,
        tokens,
        tokens,
        hidden,
        ((wide, D), BF),
        ((width, D), BF),
        ((dp_size, 4, shared.shape[0], 2 * HS) if gathers_pair else (D, 2 * HS), BF),
        ((query_width, length), BF),
        ((query_width, length), BF),
        ((2 * HS, length), F32),
        ((8, D), F32),
        ((8, wide), F32),
        ((2 * wide, columns), F32),
        ((local, D), BF),
    ]
    vmem = pl.BlockSpec(memory_space=pltpu.VMEM)
    copies = 64 + 12 * dp_size
    work = query_width * length * length
    return pl.pallas_call(
        functools.partial(first_kernel, dp_size),
        out_shape=[jax.ShapeDtypeStruct(shape, kind) for shape, kind in outs],
        in_specs=[pl.BlockSpec(memory_space=pl.ANY)] * 4 + [vmem] * 5,
        out_specs=[pl.BlockSpec(memory_space=pl.ANY)] * 8 + [vmem] * (len(outs) - 8),
        scratch_shapes=[pltpu.VMEM(shape, kind) for shape, kind in outs[:8]]
        + [
            pltpu.VMEM(hidden[0], BF),
            pltpu.VMEM((wide, D), BF),
            pltpu.VMEM((width, columns), BF),
            pltpu.VMEM((wide, columns), BF),
            pltpu.VMEM((wide, columns), BF),
            pltpu.VMEM((shared.shape[0] if gathers_pair else 16, 2 * HS), BF),
            pltpu.VMEM(vector.shape, F32),
            pltpu.VMEM((query_width, 1), F32),
            pltpu.VMEM((2 * HS, 1), F32),
            pltpu.VMEM(held, BF),
            pltpu.VMEM((4, local, D), BF),
            pltpu.VMEM((2 * HS, D), BF),
            pltpu.VMEM((query_width, length), BF),
            pltpu.VMEM((query_width, length), BF),
            pltpu.VMEM((HS, length), BF),
            pltpu.VMEM((HS, length), BF),
            pltpu.VMEM((length, HS), BF),
            pltpu.VMEM((length, HS), BF),
            pltpu.VMEM((length, HS), F32),
            pltpu.VMEM((length, HS), F32),
            pltpu.VMEM((length, TILE), F32),
            pltpu.VMEM((length, TILE), F32),
            pltpu.VMEM((heads, 8, length), F32),
            pltpu.VMEM((1, length), jnp.int32),
            pltpu.VMEM((TILE, D), F32),
            pltpu.VMEM((2, local, D), BF),
            pltpu.VMEM((local, D), BF),
            pltpu.VMEM((local, D), F32),
            pltpu.VMEM(held, BF),
            pltpu.VMEM(held, BF),
            pltpu.VMEM(entry.shape, entry.dtype),
            pltpu.VMEM(leave.shape, leave.dtype),
            pltpu.SemaphoreType.DMA((copies,)),
            pltpu.SemaphoreType.DMA((copies,)),
        ],
        compiler_params=pltpu.CompilerParams(
            collective_id=0, has_side_effects=True, vmem_limit_bytes=59 << 20
        ),
        cost_estimate=pl.CostEstimate(
            flops=60 * work, bytes_accessed=30 << 20, transcendentals=work // HS
        ),
        name="gather_attend",
    )(x, c, entry, leave, shared, ids, vector, cosine, sine)


def column_sum(rows):
    return jnp.sum(rows, 0, keepdims=True)


def row_of(column):
    size = column.shape[0]
    down = lax.broadcasted_iota(jnp.int32, (size, size), 0)
    along = lax.broadcasted_iota(jnp.int32, (size, size), 1)
    return column_sum(jnp.where(down == along, column, 0.0))


def as_row(array):
    return array.reshape(1, -1) if array.ndim == 1 else array


def gap_of(grad, weight, first, second, anchor, rate, decay):
    return anchor - adamw_update(weight, first, second, grad, rate, decay)[2]


def second_kernel(dp_size, sums_pair, shares, *refs):
    refs = iter(refs)

    def take(number):
        return [next(refs) for _ in range(number)]

    late = take(3)
    xg_far, dh_far, ot_far = take(3)
    if shares:
        entry, leave = (take(4), take(4))
    y_sum, up_w, small, kvw, dqt, pair_grad, norm_ref, ub_grad = take(8)
    if shares:
        shared, vector = (take(4) for _ in range(2))
    u_land, y_land, small_own, vector_row, shared_home, pair_parts = take(6)
    if shares:
        entry_sum, exit_sum, shared_sum, vector_sum = take(4)
    small_land, vector_home, stats, v_next, v_core, v_dp, s_core, s_next, s_dp = take(9)
    part_core, part_from = take(2)
    u_next, u_got, u_keep, u_home = take(4)
    p_from, p_next, p_got, full, g_send, g_recv = take(6)
    if shares:
        wide_buffers = [take(4), take(4)]
        small_buffers = [take(4), take(4)]
        shared_buffers, vector_buffers = (take(4), take(4))
        wide_held = take(4)
        small_held = [take(4), take(4)]
    cg, a1, big_g = take(3)
    xg, dh, ot = take(3)
    send, receive = take(2)

    place = Place(dp_size)
    copies = Copies(send, receive)
    local = xg.shape[1]
    wide = dh.shape[2]
    columns = small_own.shape[1]
    query_width = ot.shape[0]
    place.meet([place.across])
    slot_loads = {
        slot: [
            copies.local(far.at[slot], near.at[slot]) for far, near in ((dh_far, dh), (xg_far, xg))
        ]
        for slot in (3, 2, 1, 0)
    }
    loads = [copies.local(source, target) for source, target in zip(late, (cg, a1, big_g))]
    ot_load = copies.local(ot_far, ot)
    if shares:
        rest = pl.ds(query_width, wide)
        first_rows = pl.ds(0, query_width)
        wide_loads = [copies.local(ref.at[rest], to) for ref, to in zip(entry, wide_held)]
        small_loads = [
            copies.local(ref.at[first_rows], to)
            for olds, tos in zip((entry, leave), small_held)
            for ref, to in zip(olds, tos)
        ]
    def sent_home(source, target):
        return copies.swapped(source, target, place.is_swapped, place.swap)

    y_home = sent_home(y_sum, y_land)
    y_home[0]()
    pair_core = copies.remote(pair_grad.at[:, pl.ds(2 * local, 2 * local)], p_from, place.core)
    stats[...] = jnp.zeros_like(stats)

    def normal_of(slot):
        inputs = xg[slot].astype(F32)
        centered = inputs - jnp.mean(inputs, -1, keepdims=True)
        return centered * lax.rsqrt(jnp.mean(centered * centered, -1, keepdims=True) + NORM_EPS)

    def joined_of(slot):
        for copy in slot_loads[slot]:
            copy.wait()
        tokens = pl.ds(slot * local, local)
        first = dot_tn(dqt[:, tokens], small[:query_width, :])
        second = dot(dh[slot], up_w[...])
        normal = normal_of(slot)
        stats[0:1, :D] += column_sum(first * normal)
        stats[1:2, :D] += column_sum(first)
        stats[2:3, :D] += column_sum(second * normal)
        stats[3:4, :D] += column_sum(second)
        return first * norm_ref[0:1, :] + second * norm_ref[2:3, :]

    class GroupSum:
        def __init__(self, olds, grads, total, start, grad_start, size, buffers):
            self.olds, self.grads, self.total, self.buffers = (olds, grads, total, buffers)
            self.held = [pl.ds(pl.multiple_of(at * size, 8), size) for at in (place.half, 1 - place.half)]
            self.own, self.other = (
                pl.ds(pl.multiple_of(start + at * size, 8), size) for at in (place.half, 1 - place.half)
            )
            self.grad_own, self.grad_other = (
                pl.ds(pl.multiple_of(grad_start + at * size, 8), size)
                for at in (place.half, 1 - place.half)
            )

        def gap(self, at, grad_span):
            olds = (ref[self.held[at], :] for ref in self.olds)
            return gap_of(self.grads[grad_span, :], *olds, MATRIX_RATE, MATRIX_DECAY)

        def to_core(self):
            sent, got = self.buffers[:2]
            sent[...] = self.gap(1, self.grad_other)
            self.copy = copies.remote(sent, got, place.core)
            self.total[self.own, :] = self.gap(0, self.grad_own)

        def to_chip(self):
            self.copy.wait_recv()
            low, far = self.buffers[2:]
            low[...] = (self.total[self.own, :] + self.buffers[1][...]).astype(BF)
            self.copy = copies.remote(low, far, place.across)

        def back(self):
            self.copy.wait_recv()
            low, far = self.buffers[2:]
            self.total[self.own, :] = low[...].astype(F32) + far[...].astype(F32)
            part = self.total.at[self.own]
            self.copy = copies.remote(part, part, place.core)

    step = local // 2
    spans = [pl.ds(at * step, step) for at in range(2)]
    u_cores = {}
    for slot in (3, 2):
        at = slot - 2
        part_core[at] = joined_of(slot).astype(BF)
        u_cores[at] = copies.remote(part_core.at[at], part_from.at[at], place.core)
    pair_core.wait_recv()
    p_next[...] = pair_grad[:, local : 2 * local] + p_from[:, local:]
    pair_next = copies.remote(p_next, p_got, place.next)
    joined = joined_of(1)
    u_cores[1].wait_recv()
    u_next[...] = (joined + part_from[1].astype(F32)).astype(BF)
    u_nexts = [copies.remote(u_next.at[span], u_got.at[span], place.next) for span in spans]
    joined = joined_of(0)
    u_cores[0].wait_recv()
    joined = joined + part_from[0].astype(F32)
    pair_next.wait_recv()
    pair_sum = (pair_grad[:, :local] + p_from[:, :local] + p_got[...]).astype(BF)
    through_pair = dot_nt(pair_sum.T, kvw[...])
    u_keep[...] = joined + through_pair * norm_ref[0:1, :]
    u_homes = [sent_home(u_home.at[span], u_land.at[span]) for span in spans]

    def arrives(nexts, keep, got, home, homes, at):
        nexts[at].wait_recv()
        span = spans[at]
        home[span, :] = (keep[span, :] + got[span, :].astype(F32)).astype(BF)
        homes[at][0]()

    loads[0].wait()
    loads[1].wait()
    stats[0:1, :D] += column_sum(through_pair * normal_of(0))
    stats[1:2, :D] += column_sum(through_pair)
    stats[4:5, :D] = column_sum(cg[0].astype(F32))
    stats[5:6, : 2 * HS] = row_of(jnp.sum(pair_sum.astype(F32), 1, keepdims=True))
    tail = pl.ds(8 + place.rank, 1)
    stats[tail, :query_width] = row_of(jnp.sum(dqt[...].astype(F32), 1, keepdims=True))
    stats[tail, query_width : query_width + wide] = ub_grad[0:1, :]
    vector_core = copies.remote(stats, v_core, place.core)
    pair_parts[...] = dot(pair_sum, a1[0]).T.reshape(pair_parts.shape)
    if sums_pair:
        shared_core = copies.remote(pair_parts, s_core, place.core)

    ot_load.wait()
    turned = 0.0
    turned_out = 0.0
    for slot in range(4):
        tokens = pl.ds(slot * local, local)
        turned = turned + dot(dqt[:, tokens], a1[slot])
        turned_out = turned_out + dot(ot[:, tokens], cg[slot])
    if shares:
        full[:query_width, :] = turned
        full[query_width:, :] = turned_out
        other = pl.ds(pl.multiple_of((1 - place.dp) * columns, 128), columns)
        g_send[...] = full[:, other].astype(BF)
        small_sum = copies.remote(g_send, g_recv, place.dp_peers[0])
        small_home = copies.homeward(g_send, small_land, place.swap)
        small_own[...] = full[:, pl.ds(pl.multiple_of(place.dp * columns, 128), columns)]
    else:
        small_own[:query_width, :] = turned
        small_own[query_width:, :] = turned_out

    vector_core.wait_recv()
    copies.sent(vector_core)
    stats[...] = stats[...] + v_core[...]
    vector_next = copies.remote(stats, v_next, place.next)
    if sums_pair:
        shared_core.wait_recv()
        copies.sent(shared_core)
        pair_parts[...] = pair_parts[...] + s_core[...]
        shared_next = [
            copies.remote(pair_parts.at[at * 4 + flip_one(place.rank)], s_next.at[at], place.next)
            for at in range(dp_size)
        ]
    wide_sums, small_sums = ([], [])
    loads[2].wait()
    if shares:
        half = wide // 2
        for copy in wide_loads:
            copy.wait()
        wide_sums.append(
            GroupSum(wide_held, big_g, entry_sum, query_width, 0, half, wide_buffers[0])
        )
        wide_sums[0].to_core()
        wide_loads = [copies.local(ref.at[rest], to) for ref, to in zip(leave, wide_held)]

    if shares:
        wide_sums[0].to_chip()
        small_sum.wait_recv()
        copies.sent(small_sum)
        total = small_own[...] + g_recv[...].astype(F32)
        small_own[...] = total

        @pl.when(place.is_swapped)
        def _():
            g_send[...] = total.astype(BF)
            small_home.start()

    u_move = functools.partial(arrives, u_nexts, u_keep, u_got, u_home, u_homes)
    u_move(0)
    vector_next.wait_recv()
    copies.sent(vector_next)
    stats[...] = stats[...] + v_next[...]
    vector_dp = [
        copies.remote(stats, v_dp.at[at], peer) for at, peer in enumerate(place.dp_peers)
    ]
    if sums_pair:
        for at, copy in enumerate(shared_next):
            copy.wait_recv()
            s_next[at] = s_next[at] + pair_parts[at * 4 + place.rank]
        shared_dp = [
            copies.remote(s_next.at[(place.dp + at + 1) % dp_size], s_dp.at[at], peer)
            for at, peer in enumerate(place.dp_peers)
        ]
    u_move(1)
    for copy in vector_dp:
        copy.wait_recv()
        copies.sent(copy)
    total = stats[...]
    for at in range(dp_size - 1):
        total = total + v_dp[at]
    stats[...] = total
    late_homes = [sent_home(stats, vector_home)]
    if sums_pair:
        for copy in shared_dp:
            copy.wait_recv()
        total = s_next[place.dp]
        for at in range(dp_size - 1):
            total = total + s_dp[at]
        s_core[0] = total
        late_homes.append(sent_home(s_core.at[0], shared_home))
    for start, _ in late_homes:
        start()

    if shares:
        for copy in wide_loads:
            copy.wait()
        wide_sums.append(
            GroupSum(wide_held, big_g, exit_sum, query_width, wide, half, wide_buffers[1])
        )
        wide_sums[1].to_core()
        wide_sums[0].back()

        @pl.when(place.is_swapped)
        def _():
            small_home.wait_send()
            small_home.wait_recv()
            small_own[...] = small_land[...].astype(F32)

        wide_sums[1].to_chip()
        for copy in small_loads:
            copy.wait()
        size = query_width // 2
        for olds, start, total, buffers in (
            (small_held[0], 0, entry_sum, small_buffers[0]),
            (small_held[1], query_width, exit_sum, small_buffers[1]),
        ):
            small_sums.append(GroupSum(olds, small_own, total, 0, start, size, buffers))
            small_sums[-1].to_core()
        for part in small_sums:
            part.to_chip()

    for _, wait in late_homes:
        wait()
    part = query_width + wide
    rows = [vector_home[at : at + 1, :D] for at in (0, 1, 2, 3, 4, 4)]
    rows.append(vector_home[5:6, : 2 * HS])
    rows += [vector_home[8 + at : 9 + at, :part] for at in range(4)]
    vector_row[...] = jnp.concatenate(rows, 1)
    if shares:
        whole_sums = []
        for olds, grads, buffers, rate, decay in (
            (vector, vector_row, vector_buffers, VECTOR_RATE, 0.0),
            (shared, shared_home, shared_buffers, MATRIX_RATE, MATRIX_DECAY),
        ):
            buffers[0][...] = gap_of(grads[...], *(as_row(ref[...]) for ref in olds), rate, decay)
            whole_sums.append(copies.remote(buffers[0], buffers[1], place.core))
        for at, buffers in enumerate((vector_buffers, shared_buffers)):
            whole_sums[at].wait_recv()
            buffers[2][...] = buffers[0][...] + buffers[1][...]
            whole_sums[at] = copies.remote(buffers[2], buffers[3], place.across)
    if shares:
        for part in wide_sums[1:] + small_sums:
            part.back()
        for copy, buffers, total in (
            (whole_sums[0], vector_buffers, vector_sum),
            (whole_sums[1], shared_buffers, shared_sum),
        ):
            copy.wait_recv()
            total[...] = buffers[2][...] + buffers[3][...]
        for part in wide_sums + small_sums:
            part.copy.wait_recv()
    for _, wait in u_homes + [y_home]:
        wait()
    copies.finish()


def second_pass(dp_size, late, arrays, olds, piece):
    up_w, small = arrays[1:3]
    local = arrays[0].shape[0]
    width = small.shape[0]
    query_width = width // 2
    wide = up_w.shape[0]
    shares = len(olds) > 0
    columns = olds[0].shape[1] if shares else D
    sums_pair = piece % 16 == 0
    held = (width if shares else 16, columns)
    parts = (4 * dp_size, piece, 2 * HS) if sums_pair else (1, D, 2 * HS)
    own = (piece if sums_pair else 8, 2 * HS)
    vector = (1, 6 * D + 2 * HS + 4 * (query_width + wide))
    outs = [((local, D), BF)] * 2
    outs += [(shape, F32) for shape in ((width, columns), vector, own, parts)]
    scratch = [
        (held, BF),
        ((16, 1024), F32),
        ((16, 1024), F32),
        ((16, 1024), F32),
        ((16, 1024), F32),
        ((dp_size - 1, 16, 1024), F32),
        (parts, F32),
        ((dp_size,) + own, F32),
        ((dp_size - 1,) + own, F32),
        ((2, local, D), BF),
        ((2, local, D), BF),
        ((local, D), BF),
        ((local, D), BF),
        ((local, D), F32),
        ((local, D), BF),
        ((2 * HS, 2 * local), F32),
        ((2 * HS, local), F32),
        ((2 * HS, local), F32),
        ((width, D), F32),
        (held, BF),
        (held, BF),
    ]
    if shares:
        outs += [(shape, F32) for shape in (olds[0].shape, olds[4].shape, own, vector)]
        for size in (wide // 2, wide // 2, query_width // 2, query_width // 2):
            scratch += [((size, columns), kind) for kind in (F32, F32, BF, BF)]
        scratch += [(own, F32)] * 4 + [(vector, F32)] * 4
        scratch += [((wide, columns), F32)] * 4 + [((query_width, columns), F32)] * 8
    scratch += [(array.shape, array.dtype) for array in late]
    late = list(late) + list(olds[:8])
    arrays = late + list(arrays) + list(olds[8:])
    vmem = pl.BlockSpec(memory_space=pltpu.VMEM)
    work = 4 * local * D * D
    semaphores = pltpu.SemaphoreType.DMA((80 + 3 * dp_size,))
    return pl.pallas_call(
        functools.partial(second_kernel, dp_size, sums_pair, shares),
        out_shape=[jax.ShapeDtypeStruct(shape, kind) for shape, kind in outs],
        in_specs=[pl.BlockSpec(memory_space=pl.ANY)] * len(late) + [vmem] * (len(arrays) - len(late)),
        out_specs=[vmem] * len(outs),
        scratch_shapes=[pltpu.VMEM(shape, kind) for shape, kind in scratch]
        + [semaphores, semaphores],
        compiler_params=pltpu.CompilerParams(
            collective_id=1, has_side_effects=True, vmem_limit_bytes=60 << 20
        ),
        cost_estimate=pl.CostEstimate(flops=8 * work, bytes_accessed=30 << 20, transcendentals=0),
        name="sum_branches",
    )(*arrays)


def third_kernel(groups, *refs):
    refs = iter(refs)

    def take(number):
        return [next(refs) for _ in range(number)]

    x_ref, c_ref, u_ref, y_ref, bias_ref = take(5)
    grads = [take(2), take(2), take(1), take(1)]
    olds = [take(6) for _ in range(4)]
    out_ref, grad_ref = take(2)
    news = [take(6) for _ in range(4)]
    step = pl.program_id(0)

    @pl.when(step < 4)
    def _():
        inputs = x_ref[...].astype(F32)
        centered = inputs - jnp.mean(inputs, -1, keepdims=True)
        scale = lax.rsqrt(jnp.mean(centered * centered, -1, keepdims=True) + NORM_EPS)
        normal = centered * scale
        joined = u_ref[...].astype(F32)
        grad_ref[...] = c_ref[...].astype(F32) + scale * (
            joined
            - jnp.mean(joined, -1, keepdims=True)
            - normal * jnp.mean(joined * normal, -1, keepdims=True)
        )
        bias = bias_ref[:, 4 * D : 5 * D] + bias_ref[:, 5 * D : 6 * D]
        out_ref[...] = inputs + y_ref[...].astype(F32) + bias

    def update(at, grad, rate, decay):
        weight, first, second, anchor, velocity, total = (as_row(ref[...]) for ref in olds[at])
        first, second, weight = adamw_update(weight, first, second, grad, rate, decay)
        change = total / groups
        momentum = OUTER_BETA * velocity + change
        outer = anchor - OUTER_RATE * (change + OUTER_BETA * momentum)
        for ref, value in zip(news[at], (first, second, weight, change, momentum, outer)):
            ref[...] = value.reshape(ref.shape)

    for at in range(2):
        head, rest = grads[at]
        update(at, jnp.where(step == 0, head[...], rest[...]), MATRIX_RATE, MATRIX_DECAY)

    @pl.when(step == 0)
    def _():
        update(2, grads[2][0][...], MATRIX_RATE, MATRIX_DECAY)
        update(3, grads[3][0][...], VECTOR_RATE, 0.0)


def third_pass(groups, x, c, u, y, big, small, shared_grad, vector_grad, entry, leave, shared, vector):
    rows, columns = entry[0].shape
    size = small.shape[0] // 2
    wide = rows // size - 1

    def block(index):
        return pl.BlockSpec((size, columns), index)

    def all_of(array):
        return pl.BlockSpec(array.shape, lambda i: (0,) * array.ndim)

    here = block(lambda i: (i, 0))
    tokens = pl.BlockSpec((x.shape[0] // 4, D), lambda i: (jnp.minimum(i, 3), 0))
    grad_specs = [
        block(lambda i: (0, 0)),
        block(lambda i: (jnp.maximum(i - 1, 0), 0)),
        block(lambda i: (1, 0)),
        block(lambda i: (wide + jnp.maximum(i - 1, 0), 0)),
        all_of(shared_grad),
        all_of(vector_grad),
    ]
    specs = [here] * 12 + [all_of(array) for array in shared + vector]
    out_specs = [tokens] * 2 + [here] * 12 + [all_of(shared[0])] * 6 + [all_of(vector[0])] * 3
    out_specs += [all_of(vector[3])] * 3
    outs = [x, x] + [array for array in (entry[0], leave[0], shared[0]) for _ in range(6)]
    outs += [vector[0]] * 3 + [vector[3]] * 3
    return pl.pallas_call(
        functools.partial(third_kernel, groups),
        grid=(rows // size,),
        out_shape=[jax.ShapeDtypeStruct(array.shape, F32) for array in outs],
        in_specs=[tokens] * 4 + [all_of(vector[0])] + grad_specs + specs,
        out_specs=out_specs,
        compiler_params=pltpu.CompilerParams(vmem_limit_bytes=60 << 20),
        cost_estimate=pl.CostEstimate(flops=1 << 26, bytes_accessed=40 << 20, transcendentals=1 << 20),
        name="update_weights",
    )(x, c, u, y, vector[0], small, big, small, big, shared_grad, vector_grad, *entry, *leave, *shared, *vector)


def shards(
    hidden_in,
    doc_ids,
    out_cotangent,
    entry_weight,
    entry_first,
    entry_second,
    entry_anchor,
    entry_velocity,
    exit_weight,
    exit_first,
    exit_second,
    exit_anchor,
    exit_velocity,
    shared_weight,
    shared_first,
    shared_second,
    shared_anchor,
    shared_velocity,
    vector_weight,
    vector_first,
    vector_second,
    vector_anchor,
    vector_velocity,
):
    batch, local_len = hidden_in.shape[:2]
    parts = lax.axis_size("mp")
    group, rank = (lax.axis_index("group"), lax.axis_index("mp"))
    is_swapped = (group % 2) != (rank // 2)
    rank = jnp.where(is_swapped, jnp.bitwise_xor(rank, 2), rank)
    length = local_len * parts
    part_width = entry_weight.shape[2]
    query_width = HEADS * HS // parts
    heads = query_width // HS

    dp_size = lax.axis_size("dp")
    groups = lax.axis_size("group")
    order = jnp.bitwise_xor(jnp.arange(parts), rank)
    piece = shared_weight.shape[1]
    shared_piece = shared_weight[0]
    if piece % 16:
        pieces = gather_square(swapped_parts(shared_piece.astype(BF)))
        pieces = jnp.take(pieces, order, axis=0)
        shared_piece = gather_dp(pieces.reshape(-1, 2 * HS), 0)
    half = ROT // 2
    frequency = 10000.0 ** (-(np.arange(half) * 2.0 / ROT))
    angles = frequency.astype(np.float32)[:, None] * np.arange(length, dtype=np.float32)[None, :]
    cosine_table = jnp.asarray(np.cos(angles.astype(np.float64)).astype(np.float32))
    sine_table = jnp.asarray(np.sin(angles.astype(np.float64)).astype(np.float32))
    entry = [array[0].T for array in (entry_weight, entry_first, entry_second)]
    entry += [array.T for array in (entry_anchor, entry_velocity)]
    leave = [array[0] for array in (exit_weight, exit_first, exit_second)]
    leave += [exit_anchor, exit_velocity]
    shared = [array[0] for array in (shared_weight, shared_first, shared_second)]
    shared += [shared_anchor, shared_velocity]
    vector = [vector_weight, vector_first, vector_second, vector_anchor, vector_velocity]
    shares = dp_size == 2 and leave[0].shape[1] % 128 == 0 and piece % 16 == 0
    weights = [entry[0], leave[0]]
    if not shares:
        weights = [gather_dp(swapped_parts(array.astype(BF)), 1) for array in weights]
    (
        inputs, cots, attn_input, hidden_grad, up_w, small, pair_weight, attended,
        query_grad, pair_rows, norms, up_bias_rows, big_grad, branch,
    ) = first_pass(
        dp_size,
        hidden_in[0],
        out_cotangent[0],
        *weights,
        shared_piece,
        doc_ids,
        vector_weight,
        cosine_table,
        sine_table,
    )
    arrays = (
        branch, up_w, small, pair_weight.reshape(D, 2 * HS), query_grad,
        pair_rows, norms, up_bias_rows,
    )
    olds = [array for arrays in (entry, leave, shared, vector) for array in arrays[:4]]
    joined, branch, small_grad, vector_grad, shared_grad, pair_parts, *totals = second_pass(
        dp_size, (cots, attn_input, big_grad, inputs, hidden_grad, attended), arrays, olds if shares else [], piece
    )
    if not shares:
        big_grad, small_grad = (
            swapped_parts(scatter_dp(array, 1, F32)) for array in (big_grad, small_grad)
        )
        if piece % 16:
            grad_pieces = pair_parts.reshape(dp_size, parts, -1, 2 * HS)
            grad_pieces = jnp.take(grad_pieces, order, axis=1).swapaxes(0, 1)
            shared_grad = scatter_dp(scatter_square(grad_pieces, F32), 0, F32)
            shared_grad = swapped_parts(shared_grad.reshape(-1, 2 * HS))
        size, wide = (small_grad.shape[0] // 2, big_grad.shape[0] // 2)
        gaps = (
            gap_of(
                jnp.concatenate([small_grad[:size], big_grad[:wide]]),
                *entry[:4], MATRIX_RATE, MATRIX_DECAY,
            ),
            gap_of(
                jnp.concatenate([small_grad[size:], big_grad[wide:]]),
                *leave[:4], MATRIX_RATE, MATRIX_DECAY,
            ),
            gap_of(shared_grad, *shared[:4], MATRIX_RATE, MATRIX_DECAY),
            gap_of(vector_grad, *vector[:3], vector_anchor[None], VECTOR_RATE, 0.0),
        )
        totals = lax.psum(gaps, "group")
    block_output, input_grad, *updated = third_pass(
        groups, hidden_in[0], out_cotangent[0], joined, branch, big_grad, small_grad, shared_grad, vector_grad,
        *(arrays + [total] for arrays, total in zip((entry, leave, shared, vector), totals)),
    )
    results = [block_output[None], input_grad[None]]
    for at in range(3):
        own = updated[6 * at : 6 * at + 6]
        if at == 0:
            own = [array.T for array in own]
        results += [array[None] for array in own[:3]] + own[3:]
    results += updated[18:24]
    return tuple(results)


def solution(mesh):
    in_specs = (
        P(("group", "dp"), "mp", None),
        P(("group", "dp"), "mp"),
        P(("group", "dp"), "mp", None),
        P("group", "dp", "mp"),
        P("group", "dp", "mp"),
        P("group", "dp", "mp"),
        P("dp", "mp"),
        P("dp", "mp"),
        P("group", "mp", "dp"),
        P("group", "mp", "dp"),
        P("group", "mp", "dp"),
        P("mp", "dp"),
        P("mp", "dp"),
        P("group", ("dp", "mp"), None),
        P("group", ("dp", "mp"), None),
        P("group", ("dp", "mp"), None),
        P(("dp", "mp"), None),
        P(("dp", "mp"), None),
        P("group", None),
        P("group", None),
        P("group", None),
        P(),
        P(),
    )
    out_specs = (
        P(("group", "dp"), "mp", None),
        P(("group", "dp"), "mp", None),
        P("group", "dp", "mp"),
        P("group", "dp", "mp"),
        P("group", "dp", "mp"),
        P("dp", "mp"),
        P("dp", "mp"),
        P("dp", "mp"),
        P("group", "mp", "dp"),
        P("group", "mp", "dp"),
        P("group", "mp", "dp"),
        P("mp", "dp"),
        P("mp", "dp"),
        P("mp", "dp"),
        P("group", ("dp", "mp"), None),
        P("group", ("dp", "mp"), None),
        P("group", ("dp", "mp"), None),
        P(("dp", "mp"), None),
        P(("dp", "mp"), None),
        P(("dp", "mp"), None),
        P("group", None),
        P("group", None),
        P("group", None),
        P(),
        P(),
        P(),
    )
    return jax.shard_map(shards, mesh=mesh, in_specs=in_specs, out_specs=out_specs, check_vma=False)
```

```python
import functools
import math

import jax
import jax.numpy as jnp
import numpy as np
from jax import lax
from jax.experimental import pallas as pl
from jax.experimental.pallas import tpu as pltpu
from jax.sharding import PartitionSpec as P

D = 768
HEADS = 12
HS = 64
ROT = 16
STEP = 5
IN_COLS = 3840


NORM_EPS = 1e-05
BETA_ONE = 0.9
BETA_TWO = 0.95
ADAM_EPS = 1e-08
MATRIX_RATE = 0.03
MATRIX_DECAY = 0.1
VECTOR_RATE = 0.3
OUTER_RATE = 0.7
OUTER_BETA = 0.9

TILE = 256
F32 = jnp.float32
BF = jnp.bfloat16


def dot(left, right):
    return jnp.dot(left, right, preferred_element_type=F32)


def dot_nt(left, right):
    return lax.dot_general(left, right, (((1,), (1,)), ((), ())), preferred_element_type=F32)


def dot_tn(left, right):
    return lax.dot_general(left, right, (((0,), (0,)), ((), ())), preferred_element_type=F32)


def adamw_update(weight, first, second, gradient, step_rate, decay):
    first_new = BETA_ONE * first + (1.0 - BETA_ONE) * gradient
    second_new = BETA_TWO * second + (1.0 - BETA_TWO) * gradient * gradient
    fix_first = 1.0 - BETA_ONE**STEP
    fix_second = 1.0 - BETA_TWO**STEP
    update = first_new / fix_first / (jnp.sqrt(second_new / fix_second) + ADAM_EPS)
    return (first_new, second_new, weight - step_rate * (update + decay * weight))


def pairs_of(size, bit):
    return [(at, at ^ bit) for at in range(size)]


def over_core(array):
    return lax.ppermute(array, "group", pairs_of(lax.axis_size("group"), 1))


def over_next(array):
    return lax.ppermute(array, "mp", pairs_of(lax.axis_size("mp"), 1))


def over_dp(array):
    return lax.ppermute(array, "dp", pairs_of(2, 1))


def swapped_parts(array):
    parts = lax.axis_size("mp")
    pairs = []
    for group in range(lax.axis_size("group")):
        for rank in range(parts):
            here = group * parts + rank
            there = (group ^ 1) * parts + (rank ^ 2)
            pairs.append((here, there if group % 2 != rank // 2 else here))
    return lax.ppermute(array, ("group", "mp"), pairs)


def gather_square(own):
    pair = jnp.stack([own, over_next(own)])
    return jnp.concatenate([pair, over_core(pair)], 0)


def scatter_square(slots, send_type):
    pair = slots[:2] + over_core(slots[2:].astype(send_type)).astype(F32)
    return pair[0] + over_next(pair[1].astype(send_type)).astype(F32)


def gather_dp(own, axis):
    if lax.axis_size("dp") == 2:
        other = over_dp(own)
        first = lax.axis_index("dp") == 0
        return jnp.concatenate(
            [jnp.where(first, own, other), jnp.where(first, other, own)], axis
        )
    return lax.all_gather(own, "dp", axis=axis, tiled=True)


def scatter_dp(array, axis, send_type):
    if lax.axis_size("dp") == 2:
        size = array.shape[axis] // 2
        mine = lax.axis_index("dp")
        kept = lax.dynamic_slice_in_dim(array, mine * size, size, axis)
        sent = lax.dynamic_slice_in_dim(array, (1 - mine) * size, size, axis)
        return kept + over_dp(sent.astype(send_type)).astype(F32)
    return lax.psum_scatter(array, "dp", scatter_dimension=axis, tiled=True)


def flip_one(index):
    return index + 1 - 2 * (index % 2)


def flip_two(index):
    return index + 2 - 4 * ((index // 2) % 2)


def at_slot(slot, rank):
    rank = flip_one(rank) if slot % 2 else rank
    return flip_two(rank) if slot // 2 else rank


class Copies:
    def __init__(self, send, receive):
        self.send, self.receive, self.used, self.sends = (send, receive, 0, [])

    def remote(self, source, target, device, starts=True):
        at = self.used
        self.used += 1
        copy = pltpu.make_async_remote_copy(
            src_ref=source,
            dst_ref=target,
            send_sem=self.send.at[at],
            recv_sem=self.receive.at[at],
            device_id=device,
            device_id_type=pl.DeviceIdType.MESH,
        )
        if starts:
            copy.start()
        self.sends.append(copy)
        return copy

    def swapped(self, source, target, is_swapped, device):
        at = self.used
        self.used += 1
        far = pltpu.make_async_remote_copy(
            src_ref=source,
            dst_ref=target,
            send_sem=self.send.at[at],
            recv_sem=self.receive.at[at],
            device_id=device,
            device_id_type=pl.DeviceIdType.MESH,
        )
        near = pltpu.make_async_copy(source, target, self.receive.at[at])

        def start():
            @pl.when(is_swapped)
            def _():
                far.start()

            @pl.when(jnp.logical_not(is_swapped))
            def _():
                near.start()

        def wait():
            @pl.when(is_swapped)
            def _():
                far.wait_send()
                far.wait_recv()

            @pl.when(jnp.logical_not(is_swapped))
            def _():
                near.wait()

        return (start, wait)

    def homeward(self, source, target, device):
        at = self.used
        self.used += 1
        return pltpu.make_async_remote_copy(
            src_ref=source,
            dst_ref=target,
            send_sem=self.send.at[at],
            recv_sem=self.receive.at[at],
            device_id=device,
            device_id_type=pl.DeviceIdType.MESH,
        )

    def local(self, source, target):
        at = self.used
        self.used += 1
        copy = pltpu.make_async_copy(source, target, self.receive.at[at])
        copy.start()
        return copy

    def sent(self, copy):
        copy.wait_send()
        self.sends = [other for other in self.sends if other is not copy]

    def finish(self):
        for copy in self.sends:
            copy.wait_send()


class Place:
    def __init__(self, dp_size):
        group, self.dp, home = (lax.axis_index("group"), lax.axis_index("dp"), lax.axis_index("mp"))
        core, upper = (group % 2, home // 2)
        self.is_swapped = core != upper
        self.home = home
        self.rank = jnp.where(self.is_swapped, flip_two(home), home)
        self.swap = {"group": flip_one(group), "mp": flip_two(home)}
        self.core = {"group": flip_one(group)}
        self.across = {"group": flip_two(group)}
        self.half = core
        self.next = {"mp": flip_one(home)}
        self.dp_peers = [{"dp": (self.dp + step) % dp_size} for step in range(1, dp_size)]

    def meet(self, others=()):
        barrier = pltpu.get_barrier_semaphore()
        peers = [self.core, self.next, self.swap] + self.dp_peers + list(others)
        for peer in peers:
            pl.semaphore_signal(
                barrier, inc=1, device_id=peer, device_id_type=pl.DeviceIdType.MESH
            )
        pl.semaphore_wait(barrier, len(peers))


def column_of(row):
    size = row.shape[1]
    down = lax.broadcasted_iota(jnp.int32, (size, size), 0)
    along = lax.broadcasted_iota(jnp.int32, (size, size), 1)
    return jnp.sum(jnp.where(down == along, row, 0.0), 1, keepdims=True)


def rotate(rows, cosine, sine):
    half = ROT // 2
    one, two = (rows[:half], rows[half:ROT])
    return jnp.concatenate(
        [one * cosine - two * sine, two * cosine + one * sine, rows[ROT:]], 0
    )


def first_kernel(
    dp_size, x_ref, c_ref, entry_far, exit_far, shared_ref, ids_ref, vector_ref, cos_ref, sin_ref,
    xg_out, cg_out, a1_out, dh_out, up_out, small_out, kvw_out, ot_out,
    dqt, pair_grad, norm_ref, ub_grad, big_own, y_sum,
    xg, cg, a1, dh, up_w, small, kvw, ot, h, down_w, small_ref, up_ref, down_ref, pair_ref, vector_other, qb_ref, kvb_ref, big_land, a2,
    kvt, qt, dot_rows, kt, vt, k, v, dk, dv, s_ref, d_ref, l_ref, idr, tmp,
    y_from, y_got, y_keep, g_send, g_recv, entry_ref, exit_ref, send, receive,
):
    place = Place(dp_size)
    rank, dp = (place.rank, place.dp)
    copies = Copies(send, receive)
    local = x_ref.shape[0]
    length = 4 * local
    columns = entry_ref.shape[1]
    shares = columns != D
    query_width = small.shape[0] // 2
    wide = up_w.shape[0]
    heads = query_width // HS
    gathers_pair = shared_ref.shape[0] != D
    kept = (xg, cg, a1, dh, up_w, small, kvw, ot)
    kept_outs = (xg_out, cg_out, a1_out, dh_out, up_out, small_out, kvw_out, ot_out)
    place.meet()
    vector_core = copies.remote(vector_ref, vector_other, place.core)
    weight_loads = [copies.local(entry_far, entry_ref), copies.local(exit_far, exit_ref)]

    def swapped(source, target):
        return copies.swapped(source, target, place.is_swapped, place.swap)

    def dp_part(ref, start, size):
        return ref.at[pl.ds(start, size), pl.ds(pl.multiple_of(dp * columns, 128), columns)]

    step = local // 2
    spans = [pl.ds(at * step, step) for at in range(2)]
    x_swaps = [swapped(x_ref.at[s], xg.at[0, s]) for s in spans]
    c_swaps = [swapped(c_ref.at[s], cg.at[0, s]) for s in spans]
    ids_swap = swapped(ids_ref, idr.at[:, pl.ds(0, local)])
    small_swaps, big_swaps, big_parts = ([], [], [])
    if shares:
        small_part = dp_part(small, 0, 2 * query_width)
        small_swaps = [swapped(small_ref, small_part)]
        for at in range(0, wide, TILE):
            for source, target in ((up_ref, up_w), (down_ref, down_w)):
                big_parts.append(dp_part(target, at, TILE))
                big_swaps.append(swapped(source.at[pl.ds(at, TILE)], big_parts[-1]))
    first = [ids_swap]
    if gathers_pair:
        pair_swap = swapped(pair_ref, kvw.at[dp, place.home])
        first.append(pair_swap)
    queue = iter([start for start, _ in x_swaps + small_swaps + c_swaps])

    def start_next():
        start = next(queue, None)
        if start is not None:
            start()

    start_next()
    start_next()
    if gathers_pair:
        pair_ref[...] = shared_ref[...].astype(BF)
    for start, _ in first:
        start()
    for copy in weight_loads:
        copy.wait()
    if shares:
        small_ref[:query_width, :] = entry_ref[:query_width, :].astype(BF)
        small_ref[query_width:, :] = exit_ref[:query_width, :].astype(BF)
        up_ref[...] = entry_ref[query_width:, :].astype(BF)
        down_ref[...] = exit_ref[query_width:, :].astype(BF)
    else:
        small[:query_width, :] = entry_ref[:query_width, :]
        small[query_width:, :] = exit_ref[:query_width, :]
        up_w[...] = entry_ref[query_width:, :]
        down_w[...] = exit_ref[query_width:, :]
    vector_core.wait_recv()

    def role_vector(start, size):
        span = slice(start, start + size)
        return jnp.where(place.is_swapped, vector_other[:, span], vector_ref[:, span])

    for at in range(4):
        norm_ref[at : at + 1, :] = role_vector(at * D, D)
    kvb_ref[...] = column_of(role_vector(6 * D, 2 * HS))
    part = query_width + wide
    tail = 6 * D + 2 * HS
    in_bias = role_vector(tail, part)
    for at in range(1, 4):
        in_bias = jnp.where(rank == at, role_vector(tail + at * part, part), in_bias)
    qb_ref[...] = column_of(in_bias[:, :query_width])
    norm_ref[4:5, :] = in_bias[:, query_width:]

    def normalise(slot):
        def body(at, carry):
            span = pl.ds(pl.multiple_of(at * 128, 128), 128)
            wide = xg[slot, span, :].astype(F32)
            centered = wide - jnp.mean(wide, -1, keepdims=True)
            normal = centered * lax.rsqrt(
                jnp.mean(centered * centered, -1, keepdims=True) + NORM_EPS
            )
            a1[slot, span, :] = (normal * norm_ref[0:1, :] + norm_ref[1:2, :]).astype(BF)
            a2[slot, span, :] = (normal * norm_ref[2:3, :] + norm_ref[3:4, :]).astype(BF)
            return carry

        lax.fori_loop(0, local // 128, body, 0)

    def lanes(ref, slot):
        return ref.at[:, pl.ds(slot * local, local)]

    x_next, x_core, x_far = ([], [], [])
    for span, (_, wait) in zip(spans, x_swaps):
        wait()
        start_next()
        x_next.append(copies.remote(xg.at[0, span], xg.at[1, span], place.next))
        x_core.append(copies.remote(xg.at[0, span], xg.at[2, span], place.core))
    small_dp = []
    for _, wait in small_swaps:
        wait()
        start_next()
        small_dp += [copies.remote(small_part, small_part, peer) for peer in place.dp_peers]
    ids_swap[1]()
    ids_next = copies.remote(lanes(idr, 0), lanes(idr, 1), place.next)
    ids_core = copies.remote(lanes(idr, 0), lanes(idr, 2), place.core)
    if gathers_pair:
        pair_swap[1]()
        own_pair = kvw.at[dp, rank]
        pair_next = copies.remote(own_pair, own_pair, place.next)
        pair_core = copies.remote(own_pair, own_pair, place.core)
    c_next, c_core, c_far, big_dp = ([], [], [], [])
    for span in spans:
        c_next.append(copies.remote(cg.at[0, span], cg.at[1, span], place.next, starts=False))
        c_core.append(copies.remote(cg.at[0, span], cg.at[2, span], place.core, starts=False))
        c_far.append(copies.remote(cg.at[1, span], cg.at[3, span], place.core, starts=False))
    for part in big_parts:
        big_dp.append([copies.remote(part, part, peer, starts=False) for peer in place.dp_peers])

    def c_sends(at):
        c_next[at].start()
        c_core[at].start()

    def c_arrives(at):
        @pl.when(place.is_swapped)
        def _():
            c_swaps[at][1]()
            c_sends(at)

        if at < len(big_swaps):
            big_swaps[at][0]()

    def c_passes(at):
        c_next[at].wait_recv()
        c_far[at].start()

    def big_arrives(at):
        big_swaps[at][1]()
        if at + 2 < len(big_swaps):
            big_swaps[at + 2][0]()
        for copy in big_dp[at]:
            copy.start()

    normalise(0)
    for span, copy in zip(spans, x_next):
        copy.wait_recv()
        x_far.append(copies.remote(xg.at[1, span], xg.at[3, span], place.core))
    for at in range(2):

        @pl.when(jnp.logical_not(place.is_swapped))
        def _():
            c_swaps[at][1]()
            c_sends(at)

    ids_next.wait_recv()
    ids_far = copies.remote(lanes(idr, 1), lanes(idr, 3), place.core)
    if gathers_pair:
        pair_next.wait_recv()
        next_pair = kvw.at[dp, flip_one(rank)]
        pair_far = copies.remote(next_pair, next_pair, place.core)
        pair_core.wait_recv()
        pair_far.wait_recv()
        pair_dp = [copies.remote(kvw.at[dp], kvw.at[dp], peer) for peer in place.dp_peers]
    events = [((0, 6), c_passes, 0), ((1, 5), c_passes, 1)]
    if shares:
        places = ((0, 5), (0, 7), (1, 6), (2, 3))
        events += [(place, big_arrives, at) for at, place in enumerate(places)]
    for copy in x_core:
        copy.wait_recv()
    normalise(2)
    normalise(1)
    for copy in x_far:
        copy.wait_recv()
    normalise(3)
    for copy in small_dp:
        copy.wait_recv()
    if gathers_pair:
        for copy in pair_dp:
            copy.wait_recv()
        kvt[...] = kvw[...].reshape(D, 2 * HS).T
    else:
        kvw[...] = shared_ref[...]
        kvt[...] = shared_ref[...].T
    c_arrives(0)
    for slot in range(4):
        block = at_slot(slot, rank)
        table = pl.ds(pl.multiple_of(block * local, local), local)
        cosine, sine = (cos_ref[:, table], sin_ref[:, table])
        tokens = pl.ds(slot * local, local)
        queries = dot_nt(small[0:query_width, :], a1[slot]) + qb_ref[...]
        for head in range(heads):
            turned = rotate(queries[head * HS : (head + 1) * HS], cosine, sine).astype(BF)
            qt[head * HS : (head + 1) * HS, tokens] = turned * jnp.asarray(1.0 / math.sqrt(HS), BF)
        pairs = dot_nt(kvt[...], a1[slot]) + kvb_ref[...]
        turned = rotate(pairs[:HS], cosine, sine).astype(BF)
        kt[:, tokens] = turned
        k[tokens, :] = turned.T
        value = pairs[HS:].astype(BF)
        vt[:, tokens] = value
        v[tokens, :] = value.T
    c_arrives(1)
    for copy in (ids_core, ids_far):
        copy.wait_recv()
    ids = idr[...].astype(F32)
    first_end = jnp.sum(jnp.where(ids < 0.5, 1.0, 0.0), 1, keepdims=True)
    second_end = jnp.sum(jnp.where(ids < 1.5, 1.0, 0.0), 1, keepdims=True)

    def document(position):
        position = position.astype(F32)
        return jnp.where(position < first_end, 0.0, jnp.where(position < second_end, 1.0, 2.0))

    tiles = length // TILE
    per = tiles // 4

    def tile_at(tile):
        return pl.multiple_of(at_slot(tile // per, rank) * local + (tile % per) * TILE, TILE)

    def masked(scores, key, query):
        edge = key == 0 or query == tiles - 1
        allowed = None
        if key == query:
            down = lax.broadcasted_iota(jnp.int32, (TILE, TILE), 0)
            allowed = down <= lax.broadcasted_iota(jnp.int32, (TILE, TILE), 1)
        if edge:
            down = document(lax.broadcasted_iota(jnp.int32, (TILE, 1), 0) + key * TILE)
            along = document(lax.broadcasted_iota(jnp.int32, (1, TILE), 1) + query * TILE)
            same = down == along
            allowed = same if allowed is None else allowed & same
        return scores if allowed is None else jnp.where(allowed, scores, -1e9)

    def hooks(head, query, todo):
        for (at_head, at_query), event, at in todo:
            if query == at_query:

                @pl.when(head == at_head)
                def _():
                    event(at)

    def forward_head(head, carry):
        own = pl.ds(pl.multiple_of(head * HS, HS), HS)
        for query in range(tiles):
            hooks(head, query, events)
            at_q = pl.ds(tile_at(query), TILE)
            q = qt[own, at_q]
            highest = jnp.full((1, TILE), -jnp.inf, F32)
            for key in range(query + 1):
                scores = masked(dot(k[pl.ds(tile_at(key), TILE), :], q), key, query)
                s_ref[pl.ds(key * TILE, TILE), :] = scores
                highest = jnp.maximum(highest, jnp.max(scores, 0, keepdims=True))
            total = jnp.zeros((1, TILE), F32)
            for key in range(query + 1):
                exponent = jnp.exp(s_ref[pl.ds(key * TILE, TILE), :] - highest)
                s_ref[pl.ds(key * TILE, TILE), :] = exponent
                total = total + jnp.sum(exponent, 0, keepdims=True)
            inverse = 1.0 / total
            mixed = jnp.zeros((HS, TILE), F32)
            for key in range(query + 1):
                softmax = (s_ref[pl.ds(key * TILE, TILE), :] * inverse).astype(BF)
                mixed = mixed + dot(vt[:, pl.ds(tile_at(key), TILE)], softmax)
            ot[own, at_q] = mixed.astype(BF)
            l_ref[head, :, at_q] = jnp.broadcast_to(highest + jnp.log(total), (8, TILE))
        return carry

    lax.fori_loop(0, heads, forward_head, 0)
    for copy in c_core + c_far:
        copy.wait_recv()
    ub_grad[...] = jnp.zeros_like(ub_grad)

    def attention_grad(slot, carry):
        tokens = pl.ds(pl.multiple_of(slot * local, local), local)
        dot_rows[:, tokens] = dot_nt(small[query_width:, :], cg[slot]).astype(BF)
        return carry

    lax.fori_loop(0, 4, attention_grad, 0)
    other = pl.ds(pl.multiple_of((1 - dp) * columns, 128), columns) if shares else None
    own_part = pl.ds(pl.multiple_of(dp * columns, 128), columns) if shares else None
    sums, homes = ({}, {})

    def sum_arrives(at):
        span = pl.ds(at * TILE, TILE)
        sums[at].wait_recv()
        sums[at].wait_send()
        total = big_own[span, :] + g_recv[span, :].astype(F32)
        big_own[span, :] = total

        @pl.when(place.is_swapped)
        def _():
            g_send[span, :] = total.astype(BF)
            homes[at].start()

    pieces = wide // TILE
    for piece in range(pieces):
        units = slice(piece * TILE, (piece + 1) * TILE)
        if shares:
            for copy in big_dp[2 * piece] + big_dp[2 * piece + 1]:
                copy.wait_recv()

        def perceptron(slot, carry):
            pre = dot_nt(a2[slot], up_w[units, :]) + norm_ref[4:5, units]
            below = 0.5 * (1.0 + lax.erf(pre * math.sqrt(0.5)))
            h[slot, :, units] = (pre * below).astype(BF)
            density = jnp.exp(-0.5 * pre * pre) * (1.0 / math.sqrt(2.0 * math.pi))
            grad = dot_nt(cg[slot], down_w[units, :]) * (below + pre * density)
            grad = grad.astype(BF)
            dh[slot, :, units] = grad
            ub_grad[0:1, units] += jnp.sum(grad.astype(F32), 0, keepdims=True)
            return carry

        lax.fori_loop(0, 4, perceptron, 0)
        if piece == 0:
            for at in range(4, len(big_swaps)):
                big_arrives(at)
        if shares and piece >= 2:
            sum_arrives(piece - 2)
            sum_arrives(pieces + piece - 2)
        for at, left, right in ((piece, dh, a2), (pieces + piece, h, cg)):
            span = pl.ds(at * TILE, TILE)
            total = 0.0
            for slot in range(4):
                total = total + dot_tn(left[slot, :, units], right[slot])
            if shares:
                tmp[...] = total
                g_send[span, :] = tmp[:, other].astype(BF)
                sums[at] = copies.remote(g_send.at[span], g_recv.at[span], place.dp_peers[0])
                big_own[span, :] = tmp[:, own_part]
                homes[at] = copies.homeward(g_send.at[span], big_land.at[span], place.swap)
            else:
                big_own[span, :] = total
    copies.sends = [
        copy for copy in copies.sends if not any(copy is other for other in sums.values())
    ]
    leaving = [copies.local(held, out) for held, out in zip(kept, kept_outs)]

    def branches(slot):
        tokens = pl.ds(slot * local, local)
        return dot(h[slot], down_w[...]) + dot_tn(ot[:, tokens], small[query_width:, :])

    y_cores = {}
    for slot in (3, 2):
        at = slot - 2
        a2[at] = branches(slot).astype(BF)
        y_cores[at] = copies.remote(a2.at[at], y_from.at[at], place.core)
    branch = branches(1)
    y_cores[1].wait_recv()
    a2[2] = (branch + y_from[1].astype(F32)).astype(BF)
    y_next = copies.remote(a2.at[2], y_got, place.next)
    if shares:
        sum_arrives(pieces - 2)
        sum_arrives(2 * pieces - 2)
    branch = branches(0)
    y_cores[0].wait_recv()
    y_keep[...] = branch + y_from[0].astype(F32)
    later = []
    if shares:
        for place_of, piece in (((0, 6), pieces - 1),):
            later += [(place_of, sum_arrives, at) for at in (piece, pieces + piece)]

    dk[...] = jnp.zeros_like(dk)
    dv[...] = jnp.zeros_like(dv)

    def backward_head(head, carry):
        own = pl.ds(pl.multiple_of(head * HS, HS), HS)
        for query in range(tiles):
            hooks(head, query, later)
            at_q = pl.ds(tile_at(query), TILE)
            q, do = (qt[own, at_q], dot_rows[own, at_q])
            scaled = do * jnp.asarray(1.0 / math.sqrt(HS), BF)
            log_total = l_ref[head, 0:1, at_q]
            inner = jnp.zeros((1, TILE), F32)
            for key in range(query + 1):
                at_k = pl.ds(tile_at(key), TILE)
                at_s = pl.ds(key * TILE, TILE)
                softmax = jnp.exp(masked(dot(k[at_k, :], q), key, query) - log_total)
                prob_grad = dot(v[at_k, :], scaled)
                s_ref[at_s, :] = softmax
                d_ref[at_s, :] = prob_grad
                inner = inner + jnp.sum(softmax * prob_grad, 0, keepdims=True)
            query_grad = jnp.zeros((HS, TILE), F32)
            for key in range(query + 1):
                at_k = pl.ds(tile_at(key), TILE)
                at_s = pl.ds(key * TILE, TILE)
                softmax = s_ref[at_s, :]
                score_grad = (softmax * (d_ref[at_s, :] - inner)).astype(BF)
                query_grad = query_grad + dot(kt[:, at_k], score_grad)
                dk[at_k, :] += dot_nt(score_grad, q)
                dv[at_k, :] += dot_nt(softmax.astype(BF), do)
            table = pl.ds(query * TILE, TILE)
            dqt[own, at_q] = rotate(query_grad, cos_ref[:, table], -sin_ref[:, table]).astype(BF)
        return carry

    lax.fori_loop(0, heads, backward_head, 0)
    for slot in range(4):
        block = at_slot(slot, rank)
        table = pl.ds(pl.multiple_of(block * local, local), local)
        tokens = pl.ds(slot * local, local)
        key_grad = dk[tokens, :].T * math.sqrt(HS)
        pair_grad[0:HS, tokens] = rotate(key_grad, cos_ref[:, table], -sin_ref[:, table])
        pair_grad[HS:, tokens] = dv[tokens, :].T

    y_next.wait_recv()
    y_sum[...] = (y_keep[...] + y_got[...].astype(F32)).astype(BF)
    for copy in leaving:
        copy.wait()

    @pl.when(place.is_swapped)
    def _():
        for at, copy in homes.items():
            copy.wait_send()
            copy.wait_recv()
            span = pl.ds(at * TILE, TILE)
            big_own[span, :] = big_land[span, :].astype(F32)

    copies.finish()


def first_pass(dp_size, x, c, entry, leave, shared, ids, vector, cosine, sine):
    local = x.shape[0]
    length = 4 * local
    part, columns = entry.shape
    query_width = HEADS * HS // 4
    width = 2 * query_width
    wide = part - query_width
    heads = query_width // HS
    gathers_pair = shared.shape[0] != D
    shares = columns != D
    held = (2 * wide if shares else 16, columns)
    tokens = ((4, local, D), BF)
    hidden = ((4, local, wide), BF)
    outs = [
        tokens,
        tokens,
        tokens,
        hidden,
        ((wide, D), BF),
        ((width, D), BF),
        ((dp_size, 4, shared.shape[0], 2 * HS) if gathers_pair else (D, 2 * HS), BF),
        ((query_width, length), BF),
        ((query_width, length), BF),
        ((2 * HS, length), F32),
        ((8, D), F32),
        ((8, wide), F32),
        ((2 * wide, columns), F32),
        ((local, D), BF),
    ]
    vmem = pl.BlockSpec(memory_space=pltpu.VMEM)
    copies = 64 + 12 * dp_size
    work = query_width * length * length
    return pl.pallas_call(
        functools.partial(first_kernel, dp_size),
        out_shape=[jax.ShapeDtypeStruct(shape, kind) for shape, kind in outs],
        in_specs=[pl.BlockSpec(memory_space=pl.ANY)] * 4 + [vmem] * 5,
        out_specs=[pl.BlockSpec(memory_space=pl.ANY)] * 8 + [vmem] * (len(outs) - 8),
        scratch_shapes=[pltpu.VMEM(shape, kind) for shape, kind in outs[:8]]
        + [
            pltpu.VMEM(hidden[0], BF),
            pltpu.VMEM((wide, D), BF),
            pltpu.VMEM((width, columns), BF),
            pltpu.VMEM((wide, columns), BF),
            pltpu.VMEM((wide, columns), BF),
            pltpu.VMEM((shared.shape[0] if gathers_pair else 16, 2 * HS), BF),
            pltpu.VMEM(vector.shape, F32),
            pltpu.VMEM((query_width, 1), F32),
            pltpu.VMEM((2 * HS, 1), F32),
            pltpu.VMEM(held, BF),
            pltpu.VMEM((4, local, D), BF),
            pltpu.VMEM((2 * HS, D), BF),
            pltpu.VMEM((query_width, length), BF),
            pltpu.VMEM((query_width, length), BF),
            pltpu.VMEM((HS, length), BF),
            pltpu.VMEM((HS, length), BF),
            pltpu.VMEM((length, HS), BF),
            pltpu.VMEM((length, HS), BF),
            pltpu.VMEM((length, HS), F32),
            pltpu.VMEM((length, HS), F32),
            pltpu.VMEM((length, TILE), F32),
            pltpu.VMEM((length, TILE), F32),
            pltpu.VMEM((heads, 8, length), F32),
            pltpu.VMEM((1, length), jnp.int32),
            pltpu.VMEM((TILE, D), F32),
            pltpu.VMEM((2, local, D), BF),
            pltpu.VMEM((local, D), BF),
            pltpu.VMEM((local, D), F32),
            pltpu.VMEM(held, BF),
            pltpu.VMEM(held, BF),
            pltpu.VMEM(entry.shape, entry.dtype),
            pltpu.VMEM(leave.shape, leave.dtype),
            pltpu.SemaphoreType.DMA((copies,)),
            pltpu.SemaphoreType.DMA((copies,)),
        ],
        compiler_params=pltpu.CompilerParams(
            collective_id=0, has_side_effects=True, vmem_limit_bytes=59 << 20
        ),
        cost_estimate=pl.CostEstimate(
            flops=60 * work, bytes_accessed=30 << 20, transcendentals=work // HS
        ),
        name="gather_attend",
    )(x, c, entry, leave, shared, ids, vector, cosine, sine)


def column_sum(rows):
    return jnp.sum(rows, 0, keepdims=True)


def row_of(column):
    size = column.shape[0]
    down = lax.broadcasted_iota(jnp.int32, (size, size), 0)
    along = lax.broadcasted_iota(jnp.int32, (size, size), 1)
    return column_sum(jnp.where(down == along, column, 0.0))


def as_row(array):
    return array.reshape(1, -1) if array.ndim == 1 else array


def gap_of(grad, weight, first, second, anchor, rate, decay):
    return anchor - adamw_update(weight, first, second, grad, rate, decay)[2]


def second_kernel(dp_size, sums_pair, shares, *refs):
    refs = iter(refs)

    def take(number):
        return [next(refs) for _ in range(number)]

    late = take(3)
    xg_far, dh_far, ot_far = take(3)
    if shares:
        entry, leave = (take(4), take(4))
    y_sum, up_w, small, kvw, dqt, pair_grad, norm_ref, ub_grad = take(8)
    if shares:
        shared, vector = (take(4) for _ in range(2))
    u_land, y_land, small_own, vector_row, shared_home, pair_parts = take(6)
    if shares:
        entry_sum, exit_sum, shared_sum, vector_sum = take(4)
    small_land, vector_home, stats, v_next, v_core, v_dp, s_core, s_next, s_dp = take(9)
    part_core, part_from = take(2)
    u_next, u_got, u_keep, u_home = take(4)
    p_from, p_next, p_got, full, g_send, g_recv = take(6)
    if shares:
        wide_buffers = [take(4), take(4)]
        small_buffers = [take(4), take(4)]
        shared_buffers, vector_buffers = (take(4), take(4))
        wide_held = take(4)
        small_held = [take(4), take(4)]
    cg, a1, big_g = take(3)
    xg, dh, ot = take(3)
    send, receive = take(2)

    place = Place(dp_size)
    copies = Copies(send, receive)
    local = xg.shape[1]
    wide = dh.shape[2]
    columns = small_own.shape[1]
    query_width = ot.shape[0]
    place.meet([place.across])
    slot_loads = {
        slot: [
            copies.local(far.at[slot], near.at[slot]) for far, near in ((dh_far, dh), (xg_far, xg))
        ]
        for slot in (3, 2, 1, 0)
    }
    loads = [copies.local(source, target) for source, target in zip(late, (cg, a1, big_g))]
    ot_load = copies.local(ot_far, ot)
    if shares:
        rest = pl.ds(query_width, wide)
        first_rows = pl.ds(0, query_width)
        wide_loads = [copies.local(ref.at[rest], to) for ref, to in zip(entry, wide_held)]
        small_loads = [
            copies.local(ref.at[first_rows], to)
            for olds, tos in zip((entry, leave), small_held)
            for ref, to in zip(olds, tos)
        ]
    def sent_home(source, target):
        return copies.swapped(source, target, place.is_swapped, place.swap)

    y_home = sent_home(y_sum, y_land)
    y_home[0]()
    pair_core = copies.remote(pair_grad.at[:, pl.ds(2 * local, 2 * local)], p_from, place.core)
    stats[...] = jnp.zeros_like(stats)

    def normal_of(slot):
        inputs = xg[slot].astype(F32)
        centered = inputs - jnp.mean(inputs, -1, keepdims=True)
        return centered * lax.rsqrt(jnp.mean(centered * centered, -1, keepdims=True) + NORM_EPS)

    def joined_of(slot):
        for copy in slot_loads[slot]:
            copy.wait()
        tokens = pl.ds(slot * local, local)
        first = dot_tn(dqt[:, tokens], small[:query_width, :])
        second = dot(dh[slot], up_w[...])
        normal = normal_of(slot)
        stats[0:1, :D] += column_sum(first * normal)
        stats[1:2, :D] += column_sum(first)
        stats[2:3, :D] += column_sum(second * normal)
        stats[3:4, :D] += column_sum(second)
        return first * norm_ref[0:1, :] + second * norm_ref[2:3, :]

    class GroupSum:
        def __init__(self, olds, grads, total, start, grad_start, size, buffers):
            self.olds, self.grads, self.total, self.buffers = (olds, grads, total, buffers)
            self.held = [pl.ds(pl.multiple_of(at * size, 8), size) for at in (place.half, 1 - place.half)]
            self.own, self.other = (
                pl.ds(pl.multiple_of(start + at * size, 8), size) for at in (place.half, 1 - place.half)
            )
            self.grad_own, self.grad_other = (
                pl.ds(pl.multiple_of(grad_start + at * size, 8), size)
                for at in (place.half, 1 - place.half)
            )

        def gap(self, at, grad_span):
            olds = (ref[self.held[at], :] for ref in self.olds)
            return gap_of(self.grads[grad_span, :], *olds, MATRIX_RATE, MATRIX_DECAY)

        def to_core(self):
            sent, got = self.buffers[:2]
            sent[...] = self.gap(1, self.grad_other)
            self.copy = copies.remote(sent, got, place.core)
            self.total[self.own, :] = self.gap(0, self.grad_own)

        def to_chip(self):
            self.copy.wait_recv()
            low, far = self.buffers[2:]
            low[...] = (self.total[self.own, :] + self.buffers[1][...]).astype(BF)
            self.copy = copies.remote(low, far, place.across)

        def back(self):
            self.copy.wait_recv()
            low, far = self.buffers[2:]
            self.total[self.own, :] = low[...].astype(F32) + far[...].astype(F32)
            part = self.total.at[self.own]
            self.copy = copies.remote(part, part, place.core)

    step = local // 2
    spans = [pl.ds(at * step, step) for at in range(2)]
    u_cores = {}
    for slot in (3, 2):
        at = slot - 2
        part_core[at] = joined_of(slot).astype(BF)
        u_cores[at] = copies.remote(part_core.at[at], part_from.at[at], place.core)
    pair_core.wait_recv()
    p_next[...] = pair_grad[:, local : 2 * local] + p_from[:, local:]
    pair_next = copies.remote(p_next, p_got, place.next)
    joined = joined_of(1)
    u_cores[1].wait_recv()
    u_next[...] = (joined + part_from[1].astype(F32)).astype(BF)
    u_nexts = [
        copies.remote(u_next.at[span], u_got.at[span], place.next, starts=at == 0)
        for at, span in enumerate(spans)
    ]
    joined = joined_of(0)
    u_nexts[1].start()
    u_cores[0].wait_recv()
    joined = joined + part_from[0].astype(F32)
    pair_next.wait_recv()
    pair_sum = (pair_grad[:, :local] + p_from[:, :local] + p_got[...]).astype(BF)
    through_pair = dot_nt(pair_sum.T, kvw[...])
    u_keep[...] = joined + through_pair * norm_ref[0:1, :]
    u_homes = [sent_home(u_home.at[span], u_land.at[span]) for span in spans]

    def arrives(nexts, keep, got, home, homes, at):
        nexts[at].wait_recv()
        span = spans[at]
        home[span, :] = (keep[span, :] + got[span, :].astype(F32)).astype(BF)
        homes[at][0]()

    loads[0].wait()
    loads[1].wait()
    stats[0:1, :D] += column_sum(through_pair * normal_of(0))
    stats[1:2, :D] += column_sum(through_pair)
    stats[4:5, :D] = column_sum(cg[0].astype(F32))
    stats[5:6, : 2 * HS] = row_of(jnp.sum(pair_sum.astype(F32), 1, keepdims=True))
    tail = pl.ds(8 + place.rank, 1)
    stats[tail, :query_width] = row_of(jnp.sum(dqt[...].astype(F32), 1, keepdims=True))
    stats[tail, query_width : query_width + wide] = ub_grad[0:1, :]
    vector_core = copies.remote(stats, v_core, place.core)
    pair_parts[...] = dot(pair_sum, a1[0]).T.reshape(pair_parts.shape)
    if sums_pair:
        shared_core = copies.remote(pair_parts, s_core, place.core)

    ot_load.wait()
    turned = 0.0
    turned_out = 0.0
    for slot in range(4):
        tokens = pl.ds(slot * local, local)
        turned = turned + dot(dqt[:, tokens], a1[slot])
        turned_out = turned_out + dot(ot[:, tokens], cg[slot])
    if shares:
        full[:query_width, :] = turned
        full[query_width:, :] = turned_out
        other = pl.ds(pl.multiple_of((1 - place.dp) * columns, 128), columns)
        g_send[...] = full[:, other].astype(BF)
        small_sum = copies.remote(g_send, g_recv, place.dp_peers[0])
        small_home = copies.homeward(g_send, small_land, place.swap)
        small_own[...] = full[:, pl.ds(pl.multiple_of(place.dp * columns, 128), columns)]
    else:
        small_own[:query_width, :] = turned
        small_own[query_width:, :] = turned_out

    vector_core.wait_recv()
    copies.sent(vector_core)
    stats[...] = stats[...] + v_core[...]
    vector_next = copies.remote(stats, v_next, place.next)
    if sums_pair:
        shared_core.wait_recv()
        copies.sent(shared_core)
        pair_parts[...] = pair_parts[...] + s_core[...]
        shared_next = [
            copies.remote(pair_parts.at[at * 4 + flip_one(place.rank)], s_next.at[at], place.next)
            for at in range(dp_size)
        ]
    wide_sums, small_sums = ([], [])
    loads[2].wait()
    if shares:
        half = wide // 2
        for copy in wide_loads:
            copy.wait()
        wide_sums.append(
            GroupSum(wide_held, big_g, entry_sum, query_width, 0, half, wide_buffers[0])
        )
        wide_sums[0].to_core()
        wide_loads = [copies.local(ref.at[rest], to) for ref, to in zip(leave, wide_held)]

    if shares:
        wide_sums[0].to_chip()
        small_sum.wait_recv()
        copies.sent(small_sum)
        total = small_own[...] + g_recv[...].astype(F32)
        small_own[...] = total

        @pl.when(place.is_swapped)
        def _():
            g_send[...] = total.astype(BF)
            small_home.start()

    u_move = functools.partial(arrives, u_nexts, u_keep, u_got, u_home, u_homes)
    u_move(0)
    vector_next.wait_recv()
    copies.sent(vector_next)
    stats[...] = stats[...] + v_next[...]
    vector_dp = [
        copies.remote(stats, v_dp.at[at], peer) for at, peer in enumerate(place.dp_peers)
    ]
    if sums_pair:
        for at, copy in enumerate(shared_next):
            copy.wait_recv()
            s_next[at] = s_next[at] + pair_parts[at * 4 + place.rank]
        shared_dp = [
            copies.remote(s_next.at[(place.dp + at + 1) % dp_size], s_dp.at[at], peer)
            for at, peer in enumerate(place.dp_peers)
        ]
    u_move(1)
    for copy in vector_dp:
        copy.wait_recv()
        copies.sent(copy)
    total = stats[...]
    for at in range(dp_size - 1):
        total = total + v_dp[at]
    stats[...] = total
    late_homes = [sent_home(stats, vector_home)]
    if sums_pair:
        for copy in shared_dp:
            copy.wait_recv()
        total = s_next[place.dp]
        for at in range(dp_size - 1):
            total = total + s_dp[at]
        s_core[0] = total
        late_homes.append(sent_home(s_core.at[0], shared_home))
    for start, _ in late_homes:
        start()

    if shares:
        for copy in wide_loads:
            copy.wait()
        wide_sums.append(
            GroupSum(wide_held, big_g, exit_sum, query_width, wide, half, wide_buffers[1])
        )
        wide_sums[1].to_core()
        wide_sums[0].back()

        @pl.when(place.is_swapped)
        def _():
            small_home.wait_send()
            small_home.wait_recv()
            small_own[...] = small_land[...].astype(F32)

        wide_sums[1].to_chip()
        for copy in small_loads:
            copy.wait()
        size = query_width // 2
        for olds, start, total, buffers in (
            (small_held[0], 0, entry_sum, small_buffers[0]),
            (small_held[1], query_width, exit_sum, small_buffers[1]),
        ):
            small_sums.append(GroupSum(olds, small_own, total, 0, start, size, buffers))
            small_sums[-1].to_core()
        for part in small_sums:
            part.to_chip()

    for _, wait in late_homes:
        wait()
    part = query_width + wide
    rows = [vector_home[at : at + 1, :D] for at in (0, 1, 2, 3, 4, 4)]
    rows.append(vector_home[5:6, : 2 * HS])
    rows += [vector_home[8 + at : 9 + at, :part] for at in range(4)]
    vector_row[...] = jnp.concatenate(rows, 1)
    if shares:
        whole_sums = []
        for olds, grads, buffers, rate, decay in (
            (vector, vector_row, vector_buffers, VECTOR_RATE, 0.0),
            (shared, shared_home, shared_buffers, MATRIX_RATE, MATRIX_DECAY),
        ):
            buffers[0][...] = gap_of(grads[...], *(as_row(ref[...]) for ref in olds), rate, decay)
            whole_sums.append(copies.remote(buffers[0], buffers[1], place.core))
        for at, buffers in enumerate((vector_buffers, shared_buffers)):
            whole_sums[at].wait_recv()
            buffers[2][...] = buffers[0][...] + buffers[1][...]
            whole_sums[at] = copies.remote(buffers[2], buffers[3], place.across)
    if shares:
        for part in wide_sums[1:] + small_sums:
            part.back()
        for copy, buffers, total in (
            (whole_sums[0], vector_buffers, vector_sum),
            (whole_sums[1], shared_buffers, shared_sum),
        ):
            copy.wait_recv()
            total[...] = buffers[2][...] + buffers[3][...]
        for part in wide_sums + small_sums:
            part.copy.wait_recv()
    for _, wait in u_homes + [y_home]:
        wait()
    copies.finish()


def second_pass(dp_size, late, arrays, olds, piece):
    up_w, small = arrays[1:3]
    local = arrays[0].shape[0]
    width = small.shape[0]
    query_width = width // 2
    wide = up_w.shape[0]
    shares = len(olds) > 0
    columns = olds[0].shape[1] if shares else D
    sums_pair = piece % 16 == 0
    held = (width if shares else 16, columns)
    parts = (4 * dp_size, piece, 2 * HS) if sums_pair else (1, D, 2 * HS)
    own = (piece if sums_pair else 8, 2 * HS)
    vector = (1, 6 * D + 2 * HS + 4 * (query_width + wide))
    outs = [((local, D), BF)] * 2
    outs += [(shape, F32) for shape in ((width, columns), vector, own, parts)]
    scratch = [
        (held, BF),
        ((16, 1024), F32),
        ((16, 1024), F32),
        ((16, 1024), F32),
        ((16, 1024), F32),
        ((dp_size - 1, 16, 1024), F32),
        (parts, F32),
        ((dp_size,) + own, F32),
        ((dp_size - 1,) + own, F32),
        ((2, local, D), BF),
        ((2, local, D), BF),
        ((local, D), BF),
        ((local, D), BF),
        ((local, D), F32),
        ((local, D), BF),
        ((2 * HS, 2 * local), F32),
        ((2 * HS, local), F32),
        ((2 * HS, local), F32),
        ((width, D), F32),
        (held, BF),
        (held, BF),
    ]
    if shares:
        outs += [(shape, F32) for shape in (olds[0].shape, olds[4].shape, own, vector)]
        for size in (wide // 2, wide // 2, query_width // 2, query_width // 2):
            scratch += [((size, columns), kind) for kind in (F32, F32, BF, BF)]
        scratch += [(own, F32)] * 4 + [(vector, F32)] * 4
        scratch += [((wide, columns), F32)] * 4 + [((query_width, columns), F32)] * 8
    scratch += [(array.shape, array.dtype) for array in late]
    late = list(late) + list(olds[:8])
    arrays = late + list(arrays) + list(olds[8:])
    vmem = pl.BlockSpec(memory_space=pltpu.VMEM)
    work = 4 * local * D * D
    semaphores = pltpu.SemaphoreType.DMA((80 + 3 * dp_size,))
    return pl.pallas_call(
        functools.partial(second_kernel, dp_size, sums_pair, shares),
        out_shape=[jax.ShapeDtypeStruct(shape, kind) for shape, kind in outs],
        in_specs=[pl.BlockSpec(memory_space=pl.ANY)] * len(late) + [vmem] * (len(arrays) - len(late)),
        out_specs=[vmem] * len(outs),
        scratch_shapes=[pltpu.VMEM(shape, kind) for shape, kind in scratch]
        + [semaphores, semaphores],
        compiler_params=pltpu.CompilerParams(
            collective_id=1, has_side_effects=True, vmem_limit_bytes=60 << 20
        ),
        cost_estimate=pl.CostEstimate(flops=8 * work, bytes_accessed=30 << 20, transcendentals=0),
        name="sum_branches",
    )(*arrays)


def third_kernel(groups, *refs):
    refs = iter(refs)

    def take(number):
        return [next(refs) for _ in range(number)]

    x_ref, c_ref, u_ref, y_ref, bias_ref = take(5)
    grads = [take(2), take(2), take(1), take(1)]
    olds = [take(6) for _ in range(4)]
    out_ref, grad_ref = take(2)
    news = [take(6) for _ in range(4)]
    step = pl.program_id(0)

    @pl.when(step < 4)
    def _():
        inputs = x_ref[...].astype(F32)
        centered = inputs - jnp.mean(inputs, -1, keepdims=True)
        scale = lax.rsqrt(jnp.mean(centered * centered, -1, keepdims=True) + NORM_EPS)
        normal = centered * scale
        joined = u_ref[...].astype(F32)
        grad_ref[...] = c_ref[...].astype(F32) + scale * (
            joined
            - jnp.mean(joined, -1, keepdims=True)
            - normal * jnp.mean(joined * normal, -1, keepdims=True)
        )
        bias = bias_ref[:, 4 * D : 5 * D] + bias_ref[:, 5 * D : 6 * D]
        out_ref[...] = inputs + y_ref[...].astype(F32) + bias

    def update(at, grad, rate, decay):
        weight, first, second, anchor, velocity, total = (as_row(ref[...]) for ref in olds[at])
        first, second, weight = adamw_update(weight, first, second, grad, rate, decay)
        change = total / groups
        momentum = OUTER_BETA * velocity + change
        outer = anchor - OUTER_RATE * (change + OUTER_BETA * momentum)
        for ref, value in zip(news[at], (first, second, weight, change, momentum, outer)):
            ref[...] = value.reshape(ref.shape)

    for at in range(2):
        head, rest = grads[at]
        update(at, jnp.where(step == 0, head[...], rest[...]), MATRIX_RATE, MATRIX_DECAY)

    @pl.when(step == 0)
    def _():
        update(2, grads[2][0][...], MATRIX_RATE, MATRIX_DECAY)
        update(3, grads[3][0][...], VECTOR_RATE, 0.0)


def third_pass(groups, x, c, u, y, big, small, shared_grad, vector_grad, entry, leave, shared, vector):
    rows, columns = entry[0].shape
    size = small.shape[0] // 2
    wide = rows // size - 1

    def block(index):
        return pl.BlockSpec((size, columns), index)

    def all_of(array):
        return pl.BlockSpec(array.shape, lambda i: (0,) * array.ndim)

    here = block(lambda i: (i, 0))
    tokens = pl.BlockSpec((x.shape[0] // 4, D), lambda i: (jnp.minimum(i, 3), 0))
    grad_specs = [
        block(lambda i: (0, 0)),
        block(lambda i: (jnp.maximum(i - 1, 0), 0)),
        block(lambda i: (1, 0)),
        block(lambda i: (wide + jnp.maximum(i - 1, 0), 0)),
        all_of(shared_grad),
        all_of(vector_grad),
    ]
    specs = [here] * 12 + [all_of(array) for array in shared + vector]
    out_specs = [tokens] * 2 + [here] * 12 + [all_of(shared[0])] * 6 + [all_of(vector[0])] * 3
    out_specs += [all_of(vector[3])] * 3
    outs = [x, x] + [array for array in (entry[0], leave[0], shared[0]) for _ in range(6)]
    outs += [vector[0]] * 3 + [vector[3]] * 3
    return pl.pallas_call(
        functools.partial(third_kernel, groups),
        grid=(rows // size,),
        out_shape=[jax.ShapeDtypeStruct(array.shape, F32) for array in outs],
        in_specs=[tokens] * 4 + [all_of(vector[0])] + grad_specs + specs,
        out_specs=out_specs,
        compiler_params=pltpu.CompilerParams(vmem_limit_bytes=60 << 20),
        cost_estimate=pl.CostEstimate(flops=1 << 26, bytes_accessed=40 << 20, transcendentals=1 << 20),
        name="update_weights",
    )(x, c, u, y, vector[0], small, big, small, big, shared_grad, vector_grad, *entry, *leave, *shared, *vector)


def shards(
    hidden_in,
    doc_ids,
    out_cotangent,
    entry_weight,
    entry_first,
    entry_second,
    entry_anchor,
    entry_velocity,
    exit_weight,
    exit_first,
    exit_second,
    exit_anchor,
    exit_velocity,
    shared_weight,
    shared_first,
    shared_second,
    shared_anchor,
    shared_velocity,
    vector_weight,
    vector_first,
    vector_second,
    vector_anchor,
    vector_velocity,
):
    batch, local_len = hidden_in.shape[:2]
    parts = lax.axis_size("mp")
    group, rank = (lax.axis_index("group"), lax.axis_index("mp"))
    is_swapped = (group % 2) != (rank // 2)
    rank = jnp.where(is_swapped, jnp.bitwise_xor(rank, 2), rank)
    length = local_len * parts
    part_width = entry_weight.shape[2]
    query_width = HEADS * HS // parts
    heads = query_width // HS

    dp_size = lax.axis_size("dp")
    groups = lax.axis_size("group")
    order = jnp.bitwise_xor(jnp.arange(parts), rank)
    piece = shared_weight.shape[1]
    shared_piece = shared_weight[0]
    if piece % 16:
        pieces = gather_square(swapped_parts(shared_piece.astype(BF)))
        pieces = jnp.take(pieces, order, axis=0)
        shared_piece = gather_dp(pieces.reshape(-1, 2 * HS), 0)
    half = ROT // 2
    frequency = 10000.0 ** (-(np.arange(half) * 2.0 / ROT))
    angles = frequency.astype(np.float32)[:, None] * np.arange(length, dtype=np.float32)[None, :]
    cosine_table = jnp.asarray(np.cos(angles.astype(np.float64)).astype(np.float32))
    sine_table = jnp.asarray(np.sin(angles.astype(np.float64)).astype(np.float32))
    entry = [array[0].T for array in (entry_weight, entry_first, entry_second)]
    entry += [array.T for array in (entry_anchor, entry_velocity)]
    leave = [array[0] for array in (exit_weight, exit_first, exit_second)]
    leave += [exit_anchor, exit_velocity]
    shared = [array[0] for array in (shared_weight, shared_first, shared_second)]
    shared += [shared_anchor, shared_velocity]
    vector = [vector_weight, vector_first, vector_second, vector_anchor, vector_velocity]
    shares = dp_size == 2 and leave[0].shape[1] % 128 == 0 and piece % 16 == 0
    weights = [entry[0], leave[0]]
    if not shares:
        weights = [gather_dp(swapped_parts(array.astype(BF)), 1) for array in weights]
    (
        inputs, cots, attn_input, hidden_grad, up_w, small, pair_weight, attended,
        query_grad, pair_rows, norms, up_bias_rows, big_grad, branch,
    ) = first_pass(
        dp_size,
        hidden_in[0],
        out_cotangent[0],
        *weights,
        shared_piece,
        doc_ids,
        vector_weight,
        cosine_table,
        sine_table,
    )
    arrays = (
        branch, up_w, small, pair_weight.reshape(D, 2 * HS), query_grad,
        pair_rows, norms, up_bias_rows,
    )
    olds = [array for arrays in (entry, leave, shared, vector) for array in arrays[:4]]
    joined, branch, small_grad, vector_grad, shared_grad, pair_parts, *totals = second_pass(
        dp_size, (cots, attn_input, big_grad, inputs, hidden_grad, attended), arrays, olds if shares else [], piece
    )
    if not shares:
        big_grad, small_grad = (
            swapped_parts(scatter_dp(array, 1, F32)) for array in (big_grad, small_grad)
        )
        if piece % 16:
            grad_pieces = pair_parts.reshape(dp_size, parts, -1, 2 * HS)
            grad_pieces = jnp.take(grad_pieces, order, axis=1).swapaxes(0, 1)
            shared_grad = scatter_dp(scatter_square(grad_pieces, F32), 0, F32)
            shared_grad = swapped_parts(shared_grad.reshape(-1, 2 * HS))
        size, wide = (small_grad.shape[0] // 2, big_grad.shape[0] // 2)
        gaps = (
            gap_of(
                jnp.concatenate([small_grad[:size], big_grad[:wide]]),
                *entry[:4], MATRIX_RATE, MATRIX_DECAY,
            ),
            gap_of(
                jnp.concatenate([small_grad[size:], big_grad[wide:]]),
                *leave[:4], MATRIX_RATE, MATRIX_DECAY,
            ),
            gap_of(shared_grad, *shared[:4], MATRIX_RATE, MATRIX_DECAY),
            gap_of(vector_grad, *vector[:3], vector_anchor[None], VECTOR_RATE, 0.0),
        )
        totals = lax.psum(gaps, "group")
    block_output, input_grad, *updated = third_pass(
        groups, hidden_in[0], out_cotangent[0], joined, branch, big_grad, small_grad, shared_grad, vector_grad,
        *(arrays + [total] for arrays, total in zip((entry, leave, shared, vector), totals)),
    )
    results = [block_output[None], input_grad[None]]
    for at in range(3):
        own = updated[6 * at : 6 * at + 6]
        if at == 0:
            own = [array.T for array in own]
        results += [array[None] for array in own[:3]] + own[3:]
    results += updated[18:24]
    return tuple(results)


def solution(mesh):
    in_specs = (
        P(("group", "dp"), "mp", None),
        P(("group", "dp"), "mp"),
        P(("group", "dp"), "mp", None),
        P("group", "dp", "mp"),
        P("group", "dp", "mp"),
        P("group", "dp", "mp"),
        P("dp", "mp"),
        P("dp", "mp"),
        P("group", "mp", "dp"),
        P("group", "mp", "dp"),
        P("group", "mp", "dp"),
        P("mp", "dp"),
        P("mp", "dp"),
        P("group", ("dp", "mp"), None),
        P("group", ("dp", "mp"), None),
        P("group", ("dp", "mp"), None),
        P(("dp", "mp"), None),
        P(("dp", "mp"), None),
        P("group", None),
        P("group", None),
        P("group", None),
        P(),
        P(),
    )
    out_specs = (
        P(("group", "dp"), "mp", None),
        P(("group", "dp"), "mp", None),
        P("group", "dp", "mp"),
        P("group", "dp", "mp"),
        P("group", "dp", "mp"),
        P("dp", "mp"),
        P("dp", "mp"),
        P("dp", "mp"),
        P("group", "mp", "dp"),
        P("group", "mp", "dp"),
        P("group", "mp", "dp"),
        P("mp", "dp"),
        P("mp", "dp"),
        P("mp", "dp"),
        P("group", ("dp", "mp"), None),
        P("group", ("dp", "mp"), None),
        P("group", ("dp", "mp"), None),
        P(("dp", "mp"), None),
        P(("dp", "mp"), None),
        P(("dp", "mp"), None),
        P("group", None),
        P("group", None),
        P("group", None),
        P(),
        P(),
        P(),
    )
    return jax.shard_map(shards, mesh=mesh, in_specs=in_specs, out_specs=out_specs, check_vma=False)
```
